32 devices in a mesh: dp: 8 (over z, y), mix: 4 (over x, core).
Axes of the slice: x: 2, y: 2, z: 4, core: 2. Of those that a mesh axis runs over, the one named last changes fastest.
Arguments:
- images_in: bfloat16 [384, 196, 384], P('dp', 'mix'), may hold values from -6 to 6
- out_grad: bfloat16 [384, 196, 384], P('dp', 'mix'), may hold values from -6 to 6
- slot_mask: int32 [384], P('dp'), may hold values from 0 to 1, as said below
- mix_gain: bfloat16 [2, 384], replicated, may hold values from 0.5 to 1.5
- mix_shift: bfloat16 [2, 384], replicated, may hold values from -3 to 3
- mix_scale: bfloat16 [2, 384], replicated, may hold values from 0.5 to 1.5
- mix_weight: bfloat16 [2, 196, 196], replicated, may hold values from -0.4375 to 0.4375
- mix_bias: bfloat16 [2, 196], replicated, may hold values from -3 to 3
- mlp_gain: bfloat16 [2, 384], replicated, may hold values from 0.5 to 1.5
- mlp_shift: bfloat16 [2, 384], replicated, may hold values from -3 to 3
- mlp_scale: bfloat16 [2, 384], replicated, may hold values from 0.5 to 1.5
- up_weight: bfloat16 [2, 384, 1536], replicated, may hold values from -0.3125 to 0.3125
- up_bias: bfloat16 [2, 1536], replicated, may hold values from -3 to 3
- down_weight: bfloat16 [2, 1536, 384], replicated, may hold values from -0.15625 to 0.15625
- down_bias: bfloat16 [2, 384], replicated, may hold values from -3 to 3
Outputs:
- output: bfloat16 [384, 196, 384], P('dp', 'mix')
- input_grad: float32 [384, 196, 384], P('dp', 'mix')
- mix_gain_grad: float32 [2, 384], P(None, 'mix')
- mix_shift_grad: float32 [2, 384], P(None, 'mix')
- mix_scale_grad: float32 [2, 384], P(None, 'mix')
- mix_weight_grad: float32 [2, 196, 196], P(None, 'mix')
- mix_bias_grad: float32 [2, 196], P(None, 'mix')
- mlp_gain_grad: float32 [2, 384], P(None, 'mix')
- mlp_shift_grad: float32 [2, 384], P(None, 'mix')
- mlp_scale_grad: float32 [2, 384], P(None, 'mix')
- up_weight_grad: float32 [2, 384, 1536], P(None, None, 'mix')
- up_bias_grad: float32 [2, 1536], P(None, 'mix')
- down_weight_grad: float32 [2, 1536, 384], P(None, 'mix')
- down_bias_grad: float32 [2, 384], P(None, 'mix')
The draws below stay inside these ranges and needn't reach their ends.
Inputs may be any that keep to these rules, and one draw needn't show every extreme that they name: `slot_mask`: 1 marks a filled slot, 0 an empty one. Each aligned group of 48 slots (those of one index of dp) holds between 36 and 48 filled slots at any positions; in every draw some group is full and some holds exactly 36.
All inputs are finite; a program needn't handle non-finite values.
Results may differ from the reference program's by a relative error of at most 0.013.
Values may be sent and summed in bfloat16 or wider, within the bound.
A program may use at most 192 MiB of HBM per device.

```python
import math
import jax
import jax.numpy as jnp
from jax import lax

D = 384
H = 1536
P_SIZE = 196
LAYERS = 2
IMG_GRP = 48
IMAGES = 384


def draw_slot_mask(key, part):
    key = jax.random.fold_in(key, 7)
    count_key, full_key, least_key, order_key = jax.random.split(key, 4)
    groups = IMAGES // IMG_GRP
    least = 3 * IMG_GRP // 4
    counts = jax.random.randint(count_key, (groups,), least, IMG_GRP + 1)
    full_at = jax.random.randint(full_key, (), 0, groups)
    least_at = (full_at + 1 + jax.random.randint(least_key, (), 0, groups - 1)) % groups
    group_ids = jnp.arange(groups)
    counts = jnp.where(group_ids == full_at, IMG_GRP, counts)
    counts = jnp.where(group_ids == least_at, least, counts)
    orders = jax.vmap(lambda inner: jax.random.permutation(inner, IMG_GRP))(jax.random.split(order_key, groups))
    return (orders < counts[:, None]).astype(jnp.int32).reshape(groups * IMG_GRP)


def shard_levels(own_key, extent, pieces, low, top_value):
    level, own = 1.0, jax.random.fold_in(own_key, 6)
    for position, blocks in pieces:
        draws = jnp.exp(jax.random.uniform(jax.random.fold_in(own, position), (blocks,), jnp.float32, low / len(pieces), top_value / len(pieces)))
        level = level * jnp.repeat(draws, extent[position] // blocks).reshape([-1 if axis == position else 1 for axis in range(len(extent))])
    return level


def centred(stream_key, shape, width, limit, shards=(), dtype=jnp.bfloat16):
    values = width * jax.random.normal(stream_key, shape, jnp.float32)
    if shards:
        values = values * shard_levels(stream_key, shape, shards, -0.22, 0.18)
    return jnp.clip(values, -limit, limit).astype(dtype)


def setup_inputs(seed: int = 0) -> dict:
    key_of = jax.random.split(jax.random.key(seed), 16)
    images_in = centred(key_of[0], (IMAGES, P_SIZE, D), 1.0, 6.0, ((0, 8), (1, 4)))
    out_grad = centred(key_of[1], (IMAGES, P_SIZE, D), 1.0, 6.0, ((0, 8), (1, 4)))
    slot_mask = draw_slot_mask(jax.random.fold_in(key_of[15], 71), 0)
    mix_gain = jnp.clip(1.0 + 0.1 * jax.random.normal(key_of[3], (LAYERS, D), jnp.float32), 0.5, 1.5).astype(jnp.bfloat16)
    mix_shift = centred(key_of[4], (LAYERS, D), 0.5, 3.0)
    mix_scale = jnp.clip(1.0 + 0.1 * jax.random.normal(key_of[5], (LAYERS, D), jnp.float32), 0.5, 1.5).astype(jnp.bfloat16)
    mix_weight = centred(key_of[6], (LAYERS, P_SIZE, P_SIZE), P_SIZE ** -0.5, 0.4375)
    mix_bias = centred(key_of[7], (LAYERS, P_SIZE), 0.5, 3.0)
    mlp_gain = jnp.clip(1.0 + 0.1 * jax.random.normal(key_of[8], (LAYERS, D), jnp.float32), 0.5, 1.5).astype(jnp.bfloat16)
    mlp_shift = centred(key_of[9], (LAYERS, D), 0.5, 3.0)
    mlp_scale = jnp.clip(1.0 + 0.1 * jax.random.normal(key_of[10], (LAYERS, D), jnp.float32), 0.5, 1.5).astype(jnp.bfloat16)
    up_weight = centred(key_of[11], (LAYERS, D, H), D ** -0.5, 0.3125)
    up_bias = centred(key_of[12], (LAYERS, H), 0.5, 3.0)
    down_weight = centred(key_of[13], (LAYERS, H, D), H ** -0.5, 0.15625)
    down_bias = centred(key_of[14], (LAYERS, D), 0.5, 3.0)
    return dict(images_in=images_in, out_grad=out_grad, slot_mask=slot_mask, mix_gain=mix_gain, mix_shift=mix_shift, mix_scale=mix_scale, mix_weight=mix_weight, mix_bias=mix_bias, mlp_gain=mlp_gain, mlp_shift=mlp_shift, mlp_scale=mlp_scale, up_weight=up_weight, up_bias=up_bias, down_weight=down_weight, down_bias=down_bias)


@jax.custom_vjp
def low(v):
    return lax.optimization_barrier(v.astype(jnp.bfloat16)).astype(jnp.float32)

@jax.custom_vjp
def low_back(v):
    return v

def low_keep(v):
    return (low(v), None)

def low_pass(kept, grad):
    return (grad,)

def back_keep(v):
    return (v, None)

def back_low(kept, grad):
    return (low(grad),)
low.defvjp(low_keep, low_pass)
low_back.defvjp(back_keep, back_low)
HIGHEST = lax.Precision.HIGHEST

def layer_forward(stream, params):
    mix_gain, mix_shift, mix_scale, mix_weight, mix_bias, mlp_gain, mlp_shift, mlp_scale, up_weight, up_bias, down_weight, down_bias = params
    mixed_in = low(mix_gain * stream + mix_shift)
    across = jnp.einsum('pq,gqc->gpc', mix_weight, mixed_in, precision=HIGHEST) + mix_bias[:, None]
    across = low_back(across)
    first = low_back(low(stream + mix_scale * across))
    normed = low(mlp_gain * first + mlp_shift)
    hidden = low_back(jnp.einsum('gpc,ch->gph', normed, up_weight, precision=HIGHEST) + up_bias)
    active = low(jax.nn.gelu(hidden))
    branch = low_back(jnp.einsum('gph,hc->gpc', active, down_weight, precision=HIGHEST) + down_bias)
    return low_back(low(first + mlp_scale * branch))

def forward_block(stream, slot_weight, params):
    for layer_index in range(LAYERS):
        stream = layer_forward(stream, tuple((entry[layer_index] for entry in params)))
    return slot_weight[:, None, None] * stream

def reference(images_in, out_grad, slot_mask, mix_gain, mix_shift, mix_scale, mix_weight, mix_bias, mlp_gain, mlp_shift, mlp_scale, up_weight, up_bias, down_weight, down_bias):
    params = tuple((entry.astype(jnp.float32) for entry in (mix_gain, mix_shift, mix_scale, mix_weight, mix_bias, mlp_gain, mlp_shift, mlp_scale, up_weight, up_bias, down_weight, down_bias)))
    group = math.gcd(IMAGES, 16)
    inputs = images_in.astype(jnp.float32).reshape(-1, group, P_SIZE, D)
    cotangents = out_grad.astype(jnp.float32).reshape(-1, group, P_SIZE, D)
    weights = slot_mask.astype(jnp.float32).reshape(-1, group)

    def block_step(totals, block):
        stream, cotangent, slot_weight = block

        def apply_block(values, parameters):
            return forward_block(values, slot_weight, parameters)
        result, pullback = jax.vjp(apply_block, stream, params)
        stream_grad, param_grads = pullback(cotangent)
        return (jax.tree.map(jnp.add, totals, param_grads), (result.astype(jnp.bfloat16), stream_grad))
    zeros = tuple((jnp.zeros(entry.shape, jnp.float32) for entry in params))
    totals, (results, stream_grads) = lax.scan(block_step, zeros, (inputs, cotangents, weights))
    output = results.reshape(IMAGES, P_SIZE, D)
    input_grad = stream_grads.reshape(IMAGES, P_SIZE, D)
    return (output, input_grad, totals[0], totals[1], totals[2], totals[3], totals[4], totals[5], totals[6], totals[7], totals[8], totals[9], totals[10], totals[11])
```

```python
import jax
import jax.numpy as jnp
from jax import lax
from jax.sharding import PartitionSpec as P


def mix_across(stream, gain_terms, mix_matrix, mix_offset):
    mixed_in = (gain_terms[0] * stream + gain_terms[1]).astype(jnp.bfloat16)
    across = jnp.einsum("pq,gqc->gpc", mix_matrix, mixed_in, preferred_element_type=jnp.float32)
    return (mixed_in, across + mix_offset[:, None])


def mlp_apply(patch_rows, gain_terms, weights):
    norm_gain, norm_shift, branch_scale = gain_terms
    up_matrix, up_offset, down_matrix, down_offset = weights
    row_values = patch_rows.astype(jnp.float32)
    normed = (norm_gain * row_values + norm_shift).astype(jnp.bfloat16)
    hidden = (
        jnp.einsum("gpc,ch->gph", normed, up_matrix, preferred_element_type=jnp.float32) + up_offset
    )
    active = jax.nn.gelu(hidden).astype(jnp.bfloat16)
    branch = (
        jnp.einsum("gph,hc->gpc", active, down_matrix, preferred_element_type=jnp.float32)
        + down_offset
    )
    return (row_values + branch_scale * branch).astype(jnp.bfloat16)


def mlp_backward(row_inputs, incoming, gain_terms, weights):
    norm_gain, norm_shift, branch_scale = gain_terms
    up_matrix, up_offset, down_matrix, down_offset = weights
    channels = row_inputs.shape[-1]
    row_values = row_inputs.reshape(-1, channels).astype(jnp.float32)
    upstream = incoming.reshape(-1, channels).astype(jnp.float32)
    normed = (norm_gain * row_values + norm_shift).astype(jnp.bfloat16)
    hidden = jnp.dot(normed, up_matrix, preferred_element_type=jnp.float32) + up_offset
    active_full, gelu_pull = jax.vjp(jax.nn.gelu, hidden)
    active = active_full.astype(jnp.bfloat16)
    branch = jnp.dot(active, down_matrix, preferred_element_type=jnp.float32) + down_offset
    scale_grad = jnp.sum(upstream * branch, axis=0)
    branch_grad = (branch_scale * upstream).astype(jnp.bfloat16)
    lower_bias = jnp.sum(branch_grad.astype(jnp.float32), axis=0)
    lower_weight = jnp.einsum("th,tc->hc", active, branch_grad, preferred_element_type=jnp.float32)
    active_grad = jnp.einsum(
        "tc,hc->th", branch_grad, down_matrix, preferred_element_type=jnp.float32
    )
    hidden_grad = gelu_pull(active_grad)[0].astype(jnp.bfloat16)
    upper_bias = jnp.sum(hidden_grad.astype(jnp.float32), axis=0)
    upper_weight = jnp.einsum("tc,th->ch", normed, hidden_grad, preferred_element_type=jnp.float32)
    normed_grad = jnp.einsum(
        "th,ch->tc", hidden_grad, up_matrix, preferred_element_type=jnp.float32
    )
    gain_grad = jnp.sum(normed_grad * row_values, axis=0)
    shift_grad = jnp.sum(normed_grad, axis=0)
    row_grad = upstream + norm_gain * normed_grad
    return (
        row_grad.reshape(incoming.shape),
        (gain_grad, shift_grad, scale_grad, upper_weight, upper_bias, lower_weight, lower_bias),
    )


def mix_backward(stream, incoming, gain_terms, mix_matrix, mix_offset):
    mixed_in, across = mix_across(stream, gain_terms, mix_matrix, mix_offset)
    scale_grad = jnp.sum(incoming * across, axis=(0, 1))
    across_grad = (gain_terms[2] * incoming).astype(jnp.bfloat16)
    bias_grad = jnp.sum(across_grad.astype(jnp.float32), axis=(0, 2))
    weight_grad = jnp.einsum(
        "gpc,gqc->pq", across_grad, mixed_in, preferred_element_type=jnp.float32
    )
    mixed_grad = jnp.einsum(
        "pq,gpc->gqc", mix_matrix, across_grad, preferred_element_type=jnp.float32
    )
    gain_grad = jnp.sum(mixed_grad * stream, axis=(0, 1))
    shift_grad = jnp.sum(mixed_grad, axis=(0, 1))
    carried = incoming + gain_terms[0] * mixed_grad
    return (carried, (gain_grad, shift_grad, scale_grad, weight_grad, bias_grad))


def reduce_grads(mix_part, mlp_part):
    members = tuple(mix_part) + tuple(mlp_part)
    scattered = tuple(
        lax.psum_scatter(
            member, "mix", scatter_dimension=1 if place == 8 else 0, tiled=True
        )
        for place, member in enumerate(members)
    )
    return lax.psum(scattered, "dp")


def local(
    images_in,
    out_grad,
    slot_mask,
    mix_gain,
    mix_shift,
    mix_scale,
    mix_weight,
    mix_bias,
    mlp_gain,
    mlp_shift,
    mlp_scale,
    up_weight,
    up_bias,
    down_weight,
    down_bias,
):
    layer_count = up_weight.shape[0]

    def first_terms(layer_index):
        return (
            mix_gain[layer_index].astype(jnp.float32),
            mix_shift[layer_index].astype(jnp.float32),
            mix_scale[layer_index].astype(jnp.float32),
        )

    def second_terms(layer_index):
        return (
            mlp_gain[layer_index].astype(jnp.float32),
            mlp_shift[layer_index].astype(jnp.float32),
            mlp_scale[layer_index].astype(jnp.float32),
        )

    def mlp_terms(layer_index):
        return (
            up_weight[layer_index],
            up_bias[layer_index].astype(jnp.float32),
            down_weight[layer_index],
            down_bias[layer_index].astype(jnp.float32),
        )

    whole = lax.all_to_all(images_in, "mix", split_axis=0, concat_axis=1, tiled=True)
    whole_grad = lax.all_to_all(out_grad, "mix", split_axis=0, concat_axis=1, tiled=True)
    own = whole.shape[0]
    slot_weight = lax.dynamic_slice_in_dim(
        slot_mask.astype(jnp.float32), lax.axis_index("mix") * own, own, 0
    )[:, None, None]
    stream = whole.astype(jnp.float32)
    image_inputs = []
    kept_rows = []
    for layer_index in range(layer_count):
        image_inputs.append(stream.astype(jnp.bfloat16))
        gain_terms = first_terms(layer_index)
        mixed_in, across = mix_across(
            stream,
            gain_terms,
            mix_weight[layer_index],
            mix_bias[layer_index].astype(jnp.float32),
        )
        first_rows = (stream + gain_terms[2] * across).astype(jnp.bfloat16)
        kept_rows.append(first_rows)
        stream = mlp_apply(first_rows, second_terms(layer_index), mlp_terms(layer_index)).astype(
            jnp.float32
        )
    output = lax.all_to_all(
        (slot_weight * stream).astype(jnp.bfloat16), "mix", split_axis=1, concat_axis=0, tiled=True
    )
    carried = slot_weight * whole_grad.astype(jnp.float32)
    per_layer = [None] * layer_count
    for layer_index in reversed(range(layer_count)):
        row_grad, mlp_part = mlp_backward(
            kept_rows[layer_index],
            carried.astype(jnp.bfloat16),
            second_terms(layer_index),
            mlp_terms(layer_index),
        )
        carried, mix_part = mix_backward(
            image_inputs[layer_index].astype(jnp.float32),
            row_grad.astype(jnp.bfloat16).astype(jnp.float32),
            first_terms(layer_index),
            mix_weight[layer_index],
            mix_bias[layer_index].astype(jnp.float32),
        )
        per_layer[layer_index] = reduce_grads(mix_part, mlp_part)
    carried = lax.all_to_all(
        carried.astype(jnp.bfloat16), "mix", split_axis=1, concat_axis=0, tiled=True
    ).astype(jnp.float32)
    stacked = tuple(
        (
            jnp.stack([per_layer[level_index][member] for level_index in range(layer_count)])
            for member in range(12)
        )
    )
    return (output, carried) + stacked


def solution(mesh):
    in_specs = (
        P("dp", "mix", None),
        P("dp", "mix", None),
        P("dp"),
        P(),
        P(),
        P(),
        P(),
        P(),
        P(),
        P(),
        P(),
        P(),
        P(),
        P(),
        P(),
    )
    out_specs = (
        P("dp", "mix", None),
        P("dp", "mix", None),
        P(None, "mix"),
        P(None, "mix"),
        P(None, "mix"),
        P(None, "mix", None),
        P(None, "mix"),
        P(None, "mix"),
        P(None, "mix"),
        P(None, "mix"),
        P(None, None, "mix"),
        P(None, "mix"),
        P(None, "mix", None),
        P(None, "mix"),
    )
    return jax.shard_map(local, mesh=mesh, in_specs=in_specs, out_specs=out_specs, check_vma=False)
```

```python
import functools
import math

import jax
import jax.numpy as jnp
from jax import lax
from jax.experimental import pallas as pl
from jax.experimental.pallas import tpu as pltpu
from jax.sharding import PartitionSpec as P

MESH = pl.DeviceIdType.MESH
F32 = jnp.float32
BF16 = jnp.bfloat16
GROUP = 16
TILE = 16
TANH_A = math.sqrt(2.0 / math.pi)
TANH_B = TANH_A * 0.044715


def dot(a, b):
    return jnp.dot(a, b, preferred_element_type=F32)


def dot_nt(a, b):
    return lax.dot_general(a, b, (((1,), (1,)), ((), ())), preferred_element_type=F32)


def iota(shape, axis):
    return lax.broadcasted_iota(jnp.int32, shape, axis)


def gelu_pair(value):
    square = value * value
    curve = jnp.tanh(value * (TANH_A + TANH_B * square))
    half = 0.5 * value
    gate = 0.5 * curve + 0.5
    slope = gate + (half * (1.0 - curve * curve)) * (TANH_A + (3.0 * TANH_B) * square)
    return value * gate, slope


def mask_lanes(mask_ref, first, count, pick):
    total = jnp.zeros(pick.shape, F32)
    for k in range(count):
        total = jnp.where(pick == k, mask_ref[first + k].astype(F32), total)
    return total


def swap_matrix():
    side = GROUP * TILE
    row, lane = iota((side, side), 0), iota((side, side), 1)
    return jnp.where((row >> 4) + ((row & 15) << 4) == lane, 1.0, 0.0)


class Sizes:
    def __init__(self, parts, slots, patches, channels, hidden, layers):
        self.parts = parts
        self.slots = slots
        self.patches = patches
        self.channels = channels
        self.hidden = hidden
        self.layers = layers
        self.groups = slots // GROUP
        self.mine = GROUP // parts
        self.main = patches // TILE * TILE
        self.block = self.mine * self.main
        self.body = parts * self.block
        self.rows = self.body + parts * self.mine
        self.image = parts * self.main
        self.mix_rows = self.image + parts * self.mine
        self.ones = self.mix_rows
        self.mix_cols = self.mix_rows + TILE
        self.pad = -(-self.mix_cols // 128) * 128
        self.left = -(-self.groups * self.mine // TILE) * TILE
        self.whole = parts * patches


def whole_kernel(
    z,
    keep,
    x_hbm, dy_hbm, mask_ref, mixw_ref, mixb_ref,
    mgain_ref, mshift_ref, mscale_ref, pgain_ref, pshift_ref, pscale_ref, downb_ref, upb_ref,
    up_hbm, down_hbm,
    out_w, out_e, dx_w, dx_e, du_hbm, dd_hbm, dm_ref, dv_ref, dub_ref,
    du_ref, dd_ref, stage, send_x, send_dy, sende_x, sende_dy, got_x, got_dy,
    xs, firsts, dys, outs_left, out_left, act, slope, up_w, down_w, mix_m, mix_t,
    load_sem, own_sem, send_sem, recv_sem, lsend_sem, lrecv_sem,
):
    dp, me = lax.axis_index("dp"), lax.axis_index("mix")
    parts, groups, channels, hidden = z.parts, z.groups, z.channels, z.hidden
    peers = [lax.rem(me + r, parts) for r in range(parts)]

    loads = []
    for k, hbm in enumerate((x_hbm, dy_hbm)):
        for g in range(groups):
            loads.append(
                pltpu.make_async_copy(
                    hbm.at[:, pl.ds(g * GROUP, GROUP), :], stage.at[g], load_sem.at[k * groups + g]
                )
            )
    w_loads = [
        pltpu.make_async_copy(up_hbm, up_w, load_sem.at[2 * groups]),
        pltpu.make_async_copy(down_hbm, down_w, load_sem.at[2 * groups + 1]),
    ]
    for copy in loads[:groups] + w_loads:
        copy.start()

    barrier = pltpu.get_barrier_semaphore()
    for r in range(1, parts):
        pl.semaphore_signal(barrier, inc=1, device_id=(dp, peers[r]), device_id_type=MESH)

    swap = swap_matrix()
    swap_b = swap.astype(BF16)
    left_all = parts * z.left

    def convert(send, g, matrix):
        for t in range(z.main // TILE):
            block = stage[g, t * TILE : (t + 1) * TILE].reshape(TILE * GROUP, channels)
            rows = dot(matrix, block).astype(BF16).reshape(GROUP, TILE, channels)
            for d in range(parts):
                for j in range(z.mine):
                    send[g, d, j * z.main + t * TILE : j * z.main + (t + 1) * TILE, :] = rows[
                        d * z.mine + j
                    ]

    def convert_left(send, lanes):
        row, lane = iota((left_all, z.slots), 0), iota((left_all, z.slots), 1)
        want = jnp.full(row.shape, -1, jnp.int32)
        for d in range(parts):
            for g in range(groups):
                base = d * z.left + g * z.mine
                inside = (row >= base) & (row < base + z.mine)
                want = jnp.where(inside, row - base + g * GROUP + d * z.mine, want)
        matrix = jnp.where(want == lane, 1.0, 0.0)
        if lanes is not None:
            matrix = matrix * lanes
        last = jnp.concatenate([stage[g, z.patches - 1] for g in range(groups)], axis=0)
        send[...] = dot(matrix.astype(BF16), last).astype(BF16).reshape(parts, z.left, channels)

    def exchange(k, g, send, target):
        copies = [pltpu.make_async_copy(send.at[g, me], target.at[g, pl.ds(me * z.block, z.block)], own_sem.at[k, g])]
        for r in range(1, parts):
            copies.append(
                pltpu.make_async_remote_copy(
                    src_ref=send.at[g, peers[r]],
                    dst_ref=target.at[g, pl.ds(me * z.block, z.block)],
                    send_sem=send_sem.at[k, g, r],
                    recv_sem=recv_sem.at[k, g, r],
                    device_id=(dp, peers[r]),
                    device_id_type=MESH,
                )
            )
        return copies

    def part_of(source, g, d):
        if len(source.shape) == 4:
            return source.at[g, d]
        return source.at[g, pl.ds(d * z.block, z.block)]

    def exchange_back(k, g, source, target):
        copies = [pltpu.make_async_copy(part_of(source, g, me), target.at[g, me], own_sem.at[k, g])]
        for r in range(1, parts):
            copies.append(
                pltpu.make_async_remote_copy(
                    src_ref=part_of(source, g, peers[r]),
                    dst_ref=target.at[g, me],
                    send_sem=send_sem.at[k, g, r],
                    recv_sem=recv_sem.at[k, g, r],
                    device_id=(dp, peers[r]),
                    device_id_type=MESH,
                )
            )
        return copies

    def exchange_left(k, send, target):
        copies = [pltpu.make_async_copy(send.at[me], target.at[me], lsend_sem.at[k, 0])]
        for r in range(1, parts):
            copies.append(
                pltpu.make_async_remote_copy(
                    src_ref=send.at[peers[r]],
                    dst_ref=target.at[me],
                    send_sem=lsend_sem.at[k, r],
                    recv_sem=lrecv_sem.at[k, r],
                    device_id=(dp, peers[r]),
                    device_id_type=MESH,
                )
            )
        return copies

    def start(copies):
        for copy in copies:
            copy.start()

    def arrive(copies):
        copies[0].wait()
        for copy in copies[1:]:
            copy.wait_recv()

    def sent(copies):
        for copy in copies[1:]:
            copy.wait_send()

    for g in range(groups):
        loads[g].wait()
        convert(send_x, g, swap_b)
        if g == 0:
            pl.semaphore_wait(barrier, parts - 1)
        start(exchange(0, g, send_x, xs.at[0]))
    convert_left(sende_x, None)
    for copy in loads[groups:]:
        copy.start()
    start(exchange_left(0, sende_x, got_x))
    for g in range(groups):
        loads[groups + g].wait()
        pick = iota((1, GROUP * TILE), 1) & 15
        lanes = mask_lanes(mask_ref, g * GROUP, GROUP, pick)
        convert(send_dy, g, (swap * lanes).astype(BF16))
        start(exchange(1, g, send_dy, dys))
    convert_left(sende_dy, mask_lanes(mask_ref, 0, z.slots, iota((1, z.slots), 1)))
    start(exchange_left(1, sende_dy, got_dy))

    size = (z.pad, z.whole)
    row, lane = iota(size, 0), iota(size, 1)
    want = row
    for m in range(1, parts):
        want = want + jnp.where(row >= m * z.main, 1, 0)
    for m in range(parts):
        base = z.image + m * z.mine
        inside = (row >= base) & (row < base + z.mine)
        want = jnp.where(inside, m * z.patches + z.patches - 1, want)
    want = jnp.where(row < z.mix_rows, want, -1)
    pick = jnp.where(want == lane, 1.0, 0.0).astype(BF16)
    spot = jnp.where((iota((z.pad, TILE), 0) == z.ones) & (iota((z.pad, TILE), 1) == 0), 1.0, 0.0)
    for l in range(z.layers):
        half = dot(pick, mixw_ref[:, l, :]).astype(BF16)
        offset = jnp.where(iota((TILE, z.whole), 0) == 0, mixb_ref[l : l + 1, :].astype(F32), 0.0)
        column = dot_nt(pick, offset.astype(BF16)).astype(BF16)
        full = dot_nt(half, pick) + dot_nt(column, spot.astype(BF16))
        mix_m[l] = full.astype(BF16)
        mix_t[l] = full.T.astype(BF16)

    for ref in (dm_ref, dv_ref, dub_ref):
        ref[...] = jnp.zeros(ref.shape, F32)

    def spread_left(got, target):
        tile = parts * z.mine
        row, lane = iota((groups * tile, left_all), 0), iota((groups * tile, left_all), 1)
        want = jnp.full(row.shape, -1, jnp.int32)
        for g in range(groups):
            for m in range(parts):
                base = g * tile + m * z.mine
                inside = (row >= base) & (row < base + z.mine)
                want = jnp.where(inside, row - base + m * z.left + g * z.mine, want)
        matrix = jnp.where(want == lane, 1.0, 0.0).astype(BF16)
        rows = dot(matrix, got[...].reshape(left_all, channels)).astype(BF16)
        for g in range(groups):
            target[g, z.body :, :] = rows[g * tile : (g + 1) * tile]

    def gather_left(source, target):
        tile = parts * z.mine
        row, lane = iota((left_all, groups * tile), 0), iota((left_all, groups * tile), 1)
        want = jnp.full(row.shape, -1, jnp.int32)
        for g in range(groups):
            for m in range(parts):
                base = m * z.left + g * z.mine
                inside = (row >= base) & (row < base + z.mine)
                want = jnp.where(inside, row - base + g * tile + m * z.mine, want)
        matrix = jnp.where(want == lane, 1.0, 0.0).astype(BF16)
        low = 0 if source.shape[1] == tile else z.body
        rows = jnp.concatenate([source[g, low:, :] for g in range(groups)], axis=0)
        target[...] = dot(matrix, rows).astype(BF16).reshape(parts, z.left, channels)

    def vector(ref, l):
        return ref[l : l + 1, :].astype(F32)

    tile_rows = parts * z.mine
    image_of = iota((tile_rows, 1), 0) & (z.mine - 1)
    ones_tile = jnp.where(iota((TILE, channels), 0) == 0, 1.0, 0.0).astype(BF16)

    def image_rows(ref, l, g, j):
        index = (g,) if l is None else (l, g)
        return [
            ref[(*index, pl.ds(m * z.block + j * z.main, z.main), slice(None))] for m in range(parts)
        ]

    def mixed_rows(l, g, j, left):
        gain, shift = vector(mgain_ref, l), vector(mshift_ref, l)
        pieces = [
            (gain * part.astype(F32) + shift).astype(BF16) for part in image_rows(xs, l, g, j)
        ]
        pieces.append(jnp.where(image_of == j, gain * left + shift, 0.0).astype(BF16))
        pieces.append(ones_tile)
        return jnp.concatenate(pieces, axis=0)

    def mix_forward(l, g):
        scale = vector(mscale_ref, l)
        left = xs[l, g, z.body :, :].astype(F32)
        left_total = jnp.zeros((tile_rows, channels), F32)
        for j in range(z.mine):
            mixed = mixed_rows(l, g, j, left)
            across = dot(mix_m[l, : z.mix_rows, : z.mix_cols], mixed)
            for m, part in enumerate(image_rows(xs, l, g, j)):
                rows = part.astype(F32) + scale * across[m * z.main : (m + 1) * z.main]
                firsts[l, g, pl.ds(m * z.block + j * z.main, z.main), :] = rows.astype(BF16)
            left_total = jnp.where(image_of == j, across[z.image :], left_total)
        firsts[l, g, z.body :, :] = (left + scale * left_total).astype(BF16)

    chunk = 512 if hidden % 512 == 0 else 128

    def slot_of(l, g):
        return l * groups + g if keep else 0

    def mlp_hidden(l, g, normed, at):
        bias = upb_ref[l : l + 1, :].astype(F32)
        for h in range(0, hidden, chunk):
            value = dot(normed, up_w[l, :, h : h + chunk]) + bias[:, h : h + chunk]
            active, grade = gelu_pair(value)
            active = active.astype(BF16)
            act[at, :, h : h + chunk] = active
            slope[at, :, h : h + chunk] = grade.astype(BF16)
            yield h, active

    def mlp_normed(l, g):
        rows = firsts[l, g].astype(F32)
        return rows, (vector(pgain_ref, l) * rows + vector(pshift_ref, l)).astype(BF16)

    def mlp_forward(l, g, target):
        rows, normed = mlp_normed(l, g)
        total = None
        for h, active in mlp_hidden(l, g, normed, slot_of(l, g)):
            term = dot(active, down_w[l, h : h + chunk, :])
            total = term if total is None else total + term
        result = rows + vector(pscale_ref, l) * (total + vector(downb_ref, l))
        result = result.astype(BF16)
        if target is not None:
            target[g] = result
        else:
            sent(exchange(0, g, send_x, xs.at[0]))
            send_x[g] = result[: z.body].reshape(parts, z.block, channels)
            outs_left[g] = result[z.body :]

    def mlp_backward(l, g):
        rows, normed = mlp_normed(l, g)
        at = slot_of(l, g)
        if not keep:
            for _ in mlp_hidden(l, g, normed, at):
                pass
        upper = dys[g].astype(F32)
        branch = (vector(pscale_ref, l) * upper).astype(BF16)
        dv_ref[l, 5:6, :] += jnp.sum(branch.astype(F32), axis=0, keepdims=True)
        normed_t, branch_t = normed.T, branch.T
        total = None
        for h in range(0, hidden, chunk):
            span = slice(h, h + chunk)
            back = dot_nt(branch, down_w[l, span, :])
            grad = (back * slope[at, :, span].astype(F32)).astype(BF16)
            dub_ref[l, :, span] += jnp.sum(grad.astype(F32), axis=0, keepdims=True)
            du_ref[:, span] += dot(normed_t, grad)
            dd_ref[:, span] += dot(branch_t, act[at, :, span])
            term = dot_nt(grad, up_w[l, :, span])
            total = term if total is None else total + term
        dv_ref[l, 3:4, :] += jnp.sum(total * rows, axis=0, keepdims=True)
        dv_ref[l, 4:5, :] += jnp.sum(total, axis=0, keepdims=True)
        dys[g] = (upper + vector(pgain_ref, l) * total).astype(BF16)

    def mix_backward(l, g, target):
        gain, scale = vector(mgain_ref, l), vector(mscale_ref, l)
        left = xs[l, g, z.body :, :].astype(F32)
        left_grad = dys[g, z.body :, :].astype(F32)
        left_total = jnp.zeros((tile_rows, channels), F32)
        sums = [jnp.zeros((1, channels), F32) for _ in range(3)]
        for j in range(z.mine):
            mixed = mixed_rows(l, g, j, left)
            grads = [part.astype(F32) for part in image_rows(dys, None, g, j)]
            pieces = [(scale * part).astype(BF16) for part in grads]
            pieces.append(jnp.where(image_of == j, scale * left_grad, 0.0).astype(BF16))
            across = jnp.concatenate(pieces, axis=0)
            dm_ref[l, : z.mix_rows, : z.mix_cols] += dot_nt(across, mixed)
            back = dot(mix_t[l, : z.mix_cols, : z.mix_rows], across)
            for m, part in enumerate(image_rows(xs, l, g, j)):
                some = back[m * z.main : (m + 1) * z.main]
                sums[0] += jnp.sum(some * part.astype(F32), axis=0, keepdims=True)
                sums[1] += jnp.sum(some, axis=0, keepdims=True)
                target[g, pl.ds(m * z.block + j * z.main, z.main), :] = (
                    grads[m] + gain * some
                ).astype(BF16)
            left_total = jnp.where(image_of == j, back[z.image : z.mix_rows], left_total)
            sums[2] += back[z.ones : z.ones + 1]
        sums[0] += jnp.sum(left_total * left, axis=0, keepdims=True)
        sums[1] += jnp.sum(left_total, axis=0, keepdims=True)
        target[g, z.body :, :] = (left_grad + gain * left_total).astype(BF16)
        for k in range(3):
            dv_ref[l, k : k + 1, :] += sums[k]

    for copy in w_loads:
        copy.wait()
    arrive(exchange_left(0, sende_x, got_x))
    spread_left(got_x, xs.at[0])

    def forward(g, carry):
        arrive(exchange(0, g, send_x, xs.at[0]))
        for l in range(z.layers):
            mix_forward(l, g)
            mlp_forward(l, g, xs.at[l + 1] if l + 1 < z.layers else None)
        return carry

    lax.fori_loop(0, groups, forward, 0)
    gather_left(outs_left, out_left)

    arrive(exchange_left(1, sende_dy, got_dy))
    spread_left(got_dy, dys)

    def backward(l):
        def step(g, carry):
            if l == z.layers - 1:
                arrive(exchange(1, g, send_dy, dys))
                start(exchange_back(2, g, send_x, out_w))
            mlp_backward(l, g)
            mix_backward(l, g, dys)
            if l == 0:
                start(exchange_back(3, g, dys, dx_w))
            return carry

        return step

    for l in reversed(range(z.layers)):
        for ref in (du_ref, dd_ref):
            ref[...] = jnp.zeros(ref.shape, F32)
        lax.fori_loop(0, groups, backward(l), 0)
        if l == z.layers - 1:
            start(exchange_left(2, out_left, out_e))

        turned = dd_ref[...] * down_w[l].astype(F32).T
        dv_ref[l, 6:7, :] = jnp.sum(turned, axis=1)[None, :]
        dv_ref[l, 6:7, :] += vector(downb_ref, l) * dv_ref[l, 5:6, :]
        dv_ref[l, 6:7, :] = dv_ref[l, 6:7, :] / vector(pscale_ref, l)
        total = vector(mgain_ref, l) * dv_ref[l, 0:1, :] + vector(mshift_ref, l) * dv_ref[l, 1:2, :]
        dv_ref[l, 2:3, :] = (total + dv_ref[l, 2:3, :]) / vector(mscale_ref, l)
        keeps = [
            pltpu.make_async_copy(du_ref, du_hbm.at[l], load_sem.at[0]),
            pltpu.make_async_copy(dd_ref, dd_hbm.at[l], load_sem.at[1]),
        ]
        for copy in keeps:
            copy.start()
        for copy in keeps:
            copy.wait()

    for g in range(groups):
        sent(exchange(1, g, send_dy, dys))
    sent(exchange_left(0, sende_x, got_x))
    sent(exchange_left(1, sende_dy, got_dy))
    gather_left(dys, sende_x)
    last = exchange_left(3, sende_x, dx_e)
    start(last)
    for copies in [exchange_left(2, out_left, out_e), last]:
        arrive(copies)
        sent(copies)
    for g in range(groups):
        for copies in [exchange_back(2, g, send_x, out_w), exchange_back(3, g, dys, dx_w)]:
            arrive(copies)
            sent(copies)


def finish_kernel(z, mask_ref, out_w, out_e, dx_w, dx_e, out_ref, dx_ref):
    g = pl.program_id(0)
    swap = swap_matrix()
    pick = iota((1, GROUP * TILE), 1) >> 4
    masked = (swap * mask_lanes(mask_ref, g * GROUP, GROUP, pick)).astype(BF16)
    left_all = z.parts * z.left
    row, lane = iota((GROUP, left_all), 0), iota((GROUP, left_all), 1)
    want = row + g * z.mine
    for d in range(1, z.parts):
        want = want + jnp.where(row >= d * z.mine, z.left - z.mine, 0)
    last = jnp.where(want == lane, 1.0, 0.0)
    lanes = jnp.zeros((GROUP, 1), F32)
    for k in range(GROUP):
        lanes = jnp.where(iota((GROUP, 1), 0) == k, mask_ref[g * GROUP + k].astype(F32), lanes)
    for wire, left, target, matrix, tail in (
        (out_w, out_e, out_ref, masked, (last * lanes).astype(BF16)),
        (dx_w, dx_e, dx_ref, swap.astype(BF16), last.astype(BF16)),
    ):
        for t in range(z.main // TILE):
            block = jnp.concatenate(
                [
                    wire[0, i * z.main + t * TILE : i * z.main + (t + 1) * TILE, :]
                    for i in range(GROUP)
                ],
                axis=0,
            )
            rows = dot(matrix, block).reshape(TILE, GROUP, z.channels)
            target[t * TILE : (t + 1) * TILE] = rows.astype(target.dtype)
        rows = dot(tail, left[...].reshape(left_all, z.channels))
        target[z.patches - 1] = rows.astype(target.dtype)


def local(parts, images_in, out_grad, slot_mask, mix_gain, mix_shift, mix_scale, mix_weight, mix_bias,
          mlp_gain, mlp_shift, mlp_scale, up_weight, up_bias, down_weight, down_bias):
    slots, patches, channels = images_in.shape
    layers, _, hidden = up_weight.shape
    z = Sizes(parts, slots, patches, channels, hidden, layers)
    keep = layers * z.groups * z.rows * hidden * 4 <= 30e6
    kept = layers * z.groups if keep else 1
    vmem = pl.BlockSpec(memory_space=pltpu.VMEM)
    smem = pl.BlockSpec(memory_space=pltpu.SMEM)
    hbm = pl.BlockSpec(memory_space=pl.ANY)
    wire = jax.ShapeDtypeStruct((z.groups, parts, z.block, channels), BF16)
    left = jax.ShapeDtypeStruct((parts, z.left, channels), BF16)
    dma = pltpu.SemaphoreType.DMA
    rows = (z.groups, z.rows, channels)
    out_w, out_e, dx_w, dx_e, du, dd, dm, dv, dub = pl.pallas_call(
        functools.partial(whole_kernel, z, keep),
        out_shape=(
            wire, left, wire, left,
            jax.ShapeDtypeStruct((layers, channels, hidden), F32),
            jax.ShapeDtypeStruct((layers, channels, hidden), F32),
            jax.ShapeDtypeStruct((layers, z.pad, z.pad), F32),
            jax.ShapeDtypeStruct((layers, 8, channels), F32),
            jax.ShapeDtypeStruct((layers, 1, hidden), F32),
        ),
        in_specs=[hbm, hbm, smem] + [vmem] * 10 + [hbm, hbm],
        out_specs=(hbm,) * 6 + (vmem,) * 3,
        scratch_shapes=[
            pltpu.VMEM((channels, hidden), F32),
            pltpu.VMEM((channels, hidden), F32),
            pltpu.VMEM((z.groups, patches, GROUP, channels), BF16),
            pltpu.VMEM((z.groups, parts, z.block, channels), BF16),
            pltpu.VMEM((z.groups, parts, z.block, channels), BF16),
            pltpu.VMEM((parts, z.left, channels), BF16),
            pltpu.VMEM((parts, z.left, channels), BF16),
            pltpu.VMEM((parts, z.left, channels), BF16),
            pltpu.VMEM((parts, z.left, channels), BF16),
            pltpu.VMEM((layers, *rows), BF16),
            pltpu.VMEM((layers, *rows), BF16),
            pltpu.VMEM(rows, BF16),
            pltpu.VMEM((z.groups, parts * z.mine, channels), BF16),
            pltpu.VMEM((parts, z.left, channels), BF16),
            pltpu.VMEM((kept, z.rows, hidden), BF16),
            pltpu.VMEM((kept, z.rows, hidden), BF16),
            pltpu.VMEM((layers, channels, hidden), BF16),
            pltpu.VMEM((layers, hidden, channels), BF16),
            pltpu.VMEM((layers, z.pad, z.pad), BF16),
            pltpu.VMEM((layers, z.pad, z.pad), BF16),
            dma((2 * z.groups + 2,)),
            dma((4, z.groups)),
            dma((4, z.groups, parts)),
            dma((4, z.groups, parts)),
            dma((4, parts)),
            dma((4, parts)),
        ],
        compiler_params=pltpu.CompilerParams(
            collective_id=0, has_side_effects=True, vmem_limit_bytes=64 << 20
        ),
        name="layers",
    )(
        jnp.transpose(images_in, (1, 0, 2)),
        jnp.transpose(out_grad, (1, 0, 2)),
        slot_mask,
        jnp.transpose(mix_weight, (1, 0, 2)),
        mix_bias, mix_gain, mix_shift, mix_scale, mlp_gain, mlp_shift, mlp_scale, down_bias, up_bias,
        up_weight, down_weight,
    )

    flat = (z.groups, parts * z.block, channels)
    block = pl.BlockSpec((1, *flat[1:]), lambda g: (g, 0, 0))
    whole = pl.BlockSpec(left.shape, lambda g: (0, 0, 0))
    turned = pl.BlockSpec((patches, GROUP, channels), lambda g: (0, g, 0))
    output, input_grad = pl.pallas_call(
        functools.partial(finish_kernel, z),
        grid=(z.groups,),
        out_shape=(
            jax.ShapeDtypeStruct((patches, slots, channels), BF16),
            jax.ShapeDtypeStruct((patches, slots, channels), F32),
        ),
        in_specs=[smem, block, whole, block, whole],
        out_specs=(turned, turned),
        name="finish",
    )(slot_mask, out_w.reshape(flat), out_e, dx_w.reshape(flat), dx_e)
    output = jnp.transpose(output, (1, 0, 2))
    input_grad = jnp.transpose(input_grad, (1, 0, 2))

    main = dm[:, : z.image, : z.image].reshape(layers, parts, z.main, parts, z.main)
    edge_q = dm[:, : z.image, z.image : z.mix_rows].reshape(layers, parts, z.main, parts, z.mine).sum(-1)
    edge_p = dm[:, z.image : z.mix_rows, : z.image].reshape(layers, parts, z.mine, parts, z.main).sum(2)
    corner = dm[:, z.image : z.mix_rows, z.image : z.mix_rows].reshape(layers, parts, z.mine, parts, z.mine).sum((2, 4))
    top = jnp.concatenate([main, edge_q[..., None]], axis=-1)
    low = jnp.concatenate([edge_p, corner[..., None]], axis=-1)
    weight = jnp.concatenate([top, low[:, :, None]], axis=2).reshape(layers, z.whole, z.whole)
    bias_main = dm[:, : z.image, z.ones].reshape(layers, parts, z.main)
    bias_edge = dm[:, z.image : z.mix_rows, z.ones].reshape(layers, parts, z.mine).sum(-1)
    bias = jnp.concatenate([bias_main, bias_edge[..., None]], axis=-1).reshape(layers, z.whole)
    shares = [dv[:, 0], dv[:, 1], dv[:, 2], weight, bias, dv[:, 3], dv[:, 4], dv[:, 6], du, dub[:, 0], dd, dv[:, 5]]
    axes = [1, 1, 1, 1, 1, 1, 1, 1, 2, 1, 2, 1]
    shares = tuple(
        lax.psum_scatter(share, "mix", scatter_dimension=axis, tiled=True)
        for share, axis in zip(shares, axes)
    )
    grads = list(lax.psum(shares, "dp"))
    grads[10] = jnp.swapaxes(grads[10], 1, 2)
    return (output, input_grad, *grads)


def solution(mesh):
    in_specs = (P("dp", "mix", None), P("dp", "mix", None), P("dp")) + (P(),) * 12
    out_specs = (
        P("dp", "mix", None),
        P("dp", "mix", None),
        P(None, "mix"),
        P(None, "mix"),
        P(None, "mix"),
        P(None, "mix", None),
        P(None, "mix"),
        P(None, "mix"),
        P(None, "mix"),
        P(None, "mix"),
        P(None, None, "mix"),
        P(None, "mix"),
        P(None, "mix", None),
        P(None, "mix"),
    )
    return jax.shard_map(
        functools.partial(local, mesh.shape["mix"]),
        mesh=mesh,
        in_specs=in_specs,
        out_specs=out_specs,
        check_vma=False,
    )
```

```python
import functools
import math

import jax
import jax.numpy as jnp
from jax import lax
from jax.experimental import pallas as pl
from jax.experimental.pallas import tpu as pltpu
from jax.sharding import PartitionSpec as P

MESH = pl.DeviceIdType.MESH
F32 = jnp.float32
BF16 = jnp.bfloat16
GROUP = 16
TILE = 16
TANH_A = math.sqrt(2.0 / math.pi)
TANH_B = TANH_A * 0.044715


def dot(a, b):
    return jnp.dot(a, b, preferred_element_type=F32)


def dot_nt(a, b):
    return lax.dot_general(a, b, (((1,), (1,)), ((), ())), preferred_element_type=F32)


def iota(shape, axis):
    return lax.broadcasted_iota(jnp.int32, shape, axis)


def gelu_pair(value):
    square = value * value
    curve = jnp.tanh(value * (TANH_A + TANH_B * square))
    half = 0.5 * value
    gate = 0.5 * curve + 0.5
    slope = gate + (half * (1.0 - curve * curve)) * (TANH_A + (3.0 * TANH_B) * square)
    return value * gate, slope


def mask_lanes(mask_ref, first, count, pick):
    total = jnp.zeros(pick.shape, F32)
    for k in range(count):
        total = jnp.where(pick == k, mask_ref[first + k].astype(F32), total)
    return total


def swap_matrix():
    side = GROUP * TILE
    row, lane = iota((side, side), 0), iota((side, side), 1)
    return jnp.where((row >> 4) + ((row & 15) << 4) == lane, 1.0, 0.0)


class Sizes:
    def __init__(self, parts, copies, slots, patches, channels, hidden, layers):
        self.parts = parts
        self.slots = slots
        self.patches = patches
        self.channels = channels
        self.hidden = hidden
        self.layers = layers
        self.groups = slots // GROUP
        self.mine = GROUP // parts
        self.main = patches // TILE * TILE
        self.block = self.mine * self.main
        self.body = parts * self.block
        self.rows = self.body + parts * self.mine
        self.image = parts * self.main
        self.mix_rows = self.image + parts * self.mine
        self.ones = self.mix_rows
        self.mix_cols = self.mix_rows + TILE
        self.pad = -(-self.mix_cols // 128) * 128
        self.left = -(-self.groups * self.mine // TILE) * TILE
        self.whole = parts * patches
        self.quarters = hidden // channels
        self.far = min(copies // 2, 4)
        self.rest = copies // (2 * self.far)
        cuts = 2 * self.far
        step = TILE * cuts
        tail = self.main + 2 * TILE
        self.job_rows = [-(-count // step) * step for count in (channels, channels + tail)]
        self.shares = [count // cuts for count in self.job_rows]
        act_rows = 2 * self.quarters * self.rows * self.groups
        at = (layers - 1) * act_rows
        self.places = []
        for layer in range(layers):
            for kind in range(2):
                count, share = self.job_rows[kind], self.shares[kind]
                place = {}
                for name, size in (
                    ("pay", 4 * count),
                    ("got_pair", 2 * count),
                    ("got_near", count),
                    ("got_far", (self.far - 1) * 2 * share),
                    ("got_cross", share),
                    ("got_rest", (self.rest - 1) * share),
                    ("final", share),
                ):
                    place[name] = at
                    at += size
                self.places.append(place)
        self.kept_rows = max(at, layers * act_rows)


def whole_kernel(
    z,
    x_hbm, dy_hbm, mask_ref, mixw_ref, mixb_ref,
    mgain_ref, mshift_ref, mscale_ref, pgain_ref, pshift_ref, pscale_ref, downb_ref, upb_ref,
    up_hbm, down_hbm,
    out_w, out_e, dx_w, dx_e, sum_d, sum_u,
    du_ref, dd_ref, dm_ref, dv_ref, dub_ref, stage, send_x, send_dy, sende_x, sende_dy, got_x, got_dy,
    xs, firsts, dys, outs_left, out_left, kept, up_w, down_w, mix_m, mix_t,
    load_sem, own_sem, send_sem, recv_sem, lsend_sem, lrecv_sem, job_send, job_recv, free_sem,
):
    dp, me = lax.axis_index("dp"), lax.axis_index("mix")
    parts, groups, channels, hidden = z.parts, z.groups, z.channels, z.hidden
    peers = [lax.rem(me + r, parts) for r in range(parts)]

    loads = []
    for k, hbm in enumerate((x_hbm, dy_hbm)):
        for g in range(groups):
            loads.append(
                pltpu.make_async_copy(
                    hbm.at[:, pl.ds(g * GROUP, GROUP), :], stage.at[g], load_sem.at[k * groups + g]
                )
            )
    w_loads = [
        pltpu.make_async_copy(up_hbm, up_w, load_sem.at[2 * groups]),
        pltpu.make_async_copy(down_hbm, down_w, load_sem.at[2 * groups + 1]),
    ]
    for copy in loads[:groups] + w_loads:
        copy.start()

    barrier = pltpu.get_barrier_semaphore()
    near, upper_place = lax.rem(dp, 2), lax.div(dp, 2)
    far, rest = lax.rem(upper_place, z.far), lax.div(upper_place, z.far)
    row_peers = [(dp, peers[r]) for r in range(1, parts)]
    near_peer = (dp + 1 - 2 * near, me)
    far_places = [lax.rem(far + r, z.far) for r in range(z.far)]
    far_peers = [((rest * z.far + far_places[r]) * 2 + near, me) for r in range(z.far)]
    rest_peers = [
        ((lax.rem(rest + r, z.rest) * z.far + far) * 2 + near, me) for r in range(z.rest)
    ]
    job_peers = row_peers + [near_peer] + far_peers[1:] + rest_peers[1:]
    for peer in job_peers:
        pl.semaphore_signal(barrier, inc=1, device_id=peer, device_id_type=MESH)

    swap = swap_matrix()
    swap_b = swap.astype(BF16)
    left_all = parts * z.left

    def convert(send, g, matrix):
        for t in range(z.main // TILE):
            block = stage[g, t * TILE : (t + 1) * TILE].reshape(TILE * GROUP, channels)
            rows = dot(matrix, block).astype(BF16).reshape(GROUP, TILE, channels)
            for d in range(parts):
                for j in range(z.mine):
                    send[g, d, j * z.main + t * TILE : j * z.main + (t + 1) * TILE, :] = rows[
                        d * z.mine + j
                    ]

    def convert_left(send, lanes):
        row, lane = iota((left_all, z.slots), 0), iota((left_all, z.slots), 1)
        want = jnp.full(row.shape, -1, jnp.int32)
        for d in range(parts):
            for g in range(groups):
                base = d * z.left + g * z.mine
                inside = (row >= base) & (row < base + z.mine)
                want = jnp.where(inside, row - base + g * GROUP + d * z.mine, want)
        matrix = jnp.where(want == lane, 1.0, 0.0)
        if lanes is not None:
            matrix = matrix * lanes
        last = jnp.concatenate([stage[g, z.patches - 1] for g in range(groups)], axis=0)
        send[...] = dot(matrix.astype(BF16), last).astype(BF16).reshape(parts, z.left, channels)

    def exchange(k, g, send, target):
        copies = [lambda: pltpu.make_async_copy(send.at[g, me], target.at[g, pl.ds(me * z.block, z.block)], own_sem.at[k, g])]
        for r in range(1, parts):
            copies.append(
                pltpu.make_async_remote_copy(
                    src_ref=send.at[g, peers[r]],
                    dst_ref=target.at[g, pl.ds(me * z.block, z.block)],
                    send_sem=send_sem.at[k, g, r],
                    recv_sem=recv_sem.at[k, g, r],
                    device_id=(dp, peers[r]),
                    device_id_type=MESH,
                )
            )
        return copies

    def part_of(source, g, d):
        if len(source.shape) == 4:
            return source.at[g, d]
        return source.at[g, pl.ds(d * z.block, z.block)]

    def exchange_back(k, g, source, target):
        copies = [lambda: pltpu.make_async_copy(part_of(source, g, me), target.at[g, me], own_sem.at[k, g])]
        for r in range(1, parts):
            copies.append(
                pltpu.make_async_remote_copy(
                    src_ref=part_of(source, g, peers[r]),
                    dst_ref=target.at[g, me],
                    send_sem=send_sem.at[k, g, r],
                    recv_sem=recv_sem.at[k, g, r],
                    device_id=(dp, peers[r]),
                    device_id_type=MESH,
                )
            )
        return copies

    def exchange_left(k, send, target):
        copies = [lambda: pltpu.make_async_copy(send.at[me], target.at[me], lsend_sem.at[k, 0])]
        for r in range(1, parts):
            copies.append(
                pltpu.make_async_remote_copy(
                    src_ref=send.at[peers[r]],
                    dst_ref=target.at[me],
                    send_sem=lsend_sem.at[k, r],
                    recv_sem=lrecv_sem.at[k, r],
                    device_id=(dp, peers[r]),
                    device_id_type=MESH,
                )
            )
        return copies

    def start(copies):
        copies[0]().start()
        for copy in copies[1:]:
            copy.start()

    def arrive(copies):
        copies[0]().wait()
        for copy in copies[1:]:
            copy.wait_recv()

    def sent(copies):
        for copy in copies[1:]:
            copy.wait_send()

    for g in range(groups):
        loads[g].wait()
        convert(send_x, g, swap_b)
        if g == 0:
            pl.semaphore_wait(barrier, len(job_peers))
        start(exchange(0, g, send_x, xs.at[0]))
    convert_left(sende_x, None)
    for copy in loads[groups:]:
        copy.start()
    start(exchange_left(0, sende_x, got_x))
    for g in range(groups):
        loads[groups + g].wait()
        pick = iota((1, GROUP * TILE), 1) & 15
        lanes = mask_lanes(mask_ref, g * GROUP, GROUP, pick)
        convert(send_dy, g, (swap * lanes).astype(BF16))
        start(exchange(1, g, send_dy, dys))
    convert_left(sende_dy, mask_lanes(mask_ref, 0, z.slots, iota((1, z.slots), 1)))
    start(exchange_left(1, sende_dy, got_dy))

    size = (z.pad, z.whole)
    row, lane = iota(size, 0), iota(size, 1)
    want = row
    for m in range(1, parts):
        want = want + jnp.where(row >= m * z.main, 1, 0)
    for m in range(parts):
        base = z.image + m * z.mine
        inside = (row >= base) & (row < base + z.mine)
        want = jnp.where(inside, m * z.patches + z.patches - 1, want)
    want = jnp.where(row < z.mix_rows, want, -1)
    pick = jnp.where(want == lane, 1.0, 0.0).astype(BF16)
    spot = jnp.where((iota((z.pad, TILE), 0) == z.ones) & (iota((z.pad, TILE), 1) == 0), 1.0, 0.0)
    for l in range(z.layers):
        half = dot(pick, mixw_ref[:, l, :]).astype(BF16)
        offset = jnp.where(iota((TILE, z.whole), 0) == 0, mixb_ref[l : l + 1, :].astype(F32), 0.0)
        column = dot_nt(pick, offset.astype(BF16)).astype(BF16)
        full = dot_nt(half, pick) + dot_nt(column, spot.astype(BF16))
        mix_m[l] = full.astype(BF16)
        mix_t[l] = full.T.astype(BF16)

    for ref in (dm_ref, dv_ref, dub_ref):
        ref[...] = jnp.zeros(ref.shape, F32)

    def spread_left(got, target):
        tile = parts * z.mine
        row, lane = iota((groups * tile, left_all), 0), iota((groups * tile, left_all), 1)
        want = jnp.full(row.shape, -1, jnp.int32)
        for g in range(groups):
            for m in range(parts):
                base = g * tile + m * z.mine
                inside = (row >= base) & (row < base + z.mine)
                want = jnp.where(inside, row - base + m * z.left + g * z.mine, want)
        matrix = jnp.where(want == lane, 1.0, 0.0).astype(BF16)
        rows = dot(matrix, got[...].reshape(left_all, channels)).astype(BF16)
        for g in range(groups):
            target[g, z.body :, :] = rows[g * tile : (g + 1) * tile]

    def gather_left(source, target):
        tile = parts * z.mine
        row, lane = iota((left_all, groups * tile), 0), iota((left_all, groups * tile), 1)
        want = jnp.full(row.shape, -1, jnp.int32)
        for g in range(groups):
            for m in range(parts):
                base = m * z.left + g * z.mine
                inside = (row >= base) & (row < base + z.mine)
                want = jnp.where(inside, row - base + g * tile + m * z.mine, want)
        matrix = jnp.where(want == lane, 1.0, 0.0).astype(BF16)
        low = 0 if source.shape[1] == tile else z.body
        rows = jnp.concatenate([source[g, low:, :] for g in range(groups)], axis=0)
        target[...] = dot(matrix, rows).astype(BF16).reshape(parts, z.left, channels)

    def vector(ref, l):
        return ref[l : l + 1, :].astype(F32)

    tile_rows = parts * z.mine
    image_of = iota((tile_rows, 1), 0) & (z.mine - 1)
    ones_tile = jnp.where(iota((TILE, channels), 0) == 0, 1.0, 0.0).astype(BF16)

    def image_rows(ref, l, g, j):
        index = (g,) if l is None else (l, g)
        return [
            ref[(*index, pl.ds(m * z.block + j * z.main, z.main), slice(None))] for m in range(parts)
        ]

    def mixed_rows(l, g, j, left):
        gain, shift = vector(mgain_ref, l), vector(mshift_ref, l)
        pieces = [
            (gain * part.astype(F32) + shift).astype(BF16) for part in image_rows(xs, l, g, j)
        ]
        pieces.append(jnp.where(image_of == j, gain * left + shift, 0.0).astype(BF16))
        pieces.append(ones_tile)
        return jnp.concatenate(pieces, axis=0)

    def mix_forward(l, g):
        scale = vector(mscale_ref, l)
        left = xs[l, g, z.body :, :].astype(F32)
        left_total = jnp.zeros((tile_rows, channels), F32)
        for j in range(z.mine):
            mixed = mixed_rows(l, g, j, left)
            across = dot(mix_m[l, : z.mix_rows, : z.mix_cols], mixed)
            for m, part in enumerate(image_rows(xs, l, g, j)):
                rows = part.astype(F32) + scale * across[m * z.main : (m + 1) * z.main]
                firsts[l, g, pl.ds(m * z.block + j * z.main, z.main), :] = rows.astype(BF16)
            left_total = jnp.where(image_of == j, across[z.image :], left_total)
        firsts[l, g, z.body :, :] = (left + scale * left_total).astype(BF16)

    chunk = 512 if hidden % 512 == 0 else 128
    back_chunk = 512 if hidden % 512 == 0 else 128

    def kept_at(l, which, g, quarter):
        index = (l * 2 + which) * groups + g
        start = (index * z.quarters + quarter) * z.rows
        return start if isinstance(start, int) else pl.multiple_of(start, TILE)

    def pieces_of(h, chunk):
        pieces, at = [], h
        while at < h + chunk:
            quarter, lane = divmod(at, channels)
            end = min(channels, lane + h + chunk - at)
            pieces.append((quarter, lane, end))
            at += end - lane
        return pieces

    def keep_rows(l, which, g, h, value, chunk, first):
        value, at = value.astype(BF16), 0
        for quarter, lane, end in pieces_of(h, chunk):
            place = pl.ds(kept_at(l, which, g, quarter) + first, value.shape[0])
            kept[place, lane:end] = value[:, at : at + end - lane]
            at += end - lane

    def kept_rows(l, which, g, h, chunk):
        parts_ = [
            kept[pl.ds(kept_at(l, which, g, quarter), z.rows), lane:end]
            for quarter, lane, end in pieces_of(h, chunk)
        ]
        return jnp.concatenate(parts_, axis=1)

    def mlp_hidden(l, g, normed, first):
        bias = upb_ref[l : l + 1, :].astype(F32)
        for h in range(0, hidden, chunk):
            value = dot(normed, up_w[l, :, h : h + chunk]) + bias[:, h : h + chunk]
            active, grade = gelu_pair(value)
            active = active.astype(BF16)
            keep_rows(l, 0, g, h, active, chunk, first)
            keep_rows(l, 1, g, h, grade, chunk, first)
            yield h, active

    def mlp_normed(l, g, span=slice(None)):
        rows = firsts[l, g, span, :].astype(F32)
        return rows, (vector(pgain_ref, l) * rows + vector(pshift_ref, l)).astype(BF16)

    middle = z.rows // 2 // TILE * TILE
    spans = (slice(0, middle), slice(middle, z.rows))

    def mlp_forward(l, g, target):
        for span in spans:
            rows, normed = mlp_normed(l, g, span)
            total = None
            for h, active in mlp_hidden(l, g, normed, span.start):
                term = dot(active, down_w[l, h : h + chunk, :])
                total = term if total is None else total + term
            result = rows + vector(pscale_ref, l) * (total + vector(downb_ref, l))
            result = result.astype(BF16)
            if target is not None:
                target[g, span, :] = result
                continue
            if span.start == 0:
                sent(exchange(0, g, send_x, xs.at[0]))
            for d in range(parts):
                low, high = max(span.start, d * z.block), min(span.stop, (d + 1) * z.block)
                if low < high:
                    send_x[g, d, low - d * z.block : high - d * z.block, :] = result[
                        low - span.start : high - span.start
                    ]
            if span.stop == z.rows:
                outs_left[g] = result[z.body - span.start :]

    def mlp_backward_down(l, g):
        branch = (vector(pscale_ref, l) * dys[g].astype(F32)).astype(BF16)
        dv_ref[l, 5:6, :] += jnp.sum(branch.astype(F32), axis=0, keepdims=True)
        branch_t = branch.T
        for h in range(0, hidden, back_chunk):
            span = slice(h, h + back_chunk)
            dd_ref[:, span] += dot(branch_t, kept_rows(l, 0, g, h, back_chunk))

    def mlp_backward_up(l, g):
        rows, normed = mlp_normed(l, g)
        upper = dys[g].astype(F32)
        branch = (vector(pscale_ref, l) * upper).astype(BF16)
        normed_t = normed.T
        total = None
        for h in range(0, hidden, back_chunk):
            span = slice(h, h + back_chunk)
            back = dot_nt(branch, down_w[l, span, :])
            grad = (back * kept_rows(l, 1, g, h, back_chunk).astype(F32)).astype(BF16)
            dub_ref[l, :, span] += jnp.sum(grad.astype(F32), axis=0, keepdims=True)
            du_ref[:, span] += dot(normed_t, grad)
            term = dot_nt(grad, up_w[l, :, span])
            total = term if total is None else total + term
        dv_ref[l, 3:4, :] += jnp.sum(total * rows, axis=0, keepdims=True)
        dv_ref[l, 4:5, :] += jnp.sum(total, axis=0, keepdims=True)
        dys[g] = (upper + vector(pgain_ref, l) * total).astype(BF16)

    def mix_backward(l, g, target):
        gain, scale = vector(mgain_ref, l), vector(mscale_ref, l)
        left = xs[l, g, z.body :, :].astype(F32)
        left_grad = dys[g, z.body :, :].astype(F32)
        left_total = jnp.zeros((tile_rows, channels), F32)
        sums = [jnp.zeros((1, channels), F32) for _ in range(3)]
        for j in range(z.mine):
            mixed = mixed_rows(l, g, j, left)
            grads = [part.astype(F32) for part in image_rows(dys, None, g, j)]
            pieces = [(scale * part).astype(BF16) for part in grads]
            pieces.append(jnp.where(image_of == j, scale * left_grad, 0.0).astype(BF16))
            across = jnp.concatenate(pieces, axis=0)
            dm_ref[l, : z.mix_rows, : z.mix_cols] += dot_nt(across, mixed)
            back = dot(mix_t[l, : z.mix_cols, : z.mix_rows], across)
            for m, part in enumerate(image_rows(xs, l, g, j)):
                some = back[m * z.main : (m + 1) * z.main]
                sums[0] += jnp.sum(some * part.astype(F32), axis=0, keepdims=True)
                sums[1] += jnp.sum(some, axis=0, keepdims=True)
                target[g, pl.ds(m * z.block + j * z.main, z.main), :] = (
                    grads[m] + gain * some
                ).astype(BF16)
            left_total = jnp.where(image_of == j, back[z.image : z.mix_rows], left_total)
            sums[2] += back[z.ones : z.ones + 1]
        sums[0] += jnp.sum(left_total * left, axis=0, keepdims=True)
        sums[1] += jnp.sum(left_total, axis=0, keepdims=True)
        target[g, z.body :, :] = (left_grad + gain * left_total).astype(BF16)
        for k in range(3):
            dv_ref[l, k : k + 1, :] += sums[k]

    for copy in w_loads:
        copy.wait()
    arrive(exchange_left(0, sende_x, got_x))
    spread_left(got_x, xs.at[0])

    def forward(g, carry):
        arrive(exchange(0, g, send_x, xs.at[0]))
        for l in range(z.layers):
            mix_forward(l, g)
            mlp_forward(l, g, xs.at[l + 1] if l + 1 < z.layers else None)
        return carry

    lax.fori_loop(0, groups, forward, 0)
    gather_left(outs_left, out_left)

    arrive(exchange_left(1, sende_dy, got_dy))
    spread_left(got_dy, dys)

    low, high = lax.rem(me, 2), lax.div(me, 2)
    pair_peer = (dp, high * 2 + 1 - low)
    cross_peer = (dp, (1 - high) * 2 + low)

    def aligned(start):
        return start if isinstance(start, int) else pl.multiple_of(start, TILE)

    def span_of(start, count):
        return pl.ds(aligned(start), count)

    def remote(job, slot, source, target, peer):
        return pltpu.make_async_remote_copy(
            src_ref=source,
            dst_ref=target,
            send_sem=job_send.at[job, slot],
            recv_sem=job_recv.at[job, slot],
            device_id=peer,
            device_id_type=MESH,
        )

    class Job:
        def __init__(self, layer, kind):
            self.layer, self.kind = layer, kind
            self.number = layer * 2 + kind
            self.rows, self.share = z.job_rows[kind], z.shares[kind]
            self.place = z.places[self.number]
            self.sums = (sum_d, sum_u)[kind].at[layer]
            self.own = self.place["pay"] + low * 2 * self.rows
            self.half = self.own + near * self.rows
            self.mine = self.half + far * 2 * self.share

        def fill(self, tile_of):
            for chunk_ in range(parts):
                for t in range(self.rows // TILE):
                    k, inner = divmod(t * TILE, self.share)
                    at = self.place["pay"] + (chunk_ % 2) * 2 * self.rows
                    at += (k * 2 + chunk_ // 2) * self.share + inner
                    value = tile_of(chunk_, t)
                    if value is None:
                        kept[at : at + TILE, :] = jnp.zeros((TILE, channels), BF16)
                    else:
                        kept[at : at + TILE, : value.shape[1]] = value.astype(BF16)
                        if value.shape[1] < channels:
                            rest = channels - value.shape[1]
                            kept[at : at + TILE, value.shape[1] :] = jnp.zeros((TILE, rest), BF16)

        def pair_copy(self):
            source = kept.at[span_of(self.place["pay"] + (1 - low) * 2 * self.rows, 2 * self.rows)]
            target = kept.at[span_of(self.place["got_pair"], 2 * self.rows)]
            return remote(self.number, 0, source, target, pair_peer)

        def near_copy(self):
            source = kept.at[span_of(self.own + (1 - near) * self.rows, self.rows)]
            target = kept.at[span_of(self.place["got_near"], self.rows)]
            return remote(self.number, 1, source, target, near_peer)

        def far_copy(self, r):
            source = kept.at[span_of(self.half + far_places[r] * 2 * self.share, 2 * self.share)]
            target = kept.at[span_of(self.place["got_far"] + (r - 1) * 2 * self.share, 2 * self.share)]
            return remote(self.number, 3 + r, source, target, far_peers[r])

        def cross_copy(self):
            source = kept.at[span_of(self.mine + (1 - high) * self.share, self.share)]
            target = kept.at[span_of(self.place["got_cross"], self.share)]
            return remote(self.number, 2, source, target, cross_peer)

        def place_of(self, near_, far_):
            return self.sums.at[span_of((near_ * z.far + far_) * self.share, self.share)]

        def share_copy(self, r):
            source = kept.at[span_of(self.place["final"], self.share)]
            return remote(self.number, 3 + z.far + r, source, self.place_of(near, far), far_peers[r])

        def rest_copy(self, r):
            source = kept.at[span_of(self.mine + high * self.share, self.share)]
            target = kept.at[span_of(self.place["got_rest"] + (r - 1) * self.share, self.share)]
            return remote(self.number, 3 + 2 * z.far + r, source, target, rest_peers[r])

        def own_copy(self):
            source = kept.at[span_of(self.place["final"], self.share)]
            return pltpu.make_async_copy(source, self.place_of(near, far), own_sem.at[4, self.number])

        def back_copy(self):
            block = self.sums.at[span_of(near * z.far * self.share, z.far * self.share)]
            return remote(self.number, 3, block, block, near_peer)

        def add(self, start, count, *others):
            for at in range(0, count, 8 * TILE):
                size = min(8 * TILE, count - at)
                total = kept[span_of(start + at, size), :].astype(F32)
                for other in others:
                    total += kept[span_of(other + at, size), :].astype(F32)
                yield at, size, total.astype(BF16)

        def step(self, number):
            if number == 0:
                self.pair_copy().start()
            elif number == 1:
                self.pair_copy().wait_recv()
                for half in (1 - near, near):
                    start = half * self.rows
                    for at, size, total in self.add(
                        self.own + start, self.rows, self.place["got_pair"] + start
                    ):
                        kept[span_of(self.own + start + at, size), :] = total
                    if half is not near:
                        self.near_copy().start()
            elif number == 2:
                self.near_copy().wait_recv()
                for at, size, total in self.add(self.half, self.rows, self.place["got_near"]):
                    kept[span_of(self.half + at, size), :] = total
                for r in range(1, z.far):
                    self.far_copy(r).start()
            elif number == 3:
                for r in range(1, z.far):
                    self.far_copy(r).wait_recv()
                others = [self.place["got_far"] + (r - 1) * 2 * self.share for r in range(1, z.far)]
                for at, size, total in self.add(self.mine, 2 * self.share, *others):
                    kept[span_of(self.mine + at, size), :] = total
                self.cross_copy().start()
            elif number == 4:
                self.cross_copy().wait_recv()
                start = self.mine + high * self.share
                for at, size, total in self.add(start, self.share, self.place["got_cross"]):
                    kept[span_of(start + at, size), :] = total
                for r in range(1, z.rest):
                    self.rest_copy(r).start()
                for r in range(1, z.rest):
                    self.rest_copy(r).wait_recv()
                others = [self.place["got_rest"] + r * self.share for r in range(z.rest - 1)]
                for at, size, total in self.add(start, self.share, *others):
                    kept[span_of(self.place["final"] + at, size), :] = total
                self.own_copy().start()
                for r in range(1, z.far):
                    self.share_copy(r).start()
            elif number == 5:
                self.own_copy().wait()
                for r in range(1, z.far):
                    self.share_copy(r).wait_recv()
                self.back_copy().start()
            else:
                self.back_copy().wait()
                self.pair_copy().wait_send()
                self.near_copy().wait_send()
                self.cross_copy().wait_send()
                for r in range(1, z.far):
                    self.far_copy(r).wait_send()
                    self.share_copy(r).wait_send()
                for r in range(1, z.rest):
                    self.rest_copy(r).wait_send()

    def chunk_lanes(ref, chunk_):
        return slice(chunk_ * channels, (chunk_ + 1) * channels)

    def down_tile(chunk_, t):
        if t * TILE >= channels:
            return None
        return dd_ref[t * TILE : (t + 1) * TILE, chunk_lanes(dd_ref, chunk_)]

    def up_tile(l):
        def tile_of(chunk_, t):
            at = t * TILE
            if at < channels:
                return du_ref[at : at + TILE, chunk_lanes(du_ref, chunk_)]
            at -= channels
            if at < z.main:
                return dm_ref[l, chunk_ * z.main + at : chunk_ * z.main + at + TILE, :]
            if at == z.main:
                return dm_ref[l, z.image : z.image + TILE, :]
            if at == z.main + TILE:
                bias = dub_ref[l, :, chunk_lanes(dub_ref, chunk_)]
                rows = [dv_ref[l, 0:7, :], bias, jnp.zeros((TILE - 8, channels), F32)]
                return jnp.concatenate(rows, axis=0)
            return None

        return tile_of

    def down_sums(l):
        total = None
        for h in range(0, hidden, 2 * 128):
            span = slice(h, h + 2 * 128)
            term = dd_ref[:, span].T * down_w[l, span, :].astype(F32)
            total = term if total is None else total + term
        total = jnp.sum(total, axis=0, keepdims=True) + vector(downb_ref, l) * dv_ref[l, 5:6, :]
        dv_ref[l, 6:7, :] = total / vector(pscale_ref, l)

    def mix_sums(l):
        total = vector(mgain_ref, l) * dv_ref[l, 0:1, :] + vector(mshift_ref, l) * dv_ref[l, 1:2, :]
        dv_ref[l, 2:3, :] = (total + dv_ref[l, 2:3, :]) / vector(mscale_ref, l)

    jobs = {(l, kind): Job(l, kind) for l in range(z.layers) for kind in range(2)}
    top = z.layers - 1

    def clear(*refs):
        for ref in refs:
            ref[...] = jnp.zeros(ref.shape, F32)

    def backward_top(g, carry):
        arrive(exchange(1, g, send_dy, dys))
        start(exchange_back(2, g, send_x, out_w))
        mlp_backward_down(top, g)
        mlp_backward_up(top, g)
        mix_backward(top, g, dys)
        return carry

    clear(du_ref, dd_ref)
    lax.fori_loop(0, groups, backward_top, 0)
    start(exchange_left(2, out_left, out_e))
    for peer in job_peers:
        pl.semaphore_signal(free_sem, inc=1, device_id=peer, device_id_type=MESH)
    down_sums(top)
    mix_sums(top)
    jobs[top, 0].fill(down_tile)
    jobs[top, 1].fill(up_tile(top))
    pl.semaphore_wait(free_sem, len(job_peers))
    jobs[top, 0].step(0)
    jobs[top, 1].step(0)

    def backward_down(l):
        def step(g, carry):
            mlp_backward_down(l, g)
            return carry

        return step

    def backward_up(l, g):
        mlp_backward_up(l, g)
        mix_backward(l, g, dys)
        if l == 0:
            start(exchange_back(3, g, dys, dx_w))

    plan = {
        (0, 0): [(top, 0, 1), (top, 1, 1)],
        (0, 1): [(top, 0, 2), (0, 0, 1)],
        (0, 2): [(top, 1, 2), (top, 0, 3)],
        (0, 3): [(0, 0, 2), (top, 0, 4), (top, 1, 3)],
        (0, 4): [(0, 1, 1), (top, 1, 4), (0, 0, 3), (top, 0, 5), (0, 1, 2), (0, 0, 4), (top, 1, 5), (0, 1, 3), (0, 0, 5),
                 (0, 1, 4), (0, 1, 5), (top, 0, 6), (top, 1, 6), (0, 0, 6), (0, 1, 6)],
    }

    def run(point):
        for l, kind, number in plan.get(point, ()):
            jobs[l, kind].step(number)

    clear(du_ref, dd_ref)
    lax.fori_loop(0, groups, backward_down(0), 0)
    run((0, 0))
    down_sums(0)
    jobs[0, 0].fill(down_tile)
    jobs[0, 0].step(0)
    thirds = [groups * k // 3 for k in range(4)]
    for k in range(3):
        def step(g, carry):
            backward_up(0, g)
            return carry

        lax.fori_loop(thirds[k], thirds[k + 1], step, 0)
        run((0, k + 1))
    mix_sums(0)
    jobs[0, 1].fill(up_tile(0))
    jobs[0, 1].step(0)
    run((0, 4))

    for g in range(groups):
        sent(exchange(1, g, send_dy, dys))
    sent(exchange_left(0, sende_x, got_x))
    sent(exchange_left(1, sende_dy, got_dy))
    gather_left(dys, sende_x)
    last = exchange_left(3, sende_x, dx_e)
    start(last)
    for copies in [exchange_left(2, out_left, out_e), last]:
        arrive(copies)
        sent(copies)
    for g in range(groups):
        for copies in [exchange_back(2, g, send_x, out_w), exchange_back(3, g, dys, dx_w)]:
            arrive(copies)
            sent(copies)


def finish_kernel(
    z, mask_ref, out_w, out_e, dx_w, dx_e, sum_d, sum_u,
    out_ref, dx_ref, gain_ref, shift_ref, scale_ref, mixw_ref, mixb_ref, pgain_ref, pshift_ref, pscale_ref,
    up_ref, upb_ref, down_ref, downb_ref,
):
    g = pl.program_id(0)
    swap = swap_matrix()
    pick = iota((1, GROUP * TILE), 1) >> 4
    masked = (swap * mask_lanes(mask_ref, g * GROUP, GROUP, pick)).astype(BF16)
    left_all = z.parts * z.left
    row, lane = iota((GROUP, left_all), 0), iota((GROUP, left_all), 1)
    want = row + g * z.mine
    for d in range(1, z.parts):
        want = want + jnp.where(row >= d * z.mine, z.left - z.mine, 0)
    last = jnp.where(want == lane, 1.0, 0.0)
    lanes = jnp.zeros((GROUP, 1), F32)
    for k in range(GROUP):
        lanes = jnp.where(iota((GROUP, 1), 0) == k, mask_ref[g * GROUP + k].astype(F32), lanes)
    for wire, left, target, matrix, tail in (
        (out_w, out_e, out_ref, masked, (last * lanes).astype(BF16)),
        (dx_w, dx_e, dx_ref, swap.astype(BF16), last.astype(BF16)),
    ):
        for t in range(z.main // TILE):
            block = jnp.concatenate(
                [
                    wire[0, i * z.main + t * TILE : i * z.main + (t + 1) * TILE, :]
                    for i in range(GROUP)
                ],
                axis=0,
            )
            rows = dot(matrix, block).reshape(TILE, GROUP, z.channels)
            target[t * TILE : (t + 1) * TILE] = rows.astype(target.dtype)
        rows = dot(tail, left[...].reshape(left_all, z.channels))
        target[z.patches - 1] = rows.astype(target.dtype)


    @pl.when(g == 0)
    def _():
        me = lax.axis_index("mix")
        channels, share = z.channels, z.channels // z.parts
        row, lane = iota((z.pad, z.whole), 0), iota((z.pad, z.whole), 1)
        want = row
        for m in range(1, z.parts):
            want = want + jnp.where(row >= m * z.main, 1, 0)
        for m in range(z.parts):
            base = z.image + m * z.mine
            inside = (row >= base) & (row < base + z.mine)
            want = jnp.where(inside, m * z.patches + z.patches - 1, want)
        want = jnp.where(row < z.mix_rows, want, -1)
        order = jnp.where(want == lane, 1.0, 0.0).astype(BF16)
        lanes_in, lanes_out = iota((channels, share), 0), iota((channels, share), 1)
        own = jnp.where(lanes_in == lanes_out + me * share, 1.0, 0.0).astype(BF16)
        size = z.main + TILE
        at = iota((size, 1), 0) - z.main - me * z.mine
        edge = jnp.where((at >= 0) & (at < z.mine), 1.0, 0.0)
        fold_row, fold_lane = iota((size, z.patches), 0), iota((size, z.patches), 1)
        fold_at = fold_row - z.main - me * z.mine
        fold_to = jnp.where(
            fold_row < z.main, fold_row, jnp.where((fold_at >= 0) & (fold_at < z.mine), z.main, -1)
        )
        fold = jnp.where(fold_to == fold_lane, 1.0, 0.0).astype(BF16)
        spot = jnp.where((iota((8, z.pad), 0) == 0) & (iota((8, z.pad), 1) == z.ones), 1.0, 0.0)
        for l in range(z.layers):
            up_ref[l] = sum_u[l, :channels, :].astype(F32)
            down_ref[l] = sum_d[l, :channels, :].astype(F32).T
            rows = sum_u[l, channels : channels + size, : z.pad]
            weight = dot(rows, order)
            mixw_ref[: z.main, l, :] = weight[: z.main]
            mixw_ref[z.main, l : l + 1, :] = jnp.sum(weight * edge, axis=0, keepdims=True)
            bias = dot_nt(spot.astype(BF16), rows).astype(BF16)
            mixb_ref[l : l + 1, :] = dot(bias, fold)[:1]
            tile = sum_u[l, channels + size : channels + size + TILE, :]
            vectors = dot(tile, own)
            for k, ref in enumerate(
                (gain_ref, shift_ref, scale_ref, pgain_ref, pshift_ref, downb_ref, pscale_ref)
            ):
                ref[l : l + 1, :] = vectors[k : k + 1]
            upb_ref[l : l + 1, :] = tile[7:8, :].astype(F32)


def local(parts, copies, images_in, out_grad, slot_mask, mix_gain, mix_shift, mix_scale, mix_weight, mix_bias,
          mlp_gain, mlp_shift, mlp_scale, up_weight, up_bias, down_weight, down_bias):
    slots, patches, channels = images_in.shape
    layers, _, hidden = up_weight.shape
    z = Sizes(parts, copies, slots, patches, channels, hidden, layers)
    vmem = pl.BlockSpec(memory_space=pltpu.VMEM)
    smem = pl.BlockSpec(memory_space=pltpu.SMEM)
    hbm = pl.BlockSpec(memory_space=pl.ANY)
    wire = jax.ShapeDtypeStruct((z.groups, parts, z.block, channels), BF16)
    left = jax.ShapeDtypeStruct((parts, z.left, channels), BF16)
    dma = pltpu.SemaphoreType.DMA
    rows = (z.groups, z.rows, channels)
    out_w, out_e, dx_w, dx_e, sum_d, sum_u = pl.pallas_call(
        functools.partial(whole_kernel, z),
        out_shape=(
            wire, left, wire, left,
            jax.ShapeDtypeStruct((layers, z.job_rows[0], channels), BF16),
            jax.ShapeDtypeStruct((layers, z.job_rows[1], channels), BF16),
        ),
        in_specs=[hbm, hbm, smem] + [vmem] * 10 + [hbm, hbm],
        out_specs=(hbm,) * 6,
        scratch_shapes=[
            pltpu.VMEM((channels, hidden), F32),
            pltpu.VMEM((channels, hidden), F32),
            pltpu.VMEM((layers, z.pad, z.pad), F32),
            pltpu.VMEM((layers, 8, channels), F32),
            pltpu.VMEM((layers, 1, hidden), F32),
            pltpu.VMEM((z.groups, patches, GROUP, channels), BF16),
            pltpu.VMEM((z.groups, parts, z.block, channels), BF16),
            pltpu.VMEM((z.groups, parts, z.block, channels), BF16),
            pltpu.VMEM((parts, z.left, channels), BF16),
            pltpu.VMEM((parts, z.left, channels), BF16),
            pltpu.VMEM((parts, z.left, channels), BF16),
            pltpu.VMEM((parts, z.left, channels), BF16),
            pltpu.VMEM((layers, *rows), BF16),
            pltpu.VMEM((layers, *rows), BF16),
            pltpu.VMEM(rows, BF16),
            pltpu.VMEM((z.groups, parts * z.mine, channels), BF16),
            pltpu.VMEM((parts, z.left, channels), BF16),
            pltpu.VMEM((z.kept_rows, channels), BF16),
            pltpu.VMEM((layers, channels, hidden), BF16),
            pltpu.VMEM((layers, hidden, channels), BF16),
            pltpu.VMEM((layers, z.pad, z.pad), BF16),
            pltpu.VMEM((layers, z.pad, z.pad), BF16),
            dma((2 * z.groups + 2,)),
            dma((5, max(z.groups, 2 * layers))),
            dma((4, z.groups, parts)),
            dma((4, z.groups, parts)),
            dma((4, parts)),
            dma((4, parts)),
            dma((2 * layers, 3 + 2 * z.far + z.rest)),
            dma((2 * layers, 3 + 2 * z.far + z.rest)),
            pltpu.SemaphoreType.REGULAR,
        ],
        compiler_params=pltpu.CompilerParams(
            collective_id=0, has_side_effects=True, vmem_limit_bytes=64 << 20
        ),
        name="layers",
    )(
        jnp.transpose(images_in, (1, 0, 2)),
        jnp.transpose(out_grad, (1, 0, 2)),
        slot_mask,
        jnp.transpose(mix_weight, (1, 0, 2)),
        mix_bias, mix_gain, mix_shift, mix_scale, mlp_gain, mlp_shift, mlp_scale, down_bias, up_bias,
        up_weight, down_weight,
    )

    flat = (z.groups, parts * z.block, channels)
    block = pl.BlockSpec((1, *flat[1:]), lambda g: (g, 0, 0))
    whole = pl.BlockSpec(left.shape, lambda g: (0, 0, 0))
    turned = pl.BlockSpec((patches, GROUP, channels), lambda g: (0, g, 0))
    share = channels // parts
    small = jax.ShapeDtypeStruct((layers, share), F32)
    small_block = pl.BlockSpec(small.shape, lambda g: (0, 0))
    shapes = [
        jax.ShapeDtypeStruct((patches, slots, channels), BF16),
        jax.ShapeDtypeStruct((patches, slots, channels), F32),
        small, small, small,
        jax.ShapeDtypeStruct((patches, layers, z.whole), F32),
        jax.ShapeDtypeStruct((layers, patches), F32),
        small, small, small,
        jax.ShapeDtypeStruct((layers, channels, hidden // parts), F32),
        jax.ShapeDtypeStruct((layers, hidden // parts), F32),
        jax.ShapeDtypeStruct((layers, hidden // parts, channels), F32),
        small,
    ]

    def fixed(shape):
        return pl.BlockSpec(shape, lambda g: (0,) * len(shape))

    sums = [fixed(sum_d.shape), fixed(sum_u.shape)]
    results = list(
        pl.pallas_call(
            functools.partial(finish_kernel, z),
            grid=(z.groups,),
            out_shape=shapes,
            in_specs=[smem, block, whole, block, whole] + sums,
            out_specs=[turned, turned] + [fixed(shape.shape) for shape in shapes[2:]],
            compiler_params=pltpu.CompilerParams(vmem_limit_bytes=48 << 20),
            name="finish",
        )(slot_mask, out_w.reshape(flat), out_e, dx_w.reshape(flat), dx_e, sum_d, sum_u)
    )
    for k in (0, 1, 5):
        results[k] = jnp.transpose(results[k], (1, 0, 2))
    return tuple(results)


def solution(mesh):
    in_specs = (P("dp", "mix", None), P("dp", "mix", None), P("dp")) + (P(),) * 12
    out_specs = (
        P("dp", "mix", None),
        P("dp", "mix", None),
        P(None, "mix"),
        P(None, "mix"),
        P(None, "mix"),
        P(None, "mix", None),
        P(None, "mix"),
        P(None, "mix"),
        P(None, "mix"),
        P(None, "mix"),
        P(None, None, "mix"),
        P(None, "mix"),
        P(None, "mix", None),
        P(None, "mix"),
    )
    return jax.shard_map(
        functools.partial(local, mesh.shape["mix"], mesh.shape["dp"]),
        mesh=mesh,
        in_specs=in_specs,
        out_specs=out_specs,
        check_vma=False,
    )
```

```python
import functools
import math

import jax
import jax.numpy as jnp
from jax import lax
from jax.experimental import pallas as pl
from jax.experimental.pallas import tpu as pltpu
from jax.sharding import PartitionSpec as P

MESH = pl.DeviceIdType.MESH
F32 = jnp.float32
BF16 = jnp.bfloat16
GROUP = 16
TILE = 16
TANH_A = math.sqrt(2.0 / math.pi)
TANH_B = TANH_A * 0.044715


def dot(a, b):
    return jnp.dot(a, b, preferred_element_type=F32)


def dot_nt(a, b):
    return lax.dot_general(a, b, (((1,), (1,)), ((), ())), preferred_element_type=F32)


def iota(shape, axis):
    return lax.broadcasted_iota(jnp.int32, shape, axis)


def gelu_pair(value):
    square = value * value
    curve = jnp.tanh(value * (TANH_A + TANH_B * square))
    half = 0.5 * value
    gate = 0.5 * curve + 0.5
    slope = gate + (half * (1.0 - curve * curve)) * (TANH_A + (3.0 * TANH_B) * square)
    return value * gate, slope


def mask_lanes(mask_ref, first, count, pick):
    total = jnp.zeros(pick.shape, F32)
    for k in range(count):
        total = jnp.where(pick == k, mask_ref[first + k].astype(F32), total)
    return total


def swap_matrix():
    side = GROUP * TILE
    row, lane = iota((side, side), 0), iota((side, side), 1)
    return jnp.where((row >> 4) + ((row & 15) << 4) == lane, 1.0, 0.0)


class Sizes:
    def __init__(self, parts, copies, slots, patches, channels, hidden, layers):
        self.parts = parts
        self.slots = slots
        self.patches = patches
        self.channels = channels
        self.hidden = hidden
        self.layers = layers
        self.groups = slots // GROUP
        self.mine = GROUP // parts
        self.main = patches // TILE * TILE
        self.block = self.mine * self.main
        self.body = parts * self.block
        self.rows = self.body + parts * self.mine
        self.image = parts * self.main
        self.mix_rows = self.image + parts * self.mine
        self.ones = self.mix_rows
        self.mix_cols = self.mix_rows + TILE
        self.pad = -(-self.mix_cols // 128) * 128
        self.left = -(-self.groups * self.mine // TILE) * TILE
        self.whole = parts * patches
        self.quarters = hidden // channels
        self.far = min(copies // 2, 4)
        self.rest = copies // (2 * self.far)
        cuts = 2 * self.far
        step = TILE * cuts
        self.split = channels * 2 // 3 // TILE * TILE
        counts = (channels, self.split, channels - self.split + self.main + 2 * TILE)
        self.job_rows = [-(-count // step) * step for count in counts]
        self.job_at = [sum(self.job_rows[:kind]) for kind in range(3)]
        self.shares = [count // cuts for count in self.job_rows]
        act_rows = self.quarters * self.rows * self.groups
        self.places = []
        for layer in range(layers):
            at = (2 * (layers - 1) + layers - 1 - layer) * act_rows
            for kind in range(3):
                count, share = self.job_rows[kind], self.shares[kind]
                place = {}
                for name, size in (
                    ("pay", 4 * count),
                    ("got_pair", 2 * count),
                    ("got_near", count),
                    ("got_far", (self.far - 1) * 2 * share),
                    ("got_cross", share),
                    ("got_rest", (self.rest - 1) * share),
                    ("final", share),
                ):
                    place[name] = at
                    at += size
                self.places.append(place)
        self.kept_rows = max(at, 2 * layers * act_rows)


def whole_kernel(
    z,
    x_hbm, dy_hbm, mask_ref, mixw_ref, mixb_ref,
    mgain_ref, mshift_ref, mscale_ref, pgain_ref, pshift_ref, pscale_ref, downb_ref, upb_ref,
    up_hbm, down_hbm,
    out_w, out_e, dx_w, dx_e, sums_hbm,
    du_ref, dd_ref, dm_ref, dv_ref, dub_ref, stage, send_x, send_dy, sende_x, sende_dy, got_x, got_dy,
    xs, firsts, dys, outs_left, out_left, kept, up_w, down_w, mix_m, mix_t,
    load_sem, own_sem, send_sem, recv_sem, lsend_sem, lrecv_sem, job_send, job_recv, free_sem,
):
    dp, me = lax.axis_index("dp"), lax.axis_index("mix")
    parts, groups, channels, hidden = z.parts, z.groups, z.channels, z.hidden
    peers = [lax.rem(me + r, parts) for r in range(parts)]

    loads = []
    for k, hbm in enumerate((x_hbm, dy_hbm)):
        for g in range(groups):
            loads.append(
                pltpu.make_async_copy(
                    hbm.at[:, pl.ds(g * GROUP, GROUP), :], stage.at[g], load_sem.at[k * groups + g]
                )
            )
    w_loads = [
        pltpu.make_async_copy(up_hbm, up_w, load_sem.at[2 * groups]),
        pltpu.make_async_copy(down_hbm, down_w, load_sem.at[2 * groups + 1]),
    ]
    for copy in loads[:groups] + w_loads:
        copy.start()

    barrier = pltpu.get_barrier_semaphore()
    near, upper_place = lax.rem(dp, 2), lax.div(dp, 2)
    far, rest = lax.rem(upper_place, z.far), lax.div(upper_place, z.far)
    row_peers = [(dp, peers[r]) for r in range(1, parts)]
    near_peer = (dp + 1 - 2 * near, me)
    far_places = [lax.rem(far + r, z.far) for r in range(z.far)]
    far_peers = [((rest * z.far + far_places[r]) * 2 + near, me) for r in range(z.far)]
    rest_peers = [
        ((lax.rem(rest + r, z.rest) * z.far + far) * 2 + near, me) for r in range(z.rest)
    ]
    job_peers = row_peers + [near_peer] + far_peers[1:] + rest_peers[1:]
    for peer in job_peers:
        pl.semaphore_signal(barrier, inc=1, device_id=peer, device_id_type=MESH)

    swap = swap_matrix()
    swap_b = swap.astype(BF16)
    left_all = parts * z.left

    def convert(send, g, matrix):
        for t in range(z.main // TILE):
            block = stage[g, t * TILE : (t + 1) * TILE].reshape(TILE * GROUP, channels)
            rows = dot(matrix, block).astype(BF16).reshape(GROUP, TILE, channels)
            for d in range(parts):
                for j in range(z.mine):
                    send[g, d, j * z.main + t * TILE : j * z.main + (t + 1) * TILE, :] = rows[
                        d * z.mine + j
                    ]

    def convert_left(send, lanes):
        row, lane = iota((left_all, z.slots), 0), iota((left_all, z.slots), 1)
        want = jnp.full(row.shape, -1, jnp.int32)
        for d in range(parts):
            for g in range(groups):
                base = d * z.left + g * z.mine
                inside = (row >= base) & (row < base + z.mine)
                want = jnp.where(inside, row - base + g * GROUP + d * z.mine, want)
        matrix = jnp.where(want == lane, 1.0, 0.0)
        if lanes is not None:
            matrix = matrix * lanes
        last = jnp.concatenate([stage[g, z.patches - 1] for g in range(groups)], axis=0)
        send[...] = dot(matrix.astype(BF16), last).astype(BF16).reshape(parts, z.left, channels)

    def exchange(k, g, send, target):
        copies = [lambda: pltpu.make_async_copy(send.at[g, me], target.at[g, pl.ds(me * z.block, z.block)], own_sem.at[k, g])]
        for r in range(1, parts):
            copies.append(
                pltpu.make_async_remote_copy(
                    src_ref=send.at[g, peers[r]],
                    dst_ref=target.at[g, pl.ds(me * z.block, z.block)],
                    send_sem=send_sem.at[k, g, r],
                    recv_sem=recv_sem.at[k, g, r],
                    device_id=(dp, peers[r]),
                    device_id_type=MESH,
                )
            )
        return copies

    def part_of(source, g, d):
        if len(source.shape) == 4:
            return source.at[g, d]
        return source.at[g, pl.ds(d * z.block, z.block)]

    def exchange_back(k, g, source, target):
        copies = [lambda: pltpu.make_async_copy(part_of(source, g, me), target.at[g, me], own_sem.at[k, g])]
        for r in range(1, parts):
            copies.append(
                pltpu.make_async_remote_copy(
                    src_ref=part_of(source, g, peers[r]),
                    dst_ref=target.at[g, me],
                    send_sem=send_sem.at[k, g, r],
                    recv_sem=recv_sem.at[k, g, r],
                    device_id=(dp, peers[r]),
                    device_id_type=MESH,
                )
            )
        return copies

    def exchange_left(k, send, target):
        copies = [lambda: pltpu.make_async_copy(send.at[me], target.at[me], lsend_sem.at[k, 0])]
        for r in range(1, parts):
            copies.append(
                pltpu.make_async_remote_copy(
                    src_ref=send.at[peers[r]],
                    dst_ref=target.at[me],
                    send_sem=lsend_sem.at[k, r],
                    recv_sem=lrecv_sem.at[k, r],
                    device_id=(dp, peers[r]),
                    device_id_type=MESH,
                )
            )
        return copies

    def start(copies):
        copies[0]().start()
        for copy in copies[1:]:
            copy.start()

    def arrive(copies):
        copies[0]().wait()
        for copy in copies[1:]:
            copy.wait_recv()

    def sent(copies):
        for copy in copies[1:]:
            copy.wait_send()

    for g in range(groups):
        if g == 0:
            loads[g].wait()
        convert(send_x, g, swap_b)
        if g == 0:
            pl.semaphore_wait(barrier, len(job_peers))
        start(exchange(0, g, send_x, xs.at[0]))
        if g == 0:
            for copy in loads[1:groups]:
                copy.wait()
            convert_left(sende_x, None)
            start(exchange_left(0, sende_x, got_x))
    for copy in loads[groups:]:
        copy.start()
    for g in range(groups):
        loads[groups + g].wait()
        pick = iota((1, GROUP * TILE), 1) & 15
        lanes = mask_lanes(mask_ref, g * GROUP, GROUP, pick)
        convert(send_dy, g, (swap * lanes).astype(BF16))
        start(exchange(1, g, send_dy, dys))
    convert_left(sende_dy, mask_lanes(mask_ref, 0, z.slots, iota((1, z.slots), 1)))
    start(exchange_left(1, sende_dy, got_dy))

    size = (z.pad, z.whole)
    row, lane = iota(size, 0), iota(size, 1)
    want = row
    for m in range(1, parts):
        want = want + jnp.where(row >= m * z.main, 1, 0)
    for m in range(parts):
        base = z.image + m * z.mine
        inside = (row >= base) & (row < base + z.mine)
        want = jnp.where(inside, m * z.patches + z.patches - 1, want)
    want = jnp.where(row < z.mix_rows, want, -1)
    pick = jnp.where(want == lane, 1.0, 0.0).astype(BF16)
    spot = jnp.where((iota((z.pad, TILE), 0) == z.ones) & (iota((z.pad, TILE), 1) == 0), 1.0, 0.0)
    for l in range(z.layers):
        half = dot(pick, mixw_ref[:, l, :]).astype(BF16)
        offset = jnp.where(iota((TILE, z.whole), 0) == 0, mixb_ref[l : l + 1, :].astype(F32), 0.0)
        column = dot_nt(pick, offset.astype(BF16)).astype(BF16)
        full = dot_nt(half, pick) + dot_nt(column, spot.astype(BF16))
        mix_m[l] = full.astype(BF16)
        mix_t[l] = full.T.astype(BF16)

    for ref in (dm_ref, dv_ref, dub_ref):
        ref[...] = jnp.zeros(ref.shape, F32)

    def spread_left(got, target):
        tile = parts * z.mine
        row, lane = iota((groups * tile, left_all), 0), iota((groups * tile, left_all), 1)
        want = jnp.full(row.shape, -1, jnp.int32)
        for g in range(groups):
            for m in range(parts):
                base = g * tile + m * z.mine
                inside = (row >= base) & (row < base + z.mine)
                want = jnp.where(inside, row - base + m * z.left + g * z.mine, want)
        matrix = jnp.where(want == lane, 1.0, 0.0).astype(BF16)
        rows = dot(matrix, got[...].reshape(left_all, channels)).astype(BF16)
        for g in range(groups):
            target[g, z.body :, :] = rows[g * tile : (g + 1) * tile]

    def gather_left(source, target):
        tile = parts * z.mine
        row, lane = iota((left_all, groups * tile), 0), iota((left_all, groups * tile), 1)
        want = jnp.full(row.shape, -1, jnp.int32)
        for g in range(groups):
            for m in range(parts):
                base = m * z.left + g * z.mine
                inside = (row >= base) & (row < base + z.mine)
                want = jnp.where(inside, row - base + g * tile + m * z.mine, want)
        matrix = jnp.where(want == lane, 1.0, 0.0).astype(BF16)
        low = 0 if source.shape[1] == tile else z.body
        rows = jnp.concatenate([source[g, low:, :] for g in range(groups)], axis=0)
        target[...] = dot(matrix, rows).astype(BF16).reshape(parts, z.left, channels)

    def vector(ref, l):
        return ref[l : l + 1, :].astype(F32)

    tile_rows = parts * z.mine
    image_of = iota((tile_rows, 1), 0) & (z.mine - 1)
    ones_tile = jnp.where(iota((TILE, channels), 0) == 0, 1.0, 0.0).astype(BF16)

    def image_rows(ref, l, g, j):
        index = (g,) if l is None else (l, g)
        return [
            ref[(*index, pl.ds(m * z.block + j * z.main, z.main), slice(None))] for m in range(parts)
        ]

    def mixed_rows(l, g, j, left):
        gain, shift = vector(mgain_ref, l), vector(mshift_ref, l)
        pieces = [
            (gain * part.astype(F32) + shift).astype(BF16) for part in image_rows(xs, l, g, j)
        ]
        pieces.append(jnp.where(image_of == j, gain * left + shift, 0.0).astype(BF16))
        pieces.append(ones_tile)
        return jnp.concatenate(pieces, axis=0)

    def mix_forward(l, g):
        scale = vector(mscale_ref, l)
        left = xs[l, g, z.body :, :].astype(F32)
        left_total = jnp.zeros((tile_rows, channels), F32)
        for j in range(z.mine):
            mixed = mixed_rows(l, g, j, left)
            across = dot(mix_m[l, : z.mix_rows, : z.mix_cols], mixed)
            for m, part in enumerate(image_rows(xs, l, g, j)):
                rows = part.astype(F32) + scale * across[m * z.main : (m + 1) * z.main]
                firsts[l, g, pl.ds(m * z.block + j * z.main, z.main), :] = rows.astype(BF16)
            left_total = jnp.where(image_of == j, across[z.image :], left_total)
        firsts[l, g, z.body :, :] = (left + scale * left_total).astype(BF16)

    chunk = 512 if hidden % 512 == 0 else 128
    back_chunk = 512 if hidden % 512 == 0 else 128

    def kept_at(l, which, g, quarter):
        index = (l * 2 + which) * groups + g
        start = (index * z.quarters + quarter) * z.rows
        return start if isinstance(start, int) else pl.multiple_of(start, TILE)

    def pieces_of(h, chunk):
        pieces, at = [], h
        while at < h + chunk:
            quarter, lane = divmod(at, channels)
            end = min(channels, lane + h + chunk - at)
            pieces.append((quarter, lane, end))
            at += end - lane
        return pieces

    def keep_rows(l, which, g, h, value, chunk, first):
        value, at = value.astype(BF16), 0
        for quarter, lane, end in pieces_of(h, chunk):
            place = pl.ds(kept_at(l, which, g, quarter) + first, value.shape[0])
            kept[place, lane:end] = value[:, at : at + end - lane]
            at += end - lane

    def kept_rows(l, which, g, h, chunk):
        parts_ = [
            kept[pl.ds(kept_at(l, which, g, quarter), z.rows), lane:end]
            for quarter, lane, end in pieces_of(h, chunk)
        ]
        return jnp.concatenate(parts_, axis=1)

    def mlp_hidden(l, g, normed, first):
        bias = upb_ref[l : l + 1, :].astype(F32)
        for h in range(0, hidden, chunk):
            value = dot(normed, up_w[l, :, h : h + chunk]) + bias[:, h : h + chunk]
            active, grade = gelu_pair(value)
            active = active.astype(BF16)
            keep_rows(l, 0, g, h, active, chunk, first)
            keep_rows(l, 1, g, h, grade, chunk, first)
            yield h, active

    def mlp_normed(l, g, span=slice(None)):
        rows = firsts[l, g, span, :].astype(F32)
        return rows, (vector(pgain_ref, l) * rows + vector(pshift_ref, l)).astype(BF16)

    middle = z.rows // 2 // TILE * TILE
    spans = (slice(0, middle), slice(middle, z.rows))

    def mlp_forward(l, g, target):
        for span in spans:
            rows, normed = mlp_normed(l, g, span)
            total = None
            for h, active in mlp_hidden(l, g, normed, span.start):
                term = dot(active, down_w[l, h : h + chunk, :])
                total = term if total is None else total + term
            result = rows + vector(pscale_ref, l) * (total + vector(downb_ref, l))
            result = result.astype(BF16)
            if target is not None:
                target[g, span, :] = result
                continue
            if span.start == 0:
                sent(exchange(0, g, send_x, xs.at[0]))
            for d in range(parts):
                low, high = max(span.start, d * z.block), min(span.stop, (d + 1) * z.block)
                if low < high:
                    send_x[g, d, low - d * z.block : high - d * z.block, :] = result[
                        low - span.start : high - span.start
                    ]
            if span.stop == z.rows:
                outs_left[g] = result[z.body - span.start :]

    def mlp_backward_down(l, g):
        branch = (vector(pscale_ref, l) * dys[g].astype(F32)).astype(BF16)
        dv_ref[l, 5:6, :] += jnp.sum(branch.astype(F32), axis=0, keepdims=True)
        branch_t = branch.T
        for h in range(0, hidden, back_chunk):
            span = slice(h, h + back_chunk)
            dd_ref[:, span] += dot(branch_t, kept_rows(l, 0, g, h, back_chunk))

    def mlp_backward_up(l, g):
        rows, normed = mlp_normed(l, g)
        upper = dys[g].astype(F32)
        branch = (vector(pscale_ref, l) * upper).astype(BF16)
        normed_t = normed.T
        total = None
        for h in range(0, hidden, back_chunk):
            span = slice(h, h + back_chunk)
            back = dot_nt(branch, down_w[l, span, :])
            grad = (back * kept_rows(l, 1, g, h, back_chunk).astype(F32)).astype(BF16)
            dub_ref[l, :, span] += jnp.sum(grad.astype(F32), axis=0, keepdims=True)
            du_ref[:, span] += dot(normed_t, grad)
            term = dot_nt(grad, up_w[l, :, span])
            total = term if total is None else total + term
        dv_ref[l, 3:4, :] += jnp.sum(total * rows, axis=0, keepdims=True)
        dv_ref[l, 4:5, :] += jnp.sum(total, axis=0, keepdims=True)
        dys[g] = (upper + vector(pgain_ref, l) * total).astype(BF16)

    def mix_backward(l, g, target):
        gain, scale = vector(mgain_ref, l), vector(mscale_ref, l)
        left = xs[l, g, z.body :, :].astype(F32)
        left_grad = dys[g, z.body :, :].astype(F32)
        left_total = jnp.zeros((tile_rows, channels), F32)
        sums = [jnp.zeros((1, channels), F32) for _ in range(3)]
        for j in range(z.mine):
            mixed = mixed_rows(l, g, j, left)
            grads = [part.astype(F32) for part in image_rows(dys, None, g, j)]
            pieces = [(scale * part).astype(BF16) for part in grads]
            pieces.append(jnp.where(image_of == j, scale * left_grad, 0.0).astype(BF16))
            across = jnp.concatenate(pieces, axis=0)
            dm_ref[l, : z.mix_rows, : z.mix_cols] += dot_nt(across, mixed)
            back = dot(mix_t[l, : z.mix_cols, : z.mix_rows], across)
            for m, part in enumerate(image_rows(xs, l, g, j)):
                some = back[m * z.main : (m + 1) * z.main]
                sums[0] += jnp.sum(some * part.astype(F32), axis=0, keepdims=True)
                sums[1] += jnp.sum(some, axis=0, keepdims=True)
                target[g, pl.ds(m * z.block + j * z.main, z.main), :] = (
                    grads[m] + gain * some
                ).astype(BF16)
            left_total = jnp.where(image_of == j, back[z.image : z.mix_rows], left_total)
            sums[2] += back[z.ones : z.ones + 1]
        sums[0] += jnp.sum(left_total * left, axis=0, keepdims=True)
        sums[1] += jnp.sum(left_total, axis=0, keepdims=True)
        target[g, z.body :, :] = (left_grad + gain * left_total).astype(BF16)
        for k in range(3):
            dv_ref[l, k : k + 1, :] += sums[k]

    for copy in w_loads:
        copy.wait()
    arrive(exchange_left(0, sende_x, got_x))
    spread_left(got_x, xs.at[0])

    def forward(g, carry):
        arrive(exchange(0, g, send_x, xs.at[0]))
        for l in range(z.layers):
            mix_forward(l, g)
            mlp_forward(l, g, xs.at[l + 1] if l + 1 < z.layers else None)
        return carry

    lax.fori_loop(0, groups, forward, 0)
    gather_left(outs_left, out_left)

    arrive(exchange_left(1, sende_dy, got_dy))
    spread_left(got_dy, dys)

    low, high = lax.rem(me, 2), lax.div(me, 2)
    pair_peer = (dp, high * 2 + 1 - low)
    cross_peer = (dp, (1 - high) * 2 + low)

    def aligned(start):
        return start if isinstance(start, int) else pl.multiple_of(start, TILE)

    def span_of(start, count):
        return pl.ds(aligned(start), count)

    def remote(job, slot, source, target, peer):
        return pltpu.make_async_remote_copy(
            src_ref=source,
            dst_ref=target,
            send_sem=job_send.at[job, slot],
            recv_sem=job_recv.at[job, slot],
            device_id=peer,
            device_id_type=MESH,
        )

    class Job:
        def __init__(self, layer, kind):
            self.layer, self.kind = layer, kind
            self.number = layer * 3 + kind
            self.rows, self.share = z.job_rows[kind], z.shares[kind]
            self.place = z.places[self.number]
            self.sums = sums_hbm.at[layer]
            self.own = self.place["pay"] + low * 2 * self.rows
            self.half = self.own + near * self.rows
            self.mine = self.half + far * 2 * self.share

        def fill(self, tile_of):
            for chunk_ in range(parts):
                for t in range(self.rows // TILE):
                    k, inner = divmod(t * TILE, self.share)
                    at = self.place["pay"] + (chunk_ % 2) * 2 * self.rows
                    at += (k * 2 + chunk_ // 2) * self.share + inner
                    value = tile_of(chunk_, t)
                    if value is None:
                        kept[at : at + TILE, :] = jnp.zeros((TILE, channels), BF16)
                    else:
                        kept[at : at + TILE, : value.shape[1]] = value.astype(BF16)
                        if value.shape[1] < channels:
                            rest = channels - value.shape[1]
                            kept[at : at + TILE, value.shape[1] :] = jnp.zeros((TILE, rest), BF16)

        def pair_copy(self):
            source = kept.at[span_of(self.place["pay"] + (1 - low) * 2 * self.rows, 2 * self.rows)]
            target = kept.at[span_of(self.place["got_pair"], 2 * self.rows)]
            return remote(self.number, 0, source, target, pair_peer)

        def near_copy(self):
            source = kept.at[span_of(self.own + (1 - near) * self.rows, self.rows)]
            target = kept.at[span_of(self.place["got_near"], self.rows)]
            return remote(self.number, 1, source, target, near_peer)

        def far_copy(self, r):
            source = kept.at[span_of(self.half + far_places[r] * 2 * self.share, 2 * self.share)]
            target = kept.at[span_of(self.place["got_far"] + (r - 1) * 2 * self.share, 2 * self.share)]
            return remote(self.number, 3 + r, source, target, far_peers[r])

        def cross_copy(self):
            source = kept.at[span_of(self.mine + (1 - high) * self.share, self.share)]
            target = kept.at[span_of(self.place["got_cross"], self.share)]
            return remote(self.number, 2, source, target, cross_peer)

        def place_of(self, near_, far_):
            start = z.job_at[self.kind] + (near_ * z.far + far_) * self.share
            return self.sums.at[span_of(start, self.share)]

        def share_copy(self, r):
            source = kept.at[span_of(self.place["final"], self.share)]
            return remote(self.number, 3 + z.far + r, source, self.place_of(near, far), far_peers[r])

        def rest_copy(self, r):
            source = kept.at[span_of(self.mine + high * self.share, self.share)]
            target = kept.at[span_of(self.place["got_rest"] + (r - 1) * self.share, self.share)]
            return remote(self.number, 3 + 2 * z.far + r, source, target, rest_peers[r])

        def own_copy(self):
            source = kept.at[span_of(self.place["final"], self.share)]
            return pltpu.make_async_copy(source, self.place_of(near, far), own_sem.at[4, self.number])

        def back_copy(self):
            start = z.job_at[self.kind] + near * z.far * self.share
            block = self.sums.at[span_of(start, z.far * self.share)]
            return remote(self.number, 3, block, block, near_peer)

        def add(self, start, count, *others):
            for at in range(0, count, 8 * TILE):
                size = min(8 * TILE, count - at)
                total = kept[span_of(start + at, size), :].astype(F32)
                for other in others:
                    total += kept[span_of(other + at, size), :].astype(F32)
                yield at, size, total.astype(BF16)

        def step(self, number):
            if number == 0:
                self.pair_copy().start()
            elif number == 1:
                self.pair_copy().wait_recv()
                for half in (1 - near, near):
                    start = half * self.rows
                    for at, size, total in self.add(
                        self.own + start, self.rows, self.place["got_pair"] + start
                    ):
                        kept[span_of(self.own + start + at, size), :] = total
                    if half is not near:
                        self.near_copy().start()
            elif number == 2:
                self.near_copy().wait_recv()
                for at, size, total in self.add(self.half, self.rows, self.place["got_near"]):
                    kept[span_of(self.half + at, size), :] = total
                for r in range(1, z.far):
                    self.far_copy(r).start()
            elif number == 3:
                for r in range(1, z.far):
                    self.far_copy(r).wait_recv()
                others = [self.place["got_far"] + (r - 1) * 2 * self.share for r in range(1, z.far)]
                for at, size, total in self.add(self.mine, 2 * self.share, *others):
                    kept[span_of(self.mine + at, size), :] = total
                self.cross_copy().start()
            elif number == 4:
                self.cross_copy().wait_recv()
                start = self.mine + high * self.share
                for at, size, total in self.add(start, self.share, self.place["got_cross"]):
                    kept[span_of(start + at, size), :] = total
                for r in range(1, z.rest):
                    self.rest_copy(r).start()
                for r in range(1, z.rest):
                    self.rest_copy(r).wait_recv()
                others = [self.place["got_rest"] + r * self.share for r in range(z.rest - 1)]
                for at, size, total in self.add(start, self.share, *others):
                    kept[span_of(self.place["final"] + at, size), :] = total
                self.own_copy().start()
                for r in range(1, z.far):
                    self.share_copy(r).start()
            elif number == 5:
                self.own_copy().wait()
                for r in range(1, z.far):
                    self.share_copy(r).wait_recv()
                self.back_copy().start()
            else:
                self.back_copy().wait()
                self.pair_copy().wait_send()
                self.near_copy().wait_send()
                self.cross_copy().wait_send()
                for r in range(1, z.far):
                    self.far_copy(r).wait_send()
                    self.share_copy(r).wait_send()
                for r in range(1, z.rest):
                    self.rest_copy(r).wait_send()

    def chunk_lanes(ref, chunk_):
        return slice(chunk_ * channels, (chunk_ + 1) * channels)

    def down_tile(chunk_, t):
        if t * TILE >= channels:
            return None
        return dd_ref[t * TILE : (t + 1) * TILE, chunk_lanes(dd_ref, chunk_)]

    def up_tile(l, first):
        def tile_of(chunk_, t):
            at = t * TILE + first
            if first == 0 and at >= z.split:
                return None
            if at < channels:
                return du_ref[at : at + TILE, chunk_lanes(du_ref, chunk_)]
            at -= channels
            if at < z.main:
                return dm_ref[l, chunk_ * z.main + at : chunk_ * z.main + at + TILE, :]
            if at == z.main:
                return dm_ref[l, z.image : z.image + TILE, :]
            if at == z.main + TILE:
                bias = dub_ref[l, :, chunk_lanes(dub_ref, chunk_)]
                rows = [dv_ref[l, 0:7, :], bias, jnp.zeros((TILE - 8, channels), F32)]
                return jnp.concatenate(rows, axis=0)
            return None

        return tile_of

    def down_sums(l):
        total = None
        for h in range(0, hidden, 2 * 128):
            span = slice(h, h + 2 * 128)
            term = dd_ref[:, span].T * down_w[l, span, :].astype(F32)
            total = term if total is None else total + term
        total = jnp.sum(total, axis=0, keepdims=True) + vector(downb_ref, l) * dv_ref[l, 5:6, :]
        dv_ref[l, 6:7, :] = total / vector(pscale_ref, l)

    def mix_sums(l):
        total = vector(mgain_ref, l) * dv_ref[l, 0:1, :] + vector(mshift_ref, l) * dv_ref[l, 1:2, :]
        dv_ref[l, 2:3, :] = (total + dv_ref[l, 2:3, :]) / vector(mscale_ref, l)

    jobs = {(l, kind): Job(l, kind) for l in range(z.layers) for kind in range(3)}
    top = z.layers - 1

    def clear(*refs):
        for ref in refs:
            ref[...] = jnp.zeros(ref.shape, F32)

    def greet(number):
        for peer in job_peers:
            pl.semaphore_signal(free_sem.at[number], inc=1, device_id=peer, device_id_type=MESH)

    def met(number):
        pl.semaphore_wait(free_sem.at[number], len(job_peers))

    def run(text):
        for entry in text.split():
            l, kind, number = int(entry[0]), "dab".index(entry[1]), int(entry[2])
            jobs[l, kind].step(number)

    thirds = [groups * k // 3 for k in range(4)]

    def backward(l, plan):
        def down(g, carry):
            if l == top:
                arrive(exchange(1, g, send_dy, dys))
                start(exchange_back(2, g, send_x, out_w))
            mlp_backward_down(l, g)
            return carry

        def up(g, carry):
            mlp_backward_up(l, g)
            mix_backward(l, g, dys)
            if l == 0:
                start(exchange_back(3, g, dys, dx_w))
            return carry

        clear(du_ref, dd_ref)
        lax.fori_loop(0, groups, down, 0)
        if l == top:
            greet(0)
            start(exchange_left(2, out_left, out_e))
        run(plan[0])
        down_sums(l)
        jobs[l, 0].fill(down_tile)
        met(top - l)
        jobs[l, 0].step(0)
        for k in range(3):
            lax.fori_loop(thirds[k], thirds[k + 1], up, 0)
            if k < 2:
                run(plan[k + 1])
        if l == top:
            greet(1)
        if l == 0:
            sent(exchange_left(0, sende_x, got_x))
            gather_left(dys, sende_x)
            start(exchange_left(3, sende_x, dx_e))
        mix_sums(l)
        jobs[l, 1].fill(up_tile(l, 0))
        jobs[l, 1].step(0)
        jobs[l, 2].fill(up_tile(l, z.split))
        jobs[l, 2].step(0)
        run(plan[3])

    backward(1, ("", "1d1", "1d2", "1d3"))
    backward(0, ("1a1 1b1 1d4", "0d1 1a2 1b2 1d5", "0d2 1a3 1b3", "1a4 1b4 0d3 0a1 0b1 0d4 0a2 0b2 1a5 1b5 0a3 0b3 0d5 0a4 0b4 0a5 0b5"))
    run("1d6 1a6 1b6 0d6 0a6 0b6")

    for g in range(groups):
        sent(exchange(1, g, send_dy, dys))
    sent(exchange_left(1, sende_dy, got_dy))
    for copies in [exchange_left(2, out_left, out_e), exchange_left(3, sende_x, dx_e)]:
        arrive(copies)
        sent(copies)
    for g in range(groups):
        for copies in [exchange_back(2, g, send_x, out_w), exchange_back(3, g, dys, dx_w)]:
            arrive(copies)
            sent(copies)


def finish_kernel(
    z, mask_ref, out_w, out_e, dx_w, dx_e, sums,
    out_ref, dx_ref, gain_ref, shift_ref, scale_ref, mixw_ref, mixb_ref, pgain_ref, pshift_ref, pscale_ref,
    up_ref, upb_ref, down_ref, downb_ref,
):
    g = pl.program_id(0)
    swap = swap_matrix()
    pick = iota((1, GROUP * TILE), 1) >> 4
    masked = (swap * mask_lanes(mask_ref, g * GROUP, GROUP, pick)).astype(BF16)
    left_all = z.parts * z.left
    row, lane = iota((GROUP, left_all), 0), iota((GROUP, left_all), 1)
    want = row + g * z.mine
    for d in range(1, z.parts):
        want = want + jnp.where(row >= d * z.mine, z.left - z.mine, 0)
    last = jnp.where(want == lane, 1.0, 0.0)
    lanes = jnp.zeros((GROUP, 1), F32)
    for k in range(GROUP):
        lanes = jnp.where(iota((GROUP, 1), 0) == k, mask_ref[g * GROUP + k].astype(F32), lanes)
    for wire, left, target, matrix, tail in (
        (out_w, out_e, out_ref, masked, (last * lanes).astype(BF16)),
        (dx_w, dx_e, dx_ref, swap.astype(BF16), last.astype(BF16)),
    ):
        for t in range(z.main // TILE):
            block = jnp.concatenate(
                [
                    wire[0, i * z.main + t * TILE : i * z.main + (t + 1) * TILE, :]
                    for i in range(GROUP)
                ],
                axis=0,
            )
            rows = dot(matrix, block).reshape(TILE, GROUP, z.channels)
            target[t * TILE : (t + 1) * TILE] = rows.astype(target.dtype)
        rows = dot(tail, left[...].reshape(left_all, z.channels))
        target[z.patches - 1] = rows.astype(target.dtype)


    @pl.when(g == 0)
    def _():
        me = lax.axis_index("mix")
        channels, share = z.channels, z.channels // z.parts
        row, lane = iota((z.pad, z.whole), 0), iota((z.pad, z.whole), 1)
        want = row
        for m in range(1, z.parts):
            want = want + jnp.where(row >= m * z.main, 1, 0)
        for m in range(z.parts):
            base = z.image + m * z.mine
            inside = (row >= base) & (row < base + z.mine)
            want = jnp.where(inside, m * z.patches + z.patches - 1, want)
        want = jnp.where(row < z.mix_rows, want, -1)
        order = jnp.where(want == lane, 1.0, 0.0).astype(BF16)
        lanes_in, lanes_out = iota((channels, share), 0), iota((channels, share), 1)
        own = jnp.where(lanes_in == lanes_out + me * share, 1.0, 0.0).astype(BF16)
        size = z.main + TILE
        at = iota((size, 1), 0) - z.main - me * z.mine
        edge = jnp.where((at >= 0) & (at < z.mine), 1.0, 0.0)
        fold_row, fold_lane = iota((size, z.patches), 0), iota((size, z.patches), 1)
        fold_at = fold_row - z.main - me * z.mine
        fold_to = jnp.where(
            fold_row < z.main, fold_row, jnp.where((fold_at >= 0) & (fold_at < z.mine), z.main, -1)
        )
        fold = jnp.where(fold_to == fold_lane, 1.0, 0.0).astype(BF16)
        spot = jnp.where((iota((8, z.pad), 0) == 0) & (iota((8, z.pad), 1) == z.ones), 1.0, 0.0)
        for l in range(z.layers):
            down_ref[l] = sums[l, :channels, :].astype(F32).T
            up_ref[l, : z.split, :] = sums[l, z.job_at[1] : z.job_at[1] + z.split, :].astype(F32)
            start = z.job_at[2] + channels - z.split
            up_ref[l, z.split :, :] = sums[l, z.job_at[2] : start, :].astype(F32)
            rows = sums[l, start : start + size, : z.pad]
            weight = dot(rows, order)
            mixw_ref[: z.main, l, :] = weight[: z.main]
            mixw_ref[z.main, l : l + 1, :] = jnp.sum(weight * edge, axis=0, keepdims=True)
            bias = dot_nt(spot.astype(BF16), rows).astype(BF16)
            mixb_ref[l : l + 1, :] = dot(bias, fold)[:1]
            tile = sums[l, start + size : start + size + TILE, :]
            vectors = dot(tile, own)
            for k, ref in enumerate(
                (gain_ref, shift_ref, scale_ref, pgain_ref, pshift_ref, downb_ref, pscale_ref)
            ):
                ref[l : l + 1, :] = vectors[k : k + 1]
            upb_ref[l : l + 1, :] = tile[7:8, :].astype(F32)


def local(parts, copies, images_in, out_grad, slot_mask, mix_gain, mix_shift, mix_scale, mix_weight, mix_bias,
          mlp_gain, mlp_shift, mlp_scale, up_weight, up_bias, down_weight, down_bias):
    slots, patches, channels = images_in.shape
    layers, _, hidden = up_weight.shape
    z = Sizes(parts, copies, slots, patches, channels, hidden, layers)
    vmem = pl.BlockSpec(memory_space=pltpu.VMEM)
    smem = pl.BlockSpec(memory_space=pltpu.SMEM)
    hbm = pl.BlockSpec(memory_space=pl.ANY)
    wire = jax.ShapeDtypeStruct((z.groups, parts, z.block, channels), BF16)
    left = jax.ShapeDtypeStruct((parts, z.left, channels), BF16)
    dma = pltpu.SemaphoreType.DMA
    rows = (z.groups, z.rows, channels)
    out_w, out_e, dx_w, dx_e, sums = pl.pallas_call(
        functools.partial(whole_kernel, z),
        out_shape=(
            wire, left, wire, left,
            jax.ShapeDtypeStruct((layers, sum(z.job_rows), channels), BF16),
        ),
        in_specs=[hbm, hbm, smem] + [vmem] * 10 + [hbm, hbm],
        out_specs=(hbm,) * 5,
        scratch_shapes=[
            pltpu.VMEM((channels, hidden), F32),
            pltpu.VMEM((channels, hidden), F32),
            pltpu.VMEM((layers, z.pad, z.pad), F32),
            pltpu.VMEM((layers, 8, channels), F32),
            pltpu.VMEM((layers, 1, hidden), F32),
            pltpu.VMEM((z.groups, patches, GROUP, channels), BF16),
            pltpu.VMEM((z.groups, parts, z.block, channels), BF16),
            pltpu.VMEM((z.groups, parts, z.block, channels), BF16),
            pltpu.VMEM((parts, z.left, channels), BF16),
            pltpu.VMEM((parts, z.left, channels), BF16),
            pltpu.VMEM((parts, z.left, channels), BF16),
            pltpu.VMEM((parts, z.left, channels), BF16),
            pltpu.VMEM((layers, *rows), BF16),
            pltpu.VMEM((layers, *rows), BF16),
            pltpu.VMEM(rows, BF16),
            pltpu.VMEM((z.groups, parts * z.mine, channels), BF16),
            pltpu.VMEM((parts, z.left, channels), BF16),
            pltpu.VMEM((z.kept_rows, channels), BF16),
            pltpu.VMEM((layers, channels, hidden), BF16),
            pltpu.VMEM((layers, hidden, channels), BF16),
            pltpu.VMEM((layers, z.pad, z.pad), BF16),
            pltpu.VMEM((layers, z.pad, z.pad), BF16),
            dma((2 * z.groups + 2,)),
            dma((5, max(z.groups, 3 * layers))),
            dma((4, z.groups, parts)),
            dma((4, z.groups, parts)),
            dma((4, parts)),
            dma((4, parts)),
            dma((3 * layers, 3 + 2 * z.far + z.rest)),
            dma((3 * layers, 3 + 2 * z.far + z.rest)),
            pltpu.SemaphoreType.REGULAR((2,)),
        ],
        compiler_params=pltpu.CompilerParams(
            collective_id=0, has_side_effects=True, vmem_limit_bytes=64 << 20
        ),
        name="layers",
    )(
        jnp.transpose(images_in, (1, 0, 2)),
        jnp.transpose(out_grad, (1, 0, 2)),
        slot_mask,
        jnp.transpose(mix_weight, (1, 0, 2)),
        mix_bias, mix_gain, mix_shift, mix_scale, mlp_gain, mlp_shift, mlp_scale, down_bias, up_bias,
        up_weight, down_weight,
    )

    flat = (z.groups, parts * z.block, channels)
    block = pl.BlockSpec((1, *flat[1:]), lambda g: (g, 0, 0))
    whole = pl.BlockSpec(left.shape, lambda g: (0, 0, 0))
    turned = pl.BlockSpec((patches, GROUP, channels), lambda g: (0, g, 0))
    share = channels // parts
    small = jax.ShapeDtypeStruct((layers, share), F32)
    small_block = pl.BlockSpec(small.shape, lambda g: (0, 0))
    shapes = [
        jax.ShapeDtypeStruct((patches, slots, channels), BF16),
        jax.ShapeDtypeStruct((patches, slots, channels), F32),
        small, small, small,
        jax.ShapeDtypeStruct((patches, layers, z.whole), F32),
        jax.ShapeDtypeStruct((layers, patches), F32),
        small, small, small,
        jax.ShapeDtypeStruct((layers, channels, hidden // parts), F32),
        jax.ShapeDtypeStruct((layers, hidden // parts), F32),
        jax.ShapeDtypeStruct((layers, hidden // parts, channels), F32),
        small,
    ]

    def fixed(shape):
        return pl.BlockSpec(shape, lambda g: (0,) * len(shape))

    results = list(
        pl.pallas_call(
            functools.partial(finish_kernel, z),
            grid=(z.groups,),
            out_shape=shapes,
            in_specs=[smem, block, whole, block, whole, fixed(sums.shape)],
            out_specs=[turned, turned] + [fixed(shape.shape) for shape in shapes[2:]],
            compiler_params=pltpu.CompilerParams(vmem_limit_bytes=64 << 20),
            name="finish",
        )(slot_mask, out_w.reshape(flat), out_e, dx_w.reshape(flat), dx_e, sums)
    )
    for k in (0, 1, 5):
        results[k] = jnp.transpose(results[k], (1, 0, 2))
    return tuple(results)


def solution(mesh):
    in_specs = (P("dp", "mix", None), P("dp", "mix", None), P("dp")) + (P(),) * 12
    out_specs = (
        P("dp", "mix", None),
        P("dp", "mix", None),
        P(None, "mix"),
        P(None, "mix"),
        P(None, "mix"),
        P(None, "mix", None),
        P(None, "mix"),
        P(None, "mix"),
        P(None, "mix"),
        P(None, "mix"),
        P(None, None, "mix"),
        P(None, "mix"),
        P(None, "mix", None),
        P(None, "mix"),
    )
    return jax.shard_map(
        functools.partial(local, mesh.shape["mix"], mesh.shape["dp"]),
        mesh=mesh,
        in_specs=in_specs,
        out_specs=out_specs,
        check_vma=False,
    )
```

```python
import functools
import math

import jax
import jax.numpy as jnp
from jax import lax
from jax.experimental import pallas as pl
from jax.experimental.pallas import tpu as pltpu
from jax.sharding import PartitionSpec as P

MESH = pl.DeviceIdType.MESH
F32 = jnp.float32
BF16 = jnp.bfloat16
GROUP = 16
TILE = 16
TANH_A = math.sqrt(2.0 / math.pi)
TANH_B = TANH_A * 0.044715


def dot(a, b):
    return jnp.dot(a, b, preferred_element_type=F32)


def dot_nt(a, b):
    return lax.dot_general(a, b, (((1,), (1,)), ((), ())), preferred_element_type=F32)


def iota(shape, axis):
    return lax.broadcasted_iota(jnp.int32, shape, axis)


def gelu_pair(value):
    square = value * value
    gate = 0.5 * jnp.tanh(value * (TANH_A + TANH_B * square)) + 0.5
    active = value * gate
    return active, gate + (active - active * gate) * (2.0 * TANH_A + (6.0 * TANH_B) * square)


def mask_lanes(mask_ref, first, count, pick):
    total = jnp.zeros(pick.shape, F32)
    for k in range(count):
        total = jnp.where(pick == k, mask_ref[first + k].astype(F32), total)
    return total


def swap_matrix():
    side = GROUP * TILE
    row, lane = iota((side, side), 0), iota((side, side), 1)
    return jnp.where((row >> 4) + ((row & 15) << 4) == lane, 1.0, 0.0)


class Sizes:
    def __init__(self, parts, copies, slots, patches, channels, hidden, layers):
        self.parts = parts
        self.slots = slots
        self.patches = patches
        self.channels = channels
        self.hidden = hidden
        self.layers = layers
        self.groups = slots // GROUP
        self.mine = GROUP // parts
        self.main = patches // TILE * TILE
        self.block = self.mine * self.main
        self.body = parts * self.block
        self.rows = self.body + parts * self.mine
        self.image = parts * self.main
        self.mix_rows = self.image + parts * self.mine
        self.ones = self.mix_rows
        self.mix_cols = self.mix_rows + TILE
        self.pad = -(-self.mix_cols // 128) * 128
        self.left = -(-self.groups * self.mine // TILE) * TILE
        self.whole = parts * patches
        self.quarters = hidden // channels
        self.far = min(copies // 2, 4)
        self.rest = copies // (2 * self.far)
        cuts = 2 * self.far
        step = TILE * cuts
        self.split = channels * 2 // 3 // TILE * TILE
        counts = (channels, self.split, channels - self.split + self.main + 2 * TILE)
        self.job_rows = [-(-count // step) * step for count in counts]
        self.job_at = [sum(self.job_rows[:kind]) for kind in range(3)]
        self.shares = [count // cuts for count in self.job_rows]
        act_rows = self.quarters * self.rows * self.groups
        self.places = []
        for layer in range(layers):
            at = (2 * (layers - 1) + layers - 1 - layer) * act_rows
            for kind in range(3):
                count, share = self.job_rows[kind], self.shares[kind]
                place = {}
                for name, size in (
                    ("pay", 4 * count),
                    ("got_pair", 2 * count),
                    ("got_near", count),
                    ("got_far", (self.far - 1) * 2 * share),
                    ("got_cross", share),
                    ("got_rest", (self.rest - 1) * share),
                    ("final", share),
                ):
                    place[name] = at
                    at += size
                self.places.append(place)
        self.kept_rows = max(at, 2 * layers * act_rows)


def whole_kernel(
    z,
    x_hbm, dy_hbm, mask_ref, mixw_ref, mixb_ref,
    mgain_ref, mshift_ref, mscale_ref, pgain_ref, pshift_ref, pscale_ref, downb_ref, upb_ref,
    up_hbm, down_hbm,
    out_w, out_e, dx_w, dx_e, sums_hbm,
    du_ref, dd_ref, dm_ref, dv_ref, dub_ref, stage, send_x, send_dy, sende_x, sende_dy, got_x, got_dy,
    xs, firsts, dys, outs_left, out_left, tails, kept, up_w, down_w, mix_m, mix_t,
    load_sem, own_sem, send_sem, recv_sem, lsend_sem, lrecv_sem, job_send, job_recv, free_sem,
):
    dp, me = lax.axis_index("dp"), lax.axis_index("mix")
    parts, groups, channels, hidden = z.parts, z.groups, z.channels, z.hidden
    peers = [lax.rem(me + r, parts) for r in range(parts)]

    loads = []
    for k, hbm in enumerate((x_hbm, dy_hbm)):
        for g in range(groups):
            loads.append(
                pltpu.make_async_copy(
                    hbm.at[:, pl.ds(g * GROUP, GROUP), :], stage.at[g], load_sem.at[k * groups + g]
                )
            )
    w_loads = [
        pltpu.make_async_copy(up_hbm, up_w, load_sem.at[2 * groups]),
        pltpu.make_async_copy(down_hbm, down_w, load_sem.at[2 * groups + 1]),
    ]
    for copy in loads[:groups] + w_loads:
        copy.start()

    barrier = pltpu.get_barrier_semaphore()
    near, upper_place = lax.rem(dp, 2), lax.div(dp, 2)
    far, rest = lax.rem(upper_place, z.far), lax.div(upper_place, z.far)
    row_peers = [(dp, peers[r]) for r in range(1, parts)]
    near_peer = (dp + 1 - 2 * near, me)
    far_places = [lax.rem(far + r, z.far) for r in range(z.far)]
    far_peers = [((rest * z.far + far_places[r]) * 2 + near, me) for r in range(z.far)]
    rest_peers = [
        ((lax.rem(rest + r, z.rest) * z.far + far) * 2 + near, me) for r in range(z.rest)
    ]
    job_peers = row_peers + [near_peer] + far_peers[1:] + rest_peers[1:]
    for peer in job_peers:
        pl.semaphore_signal(barrier, inc=1, device_id=peer, device_id_type=MESH)

    swap = swap_matrix()
    swap_b = swap.astype(BF16)
    left_all = parts * z.left

    def convert(send, g, matrix):
        for t in range(z.main // TILE):
            block = stage[g, t * TILE : (t + 1) * TILE].reshape(TILE * GROUP, channels)
            rows = dot(matrix, block).astype(BF16).reshape(GROUP, TILE, channels)
            for d in range(parts):
                for j in range(z.mine):
                    send[g, d, j * z.main + t * TILE : j * z.main + (t + 1) * TILE, :] = rows[
                        d * z.mine + j
                    ]

    def convert_left(send, lanes):
        row, lane = iota((left_all, z.slots), 0), iota((left_all, z.slots), 1)
        want = jnp.full(row.shape, -1, jnp.int32)
        for d in range(parts):
            for g in range(groups):
                base = d * z.left + g * z.mine
                inside = (row >= base) & (row < base + z.mine)
                want = jnp.where(inside, row - base + g * GROUP + d * z.mine, want)
        matrix = jnp.where(want == lane, 1.0, 0.0)
        if lanes is not None:
            matrix = matrix * lanes
        last = jnp.concatenate([stage[g, z.patches - 1] for g in range(groups)], axis=0)
        send[...] = dot(matrix.astype(BF16), last).astype(BF16).reshape(parts, z.left, channels)

    def exchange(k, g, send, target):
        copies = [lambda: pltpu.make_async_copy(send.at[g, me], target.at[g, pl.ds(me * z.block, z.block)], own_sem.at[k, g])]
        for r in range(1, parts):
            copies.append(
                pltpu.make_async_remote_copy(
                    src_ref=send.at[g, peers[r]],
                    dst_ref=target.at[g, pl.ds(me * z.block, z.block)],
                    send_sem=send_sem.at[k, g, r],
                    recv_sem=recv_sem.at[k, g, r],
                    device_id=(dp, peers[r]),
                    device_id_type=MESH,
                )
            )
        return copies

    def part_of(source, g, d):
        if len(source.shape) == 4:
            return source.at[g, d]
        return source.at[g, pl.ds(d * z.block, z.block)]

    def exchange_back(k, g, source, target):
        copies = [lambda: pltpu.make_async_copy(part_of(source, g, me), target.at[g, me], own_sem.at[k, g])]
        for r in range(1, parts):
            copies.append(
                pltpu.make_async_remote_copy(
                    src_ref=part_of(source, g, peers[r]),
                    dst_ref=target.at[g, me],
                    send_sem=send_sem.at[k, g, r],
                    recv_sem=recv_sem.at[k, g, r],
                    device_id=(dp, peers[r]),
                    device_id_type=MESH,
                )
            )
        return copies

    def exchange_left(k, send, target):
        copies = [lambda: pltpu.make_async_copy(send.at[me], target.at[me], lsend_sem.at[k, 0])]
        for r in range(1, parts):
            copies.append(
                pltpu.make_async_remote_copy(
                    src_ref=send.at[peers[r]],
                    dst_ref=target.at[me],
                    send_sem=lsend_sem.at[k, r],
                    recv_sem=lrecv_sem.at[k, r],
                    device_id=(dp, peers[r]),
                    device_id_type=MESH,
                )
            )
        return copies

    def start(copies):
        copies[0]().start()
        for copy in copies[1:]:
            copy.start()

    def arrive(copies):
        copies[0]().wait()
        for copy in copies[1:]:
            copy.wait_recv()

    def sent(copies):
        for copy in copies[1:]:
            copy.wait_send()

    for g in range(groups):
        if g == 0:
            loads[g].wait()
        convert(send_x, g, swap_b)
        if g == 0:
            pl.semaphore_wait(barrier, len(job_peers))
        start(exchange(0, g, send_x, xs.at[0]))
        if g == 0:
            for copy in loads[1:groups]:
                copy.wait()
            convert_left(sende_x, None)
            start(exchange_left(0, sende_x, got_x))
    for copy in loads[groups:]:
        copy.start()
    for g in range(groups):
        loads[groups + g].wait()
        pick = iota((1, GROUP * TILE), 1) & 15
        lanes = mask_lanes(mask_ref, g * GROUP, GROUP, pick)
        convert(send_dy, g, (swap * lanes).astype(BF16))
        start(exchange(1, g, send_dy, dys))
    convert_left(sende_dy, mask_lanes(mask_ref, 0, z.slots, iota((1, z.slots), 1)))
    start(exchange_left(1, sende_dy, got_dy))

    size = (z.pad, z.whole)
    row, lane = iota(size, 0), iota(size, 1)
    want = row
    for m in range(1, parts):
        want = want + jnp.where(row >= m * z.main, 1, 0)
    for m in range(parts):
        base = z.image + m * z.mine
        inside = (row >= base) & (row < base + z.mine)
        want = jnp.where(inside, m * z.patches + z.patches - 1, want)
    want = jnp.where(row < z.mix_rows, want, -1)
    pick = jnp.where(want == lane, 1.0, 0.0).astype(BF16)
    spot = jnp.where((iota((z.pad, TILE), 0) == z.ones) & (iota((z.pad, TILE), 1) == 0), 1.0, 0.0)
    for l in range(z.layers):
        half = dot(pick, mixw_ref[:, l, :]).astype(BF16)
        offset = jnp.where(iota((TILE, z.whole), 0) == 0, mixb_ref[l : l + 1, :].astype(F32), 0.0)
        column = dot_nt(pick, offset.astype(BF16)).astype(BF16)
        full = dot_nt(half, pick) + dot_nt(column, spot.astype(BF16))
        mix_m[l] = full.astype(BF16)
        mix_t[l] = full.T.astype(BF16)

    for ref in (dm_ref, dv_ref, dub_ref):
        ref[...] = jnp.zeros(ref.shape, F32)

    def spread_left(got, target):
        tile = parts * z.mine
        row, lane = iota((groups * tile, left_all), 0), iota((groups * tile, left_all), 1)
        want = jnp.full(row.shape, -1, jnp.int32)
        for g in range(groups):
            for m in range(parts):
                base = g * tile + m * z.mine
                inside = (row >= base) & (row < base + z.mine)
                want = jnp.where(inside, row - base + m * z.left + g * z.mine, want)
        matrix = jnp.where(want == lane, 1.0, 0.0).astype(BF16)
        rows = dot(matrix, got[...].reshape(left_all, channels)).astype(BF16)
        for g in range(groups):
            target[g, z.body :, :] = rows[g * tile : (g + 1) * tile]

    def gather_left(source, target):
        tile = parts * z.mine
        row, lane = iota((left_all, groups * tile), 0), iota((left_all, groups * tile), 1)
        want = jnp.full(row.shape, -1, jnp.int32)
        for g in range(groups):
            for m in range(parts):
                base = m * z.left + g * z.mine
                inside = (row >= base) & (row < base + z.mine)
                want = jnp.where(inside, row - base + g * tile + m * z.mine, want)
        matrix = jnp.where(want == lane, 1.0, 0.0).astype(BF16)
        low = 0 if source.shape[1] == tile else z.body
        rows = jnp.concatenate([source[g, low:, :] for g in range(groups)], axis=0)
        target[...] = dot(matrix, rows).astype(BF16).reshape(parts, z.left, channels)

    def vector(ref, l):
        return ref[l : l + 1, :].astype(F32)

    tile_rows = parts * z.mine
    image_of = iota((tile_rows, 1), 0) & (z.mine - 1)
    ones_tile = jnp.where(iota((TILE, channels), 0) == 0, 1.0, 0.0).astype(BF16)

    def image_rows(ref, l, g, j):
        index = (g,) if l is None else (l, g)
        return [
            ref[(*index, pl.ds(m * z.block + j * z.main, z.main), slice(None))] for m in range(parts)
        ]

    def mixed_rows(l, g, j, left):
        gain, shift = vector(mgain_ref, l), vector(mshift_ref, l)
        pieces = [
            (gain * part.astype(F32) + shift).astype(BF16) for part in image_rows(xs, l, g, j)
        ]
        pieces.append(jnp.where(image_of == j, gain * left + shift, 0.0).astype(BF16))
        pieces.append(ones_tile)
        return jnp.concatenate(pieces, axis=0)

    def mix_forward(l, g):
        scale = vector(mscale_ref, l)
        left = xs[l, g, z.body :, :].astype(F32)
        left_total = jnp.zeros((tile_rows, channels), F32)
        for j in range(z.mine):
            mixed = mixed_rows(l, g, j, left)
            across = dot(mix_m[l, : z.mix_rows, : z.mix_cols], mixed)
            for m, part in enumerate(image_rows(xs, l, g, j)):
                rows = part.astype(F32) + scale * across[m * z.main : (m + 1) * z.main]
                firsts[l, g, pl.ds(m * z.block + j * z.main, z.main), :] = rows.astype(BF16)
            left_total = jnp.where(image_of == j, across[z.image :], left_total)
        firsts[l, g, z.body :, :] = (left + scale * left_total).astype(BF16)

    chunk = 256 if hidden % 256 == 0 else 128
    back_chunk = 512 if hidden % 512 == 0 else 128

    def kept_at(l, which, g, quarter):
        index = (l * 2 + which) * groups + g
        start = (index * z.quarters + quarter) * z.rows
        return start if isinstance(start, int) else pl.multiple_of(start, TILE)

    def pieces_of(h, chunk):
        pieces, at = [], h
        while at < h + chunk:
            quarter, lane = divmod(at, channels)
            end = min(channels, lane + h + chunk - at)
            pieces.append((quarter, lane, end))
            at += end - lane
        return pieces

    def keep_rows(l, which, g, h, value, chunk, first):
        value, at = value.astype(BF16), 0
        for quarter, lane, end in pieces_of(h, chunk):
            place = pl.ds(kept_at(l, which, g, quarter) + first, value.shape[0])
            kept[place, lane:end] = value[:, at : at + end - lane]
            at += end - lane

    def kept_rows(l, which, g, h, chunk, first, count):
        parts_ = [
            kept[pl.ds(kept_at(l, which, g, quarter) + first, count), lane:end]
            for quarter, lane, end in pieces_of(h, chunk)
        ]
        return jnp.concatenate(parts_, axis=1)

    def mlp_normed(l, g, span=slice(None)):
        rows = firsts[l, g, span, :].astype(F32)
        return rows, (vector(pgain_ref, l) * rows + vector(pshift_ref, l)).astype(BF16)

    piece = z.rows // 4 // TILE * TILE
    spans = [slice(k * piece, (k + 1) * piece if k < 3 else z.rows) for k in range(4)]

    def mlp_forward(l, g, target):
        bias = upb_ref[l : l + 1, :].astype(F32)
        normed = [mlp_normed(l, g, span)[1] for span in spans]
        steps = [(h, k) for h in range(0, hidden, chunk) for k in range(len(spans))]

        def rise(step):
            h, k = step
            return dot(normed[k], up_w[l, :, h : h + chunk]) + bias[:, h : h + chunk]

        totals, coming = [None] * len(spans), rise(steps[0])
        for at, (h, k) in enumerate(steps):
            value = coming
            if at + 1 < len(steps):
                coming = rise(steps[at + 1])
            active, grade = gelu_pair(value)
            active = active.astype(BF16)
            keep_rows(l, 0, g, h, active, chunk, spans[k].start)
            keep_rows(l, 1, g, h, grade, chunk, spans[k].start)
            term = dot(active, down_w[l, h : h + chunk, :])
            totals[k] = term if totals[k] is None else totals[k] + term
        for span, total in zip(spans, totals):
            result = firsts[l, g, span, :].astype(F32)
            result = result + vector(pscale_ref, l) * (total + vector(downb_ref, l))
            result = result.astype(BF16)
            if target is not None:
                target[g, span, :] = result
                continue
            for d in range(parts):
                low, high = max(span.start, d * z.block), min(span.stop, (d + 1) * z.block)
                if low < high:
                    send_x[g, d, low - d * z.block : high - d * z.block, :] = result[
                        low - span.start : high - span.start
                    ]
            if span.stop == z.rows:
                outs_left[g] = result[z.body - span.start :]

    def mlp_backward_down(l, g):
        branch = (vector(pscale_ref, l) * dys[g, : z.body, :].astype(F32)).astype(BF16)
        dv_ref[l, 5:6, :] += jnp.sum(branch.astype(F32), axis=0, keepdims=True)
        branch_t = branch.T
        for h in range(0, hidden, back_chunk):
            span = slice(h, h + back_chunk)
            dd_ref[:, span] += dot(branch_t, kept_rows(l, 0, g, h, back_chunk, 0, z.body))

    def left_rows(ref):
        return jnp.concatenate([ref[g, z.body :, :] for g in range(groups)], axis=0).astype(F32)

    def mlp_backward_down_left(l):
        branch = (vector(pscale_ref, l) * left_rows(dys)).astype(BF16)
        dv_ref[l, 5:6, :] += jnp.sum(branch.astype(F32), axis=0, keepdims=True)
        branch_t = branch.T
        for h in range(0, hidden, back_chunk):
            span = slice(h, h + back_chunk)
            rows = [
                kept_rows(l, 0, g, h, back_chunk, z.body, z.rows - z.body) for g in range(groups)
            ]
            dd_ref[:, span] += dot(branch_t, jnp.concatenate(rows, axis=0))

    def mlp_backward_up_left(l):
        rows = left_rows(firsts.at[l])
        normed = (vector(pgain_ref, l) * rows + vector(pshift_ref, l)).astype(BF16)
        normed_t = normed.T
        for h in range(0, hidden, back_chunk):
            span = slice(h, h + back_chunk)
            grads = jnp.concatenate([tails[g, :, span] for g in range(groups)], axis=0)
            du_ref[:, span] += dot(normed_t, grads)

    def mlp_backward_up(l, g):
        rows, normed = mlp_normed(l, g)
        upper = dys[g].astype(F32)
        branch = (vector(pscale_ref, l) * upper).astype(BF16)
        normed_t = normed[: z.body].T
        total = None
        for h in range(0, hidden, back_chunk):
            span = slice(h, h + back_chunk)
            back = dot_nt(branch, down_w[l, span, :])
            grad = (back * kept_rows(l, 1, g, h, back_chunk, 0, z.rows).astype(F32)).astype(BF16)
            dub_ref[l, :, span] += jnp.sum(grad.astype(F32), axis=0, keepdims=True)
            tails[g, :, span] = grad[z.body :]
            du_ref[:, span] += dot(normed_t, grad[: z.body])
            term = dot_nt(grad, up_w[l, :, span])
            total = term if total is None else total + term
        dv_ref[l, 3:4, :] += jnp.sum(total * rows, axis=0, keepdims=True)
        dv_ref[l, 4:5, :] += jnp.sum(total, axis=0, keepdims=True)
        dys[g] = (upper + vector(pgain_ref, l) * total).astype(BF16)

    def mix_backward(l, g, target):
        gain, scale = vector(mgain_ref, l), vector(mscale_ref, l)
        left = xs[l, g, z.body :, :].astype(F32)
        left_grad = dys[g, z.body :, :].astype(F32)
        left_total = jnp.zeros((tile_rows, channels), F32)
        sums = [jnp.zeros((1, channels), F32) for _ in range(3)]
        for j in range(z.mine):
            mixed = mixed_rows(l, g, j, left)
            grads = [part.astype(F32) for part in image_rows(dys, None, g, j)]
            pieces = [(scale * part).astype(BF16) for part in grads]
            pieces.append(jnp.where(image_of == j, scale * left_grad, 0.0).astype(BF16))
            across = jnp.concatenate(pieces, axis=0)
            dm_ref[l, : z.mix_rows, : z.mix_cols] += dot_nt(across, mixed)
            back = dot(mix_t[l, : z.mix_cols, : z.mix_rows], across)
            for m, part in enumerate(image_rows(xs, l, g, j)):
                some = back[m * z.main : (m + 1) * z.main]
                sums[0] += jnp.sum(some * part.astype(F32), axis=0, keepdims=True)
                sums[1] += jnp.sum(some, axis=0, keepdims=True)
                target[g, pl.ds(m * z.block + j * z.main, z.main), :] = (
                    grads[m] + gain * some
                ).astype(BF16)
            left_total = jnp.where(image_of == j, back[z.image : z.mix_rows], left_total)
            sums[2] += back[z.ones : z.ones + 1]
        sums[0] += jnp.sum(left_total * left, axis=0, keepdims=True)
        sums[1] += jnp.sum(left_total, axis=0, keepdims=True)
        target[g, z.body :, :] = (left_grad + gain * left_total).astype(BF16)
        for k in range(3):
            dv_ref[l, k : k + 1, :] += sums[k]

    for copy in w_loads:
        copy.wait()
    arrive(exchange_left(0, sende_x, got_x))
    spread_left(got_x, xs.at[0])

    def forward(g, carry):
        arrive(exchange(0, g, send_x, xs.at[0]))
        sent(exchange(0, g, send_x, xs.at[0]))
        for l in range(z.layers):
            mix_forward(l, g)
            mlp_forward(l, g, xs.at[l + 1] if l + 1 < z.layers else None)
        return carry

    lax.fori_loop(0, groups, forward, 0)
    gather_left(outs_left, out_left)

    arrive(exchange_left(1, sende_dy, got_dy))
    spread_left(got_dy, dys)

    low, high = lax.rem(me, 2), lax.div(me, 2)
    pair_peer = (dp, high * 2 + 1 - low)
    cross_peer = (dp, (1 - high) * 2 + low)

    def aligned(start):
        return start if isinstance(start, int) else pl.multiple_of(start, TILE)

    def span_of(start, count):
        return pl.ds(aligned(start), count)

    def remote(job, slot, source, target, peer):
        return pltpu.make_async_remote_copy(
            src_ref=source,
            dst_ref=target,
            send_sem=job_send.at[job, slot],
            recv_sem=job_recv.at[job, slot],
            device_id=peer,
            device_id_type=MESH,
        )

    class Job:
        def __init__(self, layer, kind):
            self.layer, self.kind = layer, kind
            self.number = layer * 3 + kind
            self.rows, self.share = z.job_rows[kind], z.shares[kind]
            self.place = z.places[self.number]
            self.sums = sums_hbm.at[layer]
            self.own = self.place["pay"] + low * 2 * self.rows
            self.half = self.own + near * self.rows
            self.mine = self.half + far * 2 * self.share

        def fill(self, tile_of):
            for chunk_ in range(parts):
                for t in range(self.rows // TILE):
                    k, inner = divmod(t * TILE, self.share)
                    at = self.place["pay"] + (chunk_ % 2) * 2 * self.rows
                    at += (k * 2 + chunk_ // 2) * self.share + inner
                    value = tile_of(chunk_, t)
                    if value is None:
                        kept[at : at + TILE, :] = jnp.zeros((TILE, channels), BF16)
                    else:
                        kept[at : at + TILE, : value.shape[1]] = value.astype(BF16)
                        if value.shape[1] < channels:
                            rest = channels - value.shape[1]
                            kept[at : at + TILE, value.shape[1] :] = jnp.zeros((TILE, rest), BF16)

        def pair_copy(self):
            source = kept.at[span_of(self.place["pay"] + (1 - low) * 2 * self.rows, 2 * self.rows)]
            target = kept.at[span_of(self.place["got_pair"], 2 * self.rows)]
            return remote(self.number, 0, source, target, pair_peer)

        def near_copy(self):
            source = kept.at[span_of(self.own + (1 - near) * self.rows, self.rows)]
            target = kept.at[span_of(self.place["got_near"], self.rows)]
            return remote(self.number, 1, source, target, near_peer)

        def far_copy(self, r):
            source = kept.at[span_of(self.half + far_places[r] * 2 * self.share, 2 * self.share)]
            target = kept.at[span_of(self.place["got_far"] + (r - 1) * 2 * self.share, 2 * self.share)]
            return remote(self.number, 3 + r, source, target, far_peers[r])

        def cross_copy(self):
            source = kept.at[span_of(self.mine + (1 - high) * self.share, self.share)]
            target = kept.at[span_of(self.place["got_cross"], self.share)]
            return remote(self.number, 2, source, target, cross_peer)

        def place_of(self, near_, far_):
            start = z.job_at[self.kind] + (near_ * z.far + far_) * self.share
            return self.sums.at[span_of(start, self.share)]

        def share_copy(self, r):
            source = kept.at[span_of(self.place["final"], self.share)]
            return remote(self.number, 3 + z.far + r, source, self.place_of(near, far), far_peers[r])

        def rest_copy(self, r):
            source = kept.at[span_of(self.mine + high * self.share, self.share)]
            target = kept.at[span_of(self.place["got_rest"] + (r - 1) * self.share, self.share)]
            return remote(self.number, 3 + 2 * z.far + r, source, target, rest_peers[r])

        def own_copy(self):
            source = kept.at[span_of(self.place["final"], self.share)]
            return pltpu.make_async_copy(source, self.place_of(near, far), own_sem.at[4, self.number])

        def back_copy(self):
            start = z.job_at[self.kind] + near * z.far * self.share
            block = self.sums.at[span_of(start, z.far * self.share)]
            return remote(self.number, 3, block, block, near_peer)

        def add(self, start, count, *others):
            for at in range(0, count, 8 * TILE):
                size = min(8 * TILE, count - at)
                total = kept[span_of(start + at, size), :].astype(F32)
                for other in others:
                    total += kept[span_of(other + at, size), :].astype(F32)
                yield at, size, total.astype(BF16)

        def step(self, number):
            if number == 0:
                self.pair_copy().start()
            elif number == 1:
                self.pair_copy().wait_recv()
                for half in (1 - near, near):
                    start = half * self.rows
                    for at, size, total in self.add(
                        self.own + start, self.rows, self.place["got_pair"] + start
                    ):
                        kept[span_of(self.own + start + at, size), :] = total
                    if half is not near:
                        self.near_copy().start()
            elif number == 2:
                self.near_copy().wait_recv()
                for at, size, total in self.add(self.half, self.rows, self.place["got_near"]):
                    kept[span_of(self.half + at, size), :] = total
                for r in range(1, z.far):
                    self.far_copy(r).start()
            elif number == 3:
                for r in range(1, z.far):
                    self.far_copy(r).wait_recv()
                others = [self.place["got_far"] + (r - 1) * 2 * self.share for r in range(1, z.far)]
                for at, size, total in self.add(self.mine, 2 * self.share, *others):
                    kept[span_of(self.mine + at, size), :] = total
                self.cross_copy().start()
            elif number == 4:
                self.cross_copy().wait_recv()
                start = self.mine + high * self.share
                for at, size, total in self.add(start, self.share, self.place["got_cross"]):
                    kept[span_of(start + at, size), :] = total
                for r in range(1, z.rest):
                    self.rest_copy(r).start()
                for r in range(1, z.rest):
                    self.rest_copy(r).wait_recv()
                others = [self.place["got_rest"] + r * self.share for r in range(z.rest - 1)]
                for at, size, total in self.add(start, self.share, *others):
                    kept[span_of(self.place["final"] + at, size), :] = total
                self.own_copy().start()
                for r in range(1, z.far):
                    self.share_copy(r).start()
            elif number == 5:
                self.own_copy().wait()
                for r in range(1, z.far):
                    self.share_copy(r).wait_recv()
                self.back_copy().start()
            else:
                self.back_copy().wait()
                self.pair_copy().wait_send()
                self.near_copy().wait_send()
                self.cross_copy().wait_send()
                for r in range(1, z.far):
                    self.far_copy(r).wait_send()
                    self.share_copy(r).wait_send()
                for r in range(1, z.rest):
                    self.rest_copy(r).wait_send()

    def chunk_lanes(ref, chunk_):
        return slice(chunk_ * channels, (chunk_ + 1) * channels)

    def down_tile(chunk_, t):
        if t * TILE >= channels:
            return None
        return dd_ref[t * TILE : (t + 1) * TILE, chunk_lanes(dd_ref, chunk_)]

    def up_tile(l, first):
        def tile_of(chunk_, t):
            at = t * TILE + first
            if first == 0 and at >= z.split:
                return None
            if at < channels:
                return du_ref[at : at + TILE, chunk_lanes(du_ref, chunk_)]
            at -= channels
            if at < z.main:
                return dm_ref[l, chunk_ * z.main + at : chunk_ * z.main + at + TILE, :]
            if at == z.main:
                return dm_ref[l, z.image : z.image + TILE, :]
            if at == z.main + TILE:
                bias = dub_ref[l, :, chunk_lanes(dub_ref, chunk_)]
                rows = [dv_ref[l, 0:7, :], bias, jnp.zeros((TILE - 8, channels), F32)]
                return jnp.concatenate(rows, axis=0)
            return None

        return tile_of

    def down_sums(l):
        total = None
        for h in range(0, hidden, 2 * 128):
            span = slice(h, h + 2 * 128)
            term = dd_ref[:, span].T * down_w[l, span, :].astype(F32)
            total = term if total is None else total + term
        total = jnp.sum(total, axis=0, keepdims=True) + vector(downb_ref, l) * dv_ref[l, 5:6, :]
        dv_ref[l, 6:7, :] = total / vector(pscale_ref, l)

    def mix_sums(l):
        total = vector(mgain_ref, l) * dv_ref[l, 0:1, :] + vector(mshift_ref, l) * dv_ref[l, 1:2, :]
        dv_ref[l, 2:3, :] = (total + dv_ref[l, 2:3, :]) / vector(mscale_ref, l)

    jobs = {(l, kind): Job(l, kind) for l in range(z.layers) for kind in range(3)}
    top = z.layers - 1

    def clear(*refs):
        for ref in refs:
            ref[...] = jnp.zeros(ref.shape, F32)

    def greet(number):
        for peer in job_peers:
            pl.semaphore_signal(free_sem.at[number], inc=1, device_id=peer, device_id_type=MESH)

    def met(number):
        pl.semaphore_wait(free_sem.at[number], len(job_peers))

    def run(text):
        for entry in text.split():
            l, kind, number = int(entry[0]), "dab".index(entry[1]), int(entry[2])
            jobs[l, kind].step(number)

    thirds = [groups * k // 3 for k in range(4)]

    def backward(l, plan):
        def down(g, carry):
            if l == top:
                arrive(exchange(1, g, send_dy, dys))
            mlp_backward_down(l, g)
            return carry

        def up(g, carry):
            mlp_backward_up(l, g)
            mix_backward(l, g, dys)
            return carry

        def send_back(k, source, target, first, last):
            for g in range(first, last):
                start(exchange_back(k, g, source, target))

        clear(du_ref, dd_ref)
        if l == top:
            send_back(2, send_x, out_w, 0, thirds[1])
        lax.fori_loop(0, groups, down, 0)
        mlp_backward_down_left(l)
        if l == top:
            greet(0)
            send_back(2, send_x, out_w, thirds[1], thirds[2])
        run(plan[0])
        down_sums(l)
        jobs[l, 0].fill(down_tile)
        met(top - l)
        jobs[l, 0].step(0)
        for k in range(3):
            lax.fori_loop(thirds[k], thirds[k + 1], up, 0)
            if l == top and k == 0:
                send_back(2, send_x, out_w, thirds[2], groups)
                start(exchange_left(2, out_left, out_e))
            if l == top and k == 2:
                greet(1)
            run(plan[k + 1])
            if l == 0:
                send_back(3, dys, dx_w, thirds[k], thirds[k + 1])
        if l == 0:
            sent(exchange_left(0, sende_x, got_x))
            gather_left(dys, sende_x)
            start(exchange_left(3, sende_x, dx_e))
        mlp_backward_up_left(l)
        mix_sums(l)
        jobs[l, 1].fill(up_tile(l, 0))
        jobs[l, 1].step(0)
        jobs[l, 2].fill(up_tile(l, z.split))
        jobs[l, 2].step(0)
        run(plan[4])

    backward(1, ("", "1d1", "", "1d2", ""))
    backward(
        0,
        (
            "1a1 1b1",
            "1d3 1a2 0d1",
            "1b2 1a3 1d4",
            "0d2 1b3",
            "0a1 0b1 1a4 1b4 0d3 1d5 0a2 0b2 0d4 1a5 1b5 0a3 0b3 0d5 0a4 0b4 0a5 0b5",
        ),
    )
    run("1d6 1a6 1b6 0d6 0a6 0b6")

    for g in range(groups):
        sent(exchange(1, g, send_dy, dys))
    sent(exchange_left(1, sende_dy, got_dy))
    for copies in [exchange_left(2, out_left, out_e), exchange_left(3, sende_x, dx_e)]:
        arrive(copies)
        sent(copies)
    for g in range(groups):
        for copies in [exchange_back(2, g, send_x, out_w), exchange_back(3, g, dys, dx_w)]:
            arrive(copies)
            sent(copies)


def finish_kernel(
    z, mask_ref, out_w, out_e, dx_w, dx_e, sums,
    out_ref, dx_ref, gain_ref, shift_ref, scale_ref, mixw_ref, mixb_ref, pgain_ref, pshift_ref, pscale_ref,
    up_ref, upb_ref, down_ref, downb_ref,
):
    g = pl.program_id(0)
    swap = swap_matrix()
    pick = iota((1, GROUP * TILE), 1) >> 4
    masked = (swap * mask_lanes(mask_ref, g * GROUP, GROUP, pick)).astype(BF16)
    left_all = z.parts * z.left
    row, lane = iota((GROUP, left_all), 0), iota((GROUP, left_all), 1)
    want = row + g * z.mine
    for d in range(1, z.parts):
        want = want + jnp.where(row >= d * z.mine, z.left - z.mine, 0)
    last = jnp.where(want == lane, 1.0, 0.0)
    lanes = jnp.zeros((GROUP, 1), F32)
    for k in range(GROUP):
        lanes = jnp.where(iota((GROUP, 1), 0) == k, mask_ref[g * GROUP + k].astype(F32), lanes)
    for wire, left, target, matrix, tail in (
        (out_w, out_e, out_ref, masked, (last * lanes).astype(BF16)),
        (dx_w, dx_e, dx_ref, swap.astype(BF16), last.astype(BF16)),
    ):
        for t in range(z.main // TILE):
            block = jnp.concatenate(
                [
                    wire[0, i * z.main + t * TILE : i * z.main + (t + 1) * TILE, :]
                    for i in range(GROUP)
                ],
                axis=0,
            )
            rows = dot(matrix, block).reshape(TILE, GROUP, z.channels)
            target[t * TILE : (t + 1) * TILE] = rows.astype(target.dtype)
        rows = dot(tail, left[...].reshape(left_all, z.channels))
        target[z.patches - 1] = rows.astype(target.dtype)


    @pl.when(g == 0)
    def _():
        me = lax.axis_index("mix")
        channels, share = z.channels, z.channels // z.parts
        row, lane = iota((z.pad, z.whole), 0), iota((z.pad, z.whole), 1)
        want = row
        for m in range(1, z.parts):
            want = want + jnp.where(row >= m * z.main, 1, 0)
        for m in range(z.parts):
            base = z.image + m * z.mine
            inside = (row >= base) & (row < base + z.mine)
            want = jnp.where(inside, m * z.patches + z.patches - 1, want)
        want = jnp.where(row < z.mix_rows, want, -1)
        order = jnp.where(want == lane, 1.0, 0.0).astype(BF16)
        lanes_in, lanes_out = iota((channels, share), 0), iota((channels, share), 1)
        own = jnp.where(lanes_in == lanes_out + me * share, 1.0, 0.0).astype(BF16)
        size = z.main + TILE
        at = iota((size, 1), 0) - z.main - me * z.mine
        edge = jnp.where((at >= 0) & (at < z.mine), 1.0, 0.0)
        fold_row, fold_lane = iota((size, z.patches), 0), iota((size, z.patches), 1)
        fold_at = fold_row - z.main - me * z.mine
        fold_to = jnp.where(
            fold_row < z.main, fold_row, jnp.where((fold_at >= 0) & (fold_at < z.mine), z.main, -1)
        )
        fold = jnp.where(fold_to == fold_lane, 1.0, 0.0).astype(BF16)
        spot = jnp.where((iota((8, z.pad), 0) == 0) & (iota((8, z.pad), 1) == z.ones), 1.0, 0.0)
        for l in range(z.layers):
            down_ref[l] = sums[l, :channels, :].astype(F32).T
            up_ref[l, : z.split, :] = sums[l, z.job_at[1] : z.job_at[1] + z.split, :].astype(F32)
            start = z.job_at[2] + channels - z.split
            up_ref[l, z.split :, :] = sums[l, z.job_at[2] : start, :].astype(F32)
            rows = sums[l, start : start + size, : z.pad]
            weight = dot(rows, order)
            mixw_ref[: z.main, l, :] = weight[: z.main]
            mixw_ref[z.main, l : l + 1, :] = jnp.sum(weight * edge, axis=0, keepdims=True)
            bias = dot_nt(spot.astype(BF16), rows).astype(BF16)
            mixb_ref[l : l + 1, :] = dot(bias, fold)[:1]
            tile = sums[l, start + size : start + size + TILE, :]
            vectors = dot(tile, own)
            for k, ref in enumerate(
                (gain_ref, shift_ref, scale_ref, pgain_ref, pshift_ref, downb_ref, pscale_ref)
            ):
                ref[l : l + 1, :] = vectors[k : k + 1]
            upb_ref[l : l + 1, :] = tile[7:8, :].astype(F32)


def local(parts, copies, images_in, out_grad, slot_mask, mix_gain, mix_shift, mix_scale, mix_weight, mix_bias,
          mlp_gain, mlp_shift, mlp_scale, up_weight, up_bias, down_weight, down_bias):
    slots, patches, channels = images_in.shape
    layers, _, hidden = up_weight.shape
    z = Sizes(parts, copies, slots, patches, channels, hidden, layers)
    vmem = pl.BlockSpec(memory_space=pltpu.VMEM)
    smem = pl.BlockSpec(memory_space=pltpu.SMEM)
    hbm = pl.BlockSpec(memory_space=pl.ANY)
    wire = jax.ShapeDtypeStruct((z.groups, parts, z.block, channels), BF16)
    left = jax.ShapeDtypeStruct((parts, z.left, channels), BF16)
    dma = pltpu.SemaphoreType.DMA
    rows = (z.groups, z.rows, channels)
    out_w, out_e, dx_w, dx_e, sums = pl.pallas_call(
        functools.partial(whole_kernel, z),
        out_shape=(
            wire, left, wire, left,
            jax.ShapeDtypeStruct((layers, sum(z.job_rows), channels), BF16),
        ),
        in_specs=[hbm, hbm, smem] + [vmem] * 10 + [hbm, hbm],
        out_specs=(hbm,) * 5,
        scratch_shapes=[
            pltpu.VMEM((channels, hidden), F32),
            pltpu.VMEM((channels, hidden), F32),
            pltpu.VMEM((layers, z.pad, z.pad), F32),
            pltpu.VMEM((layers, 8, channels), F32),
            pltpu.VMEM((layers, 1, hidden), F32),
            pltpu.VMEM((z.groups, patches, GROUP, channels), BF16),
            pltpu.VMEM((z.groups, parts, z.block, channels), BF16),
            pltpu.VMEM((z.groups, parts, z.block, channels), BF16),
            pltpu.VMEM((parts, z.left, channels), BF16),
            pltpu.VMEM((parts, z.left, channels), BF16),
            pltpu.VMEM((parts, z.left, channels), BF16),
            pltpu.VMEM((parts, z.left, channels), BF16),
            pltpu.VMEM((layers, *rows), BF16),
            pltpu.VMEM((layers, *rows), BF16),
            pltpu.VMEM(rows, BF16),
            pltpu.VMEM((z.groups, parts * z.mine, channels), BF16),
            pltpu.VMEM((parts, z.left, channels), BF16),
            pltpu.VMEM((z.groups, parts * z.mine, hidden), BF16),
            pltpu.VMEM((z.kept_rows, channels), BF16),
            pltpu.VMEM((layers, channels, hidden), BF16),
            pltpu.VMEM((layers, hidden, channels), BF16),
            pltpu.VMEM((layers, z.pad, z.pad), BF16),
            pltpu.VMEM((layers, z.pad, z.pad), BF16),
            dma((2 * z.groups + 2,)),
            dma((5, max(z.groups, 3 * layers))),
            dma((4, z.groups, parts)),
            dma((4, z.groups, parts)),
            dma((4, parts)),
            dma((4, parts)),
            dma((3 * layers, 3 + 2 * z.far + z.rest)),
            dma((3 * layers, 3 + 2 * z.far + z.rest)),
            pltpu.SemaphoreType.REGULAR((2,)),
        ],
        compiler_params=pltpu.CompilerParams(
            collective_id=0, has_side_effects=True, vmem_limit_bytes=64 << 20
        ),
        name="layers",
    )(
        jnp.transpose(images_in, (1, 0, 2)),
        jnp.transpose(out_grad, (1, 0, 2)),
        slot_mask,
        jnp.transpose(mix_weight, (1, 0, 2)),
        mix_bias, mix_gain, mix_shift, mix_scale, mlp_gain, mlp_shift, mlp_scale, down_bias, up_bias,
        up_weight, down_weight,
    )

    flat = (z.groups, parts * z.block, channels)
    block = pl.BlockSpec((1, *flat[1:]), lambda g: (g, 0, 0))
    whole = pl.BlockSpec(left.shape, lambda g: (0, 0, 0))
    turned = pl.BlockSpec((patches, GROUP, channels), lambda g: (0, g, 0))
    share = channels // parts
    small = jax.ShapeDtypeStruct((layers, share), F32)
    small_block = pl.BlockSpec(small.shape, lambda g: (0, 0))
    shapes = [
        jax.ShapeDtypeStruct((patches, slots, channels), BF16),
        jax.ShapeDtypeStruct((patches, slots, channels), F32),
        small, small, small,
        jax.ShapeDtypeStruct((patches, layers, z.whole), F32),
        jax.ShapeDtypeStruct((layers, patches), F32),
        small, small, small,
        jax.ShapeDtypeStruct((layers, channels, hidden // parts), F32),
        jax.ShapeDtypeStruct((layers, hidden // parts), F32),
        jax.ShapeDtypeStruct((layers, hidden // parts, channels), F32),
        small,
    ]

    def fixed(shape):
        return pl.BlockSpec(shape, lambda g: (0,) * len(shape))

    results = list(
        pl.pallas_call(
            functools.partial(finish_kernel, z),
            grid=(z.groups,),
            out_shape=shapes,
            in_specs=[smem, block, whole, block, whole, fixed(sums.shape)],
            out_specs=[turned, turned] + [fixed(shape.shape) for shape in shapes[2:]],
            compiler_params=pltpu.CompilerParams(vmem_limit_bytes=64 << 20),
            name="finish",
        )(slot_mask, out_w.reshape(flat), out_e, dx_w.reshape(flat), dx_e, sums)
    )
    for k in (0, 1, 5):
        results[k] = jnp.transpose(results[k], (1, 0, 2))
    return tuple(results)


def solution(mesh):
    in_specs = (P("dp", "mix", None), P("dp", "mix", None), P("dp")) + (P(),) * 12
    out_specs = (
        P("dp", "mix", None),
        P("dp", "mix", None),
        P(None, "mix"),
        P(None, "mix"),
        P(None, "mix"),
        P(None, "mix", None),
        P(None, "mix"),
        P(None, "mix"),
        P(None, "mix"),
        P(None, "mix"),
        P(None, None, "mix"),
        P(None, "mix"),
        P(None, "mix", None),
        P(None, "mix"),
    )
    return jax.shard_map(
        functools.partial(local, mesh.shape["mix"], mesh.shape["dp"]),
        mesh=mesh,
        in_specs=in_specs,
        out_specs=out_specs,
        check_vma=False,
    )
```

```python
import functools
import math

import jax
import jax.numpy as jnp
from jax import lax
from jax.experimental import pallas as pl
from jax.experimental.pallas import tpu as pltpu
from jax.sharding import PartitionSpec as P

MESH = pl.DeviceIdType.MESH
F32 = jnp.float32
BF16 = jnp.bfloat16
GROUP = 16
TILE = 16
TANH_A = math.sqrt(2.0 / math.pi)
TANH_B = TANH_A * 0.044715


def dot(a, b):
    return jnp.dot(a, b, preferred_element_type=F32)


def dot_nt(a, b):
    return lax.dot_general(a, b, (((1,), (1,)), ((), ())), preferred_element_type=F32)


def iota(shape, axis):
    return lax.broadcasted_iota(jnp.int32, shape, axis)


def gelu_pair(value):
    square = value * value
    gate = 0.5 * jnp.tanh(value * (TANH_A + TANH_B * square)) + 0.5
    active = value * gate
    return active, gate + (active - active * gate) * (2.0 * TANH_A + (6.0 * TANH_B) * square)


def mask_lanes(mask_ref, first, count, pick):
    total = jnp.zeros(pick.shape, F32)
    for k in range(count):
        total = jnp.where(pick == k, mask_ref[first + k].astype(F32), total)
    return total


def swap_matrix():
    side = GROUP * TILE
    row, lane = iota((side, side), 0), iota((side, side), 1)
    return jnp.where((row >> 4) + ((row & 15) << 4) == lane, 1.0, 0.0)


class Sizes:
    def __init__(self, parts, copies, slots, patches, channels, hidden, layers):
        self.parts = parts
        self.slots = slots
        self.patches = patches
        self.channels = channels
        self.hidden = hidden
        self.layers = layers
        self.groups = slots // GROUP
        self.mine = GROUP // parts
        self.main = patches // TILE * TILE
        self.block = self.mine * self.main
        self.body = parts * self.block
        self.rows = self.body + parts * self.mine
        self.image = parts * self.main
        self.mix_rows = self.image + parts * self.mine
        self.ones = self.mix_rows
        self.mix_cols = self.mix_rows + TILE
        self.pad = -(-self.mix_cols // 128) * 128
        self.left = -(-self.groups * self.mine // TILE) * TILE
        self.whole = parts * patches
        self.quarters = hidden // channels
        self.far = min(copies // 2, 4)
        self.rest = copies // (2 * self.far)
        cuts = 2 * self.far
        step = TILE * cuts
        self.split = channels * 2 // 3 // TILE * TILE
        counts = (channels, self.split, channels - self.split + self.main + 2 * TILE)
        self.job_rows = [-(-count // step) * step for count in counts]
        self.job_at = [sum(self.job_rows[:kind]) for kind in range(3)]
        self.shares = [count // cuts for count in self.job_rows]
        act_rows = self.quarters * self.rows * self.groups
        self.places = []
        for layer in range(layers):
            at = (2 * (layers - 1) + layers - 1 - layer) * act_rows
            for kind in range(3):
                count, share = self.job_rows[kind], self.shares[kind]
                place = {}
                for name, size in (
                    ("pay", 4 * count),
                    ("got_pair", 2 * count),
                    ("got_near", count),
                    ("got_far", (self.far - 1) * 2 * share),
                    ("got_cross", share),
                    ("got_rest", (self.rest - 1) * share),
                    ("final", share),
                ):
                    place[name] = at
                    at += size
                self.places.append(place)
        self.kept_rows = max(at, 2 * layers * act_rows)


def whole_kernel(
    z,
    x_hbm, dy_hbm, mask_ref, mixw_ref, mixb_ref,
    mgain_ref, mshift_ref, mscale_ref, pgain_ref, pshift_ref, pscale_ref, downb_ref, upb_ref,
    up_hbm, down_hbm,
    out_w, out_e, dx_w, dx_e, sums_hbm,
    du_ref, dd_ref, dm_ref, dv_ref, dub_ref, stage, send_x, send_dy, sende_x, sende_dy, got_x, got_dy,
    xs, firsts, dys, outs_left, out_left, tails, kept, up_w, down_w, mix_m, mix_t,
    load_sem, own_sem, send_sem, recv_sem, lsend_sem, lrecv_sem, job_send, job_recv, free_sem,
):
    dp, me = lax.axis_index("dp"), lax.axis_index("mix")
    parts, groups, channels, hidden = z.parts, z.groups, z.channels, z.hidden
    peers = [lax.rem(me + r, parts) for r in range(parts)]

    loads = []
    for k, hbm in enumerate((x_hbm, dy_hbm)):
        for g in range(groups):
            loads.append(
                pltpu.make_async_copy(
                    hbm.at[:, pl.ds(g * GROUP, GROUP), :], stage.at[g], load_sem.at[k * groups + g]
                )
            )
    w_loads = [
        pltpu.make_async_copy(up_hbm, up_w, load_sem.at[2 * groups]),
        pltpu.make_async_copy(down_hbm, down_w, load_sem.at[2 * groups + 1]),
    ]
    for copy in loads[:groups] + w_loads:
        copy.start()

    barrier = pltpu.get_barrier_semaphore()
    near, upper_place = lax.rem(dp, 2), lax.div(dp, 2)
    far, rest = lax.rem(upper_place, z.far), lax.div(upper_place, z.far)
    row_peers = [(dp, peers[r]) for r in range(1, parts)]
    near_peer = (dp + 1 - 2 * near, me)
    far_places = [lax.rem(far + r, z.far) for r in range(z.far)]
    far_peers = [((rest * z.far + far_places[r]) * 2 + near, me) for r in range(z.far)]
    rest_peers = [
        ((lax.rem(rest + r, z.rest) * z.far + far) * 2 + near, me) for r in range(z.rest)
    ]
    job_peers = row_peers + [near_peer] + far_peers[1:] + rest_peers[1:]
    for peer in job_peers:
        pl.semaphore_signal(barrier, inc=1, device_id=peer, device_id_type=MESH)

    swap = swap_matrix()
    swap_b = swap.astype(BF16)
    left_all = parts * z.left

    def convert(send, g, matrix):
        for t in range(z.main // TILE):
            block = stage[g, t * TILE : (t + 1) * TILE].reshape(TILE * GROUP, channels)
            rows = dot(matrix, block).astype(BF16).reshape(GROUP, TILE, channels)
            for d in range(parts):
                for j in range(z.mine):
                    send[g, d, j * z.main + t * TILE : j * z.main + (t + 1) * TILE, :] = rows[
                        d * z.mine + j
                    ]

    def convert_left(send, lanes):
        row, lane = iota((left_all, z.slots), 0), iota((left_all, z.slots), 1)
        want = jnp.full(row.shape, -1, jnp.int32)
        for d in range(parts):
            for g in range(groups):
                base = d * z.left + g * z.mine
                inside = (row >= base) & (row < base + z.mine)
                want = jnp.where(inside, row - base + g * GROUP + d * z.mine, want)
        matrix = jnp.where(want == lane, 1.0, 0.0)
        if lanes is not None:
            matrix = matrix * lanes
        last = jnp.concatenate([stage[g, z.patches - 1] for g in range(groups)], axis=0)
        send[...] = dot(matrix.astype(BF16), last).astype(BF16).reshape(parts, z.left, channels)

    def exchange(k, g, send, target):
        copies = [lambda: pltpu.make_async_copy(send.at[g, me], target.at[g, pl.ds(me * z.block, z.block)], own_sem.at[k, g])]
        for r in range(1, parts):
            copies.append(
                pltpu.make_async_remote_copy(
                    src_ref=send.at[g, peers[r]],
                    dst_ref=target.at[g, pl.ds(me * z.block, z.block)],
                    send_sem=send_sem.at[k, g, r],
                    recv_sem=recv_sem.at[k, g, r],
                    device_id=(dp, peers[r]),
                    device_id_type=MESH,
                )
            )
        return copies

    def part_of(source, g, d):
        if len(source.shape) == 4:
            return source.at[g, d]
        return source.at[g, pl.ds(d * z.block, z.block)]

    def exchange_back(k, g, source, target):
        copies = [lambda: pltpu.make_async_copy(part_of(source, g, me), target.at[g, me], own_sem.at[k, g])]
        for r in range(1, parts):
            copies.append(
                pltpu.make_async_remote_copy(
                    src_ref=part_of(source, g, peers[r]),
                    dst_ref=target.at[g, me],
                    send_sem=send_sem.at[k, g, r],
                    recv_sem=recv_sem.at[k, g, r],
                    device_id=(dp, peers[r]),
                    device_id_type=MESH,
                )
            )
        return copies

    def exchange_left(k, send, target):
        copies = [lambda: pltpu.make_async_copy(send.at[me], target.at[me], lsend_sem.at[k, 0])]
        for r in range(1, parts):
            copies.append(
                pltpu.make_async_remote_copy(
                    src_ref=send.at[peers[r]],
                    dst_ref=target.at[me],
                    send_sem=lsend_sem.at[k, r],
                    recv_sem=lrecv_sem.at[k, r],
                    device_id=(dp, peers[r]),
                    device_id_type=MESH,
                )
            )
        return copies

    def start(copies):
        copies[0]().start()
        for copy in copies[1:]:
            copy.start()

    def arrive(copies):
        copies[0]().wait()
        for copy in copies[1:]:
            copy.wait_recv()

    def sent(copies):
        for copy in copies[1:]:
            copy.wait_send()

    for g in range(groups):
        if g == 0:
            loads[g].wait()
        convert(send_x, g, swap_b)
        if g == 0:
            pl.semaphore_wait(barrier, len(job_peers))
        start(exchange(0, g, send_x, xs.at[0]))
        if g == 0:
            for copy in loads[1:groups]:
                copy.wait()
            convert_left(sende_x, None)
            start(exchange_left(0, sende_x, got_x))
    for copy in loads[groups:]:
        copy.start()
    for g in range(groups):
        loads[groups + g].wait()
        pick = iota((1, GROUP * TILE), 1) & 15
        lanes = mask_lanes(mask_ref, g * GROUP, GROUP, pick)
        convert(send_dy, g, (swap * lanes).astype(BF16))
        start(exchange(1, g, send_dy, dys))
    convert_left(sende_dy, mask_lanes(mask_ref, 0, z.slots, iota((1, z.slots), 1)))
    start(exchange_left(1, sende_dy, got_dy))

    size = (z.pad, z.whole)
    row, lane = iota(size, 0), iota(size, 1)
    want = row
    for m in range(1, parts):
        want = want + jnp.where(row >= m * z.main, 1, 0)
    for m in range(parts):
        base = z.image + m * z.mine
        inside = (row >= base) & (row < base + z.mine)
        want = jnp.where(inside, m * z.patches + z.patches - 1, want)
    want = jnp.where(row < z.mix_rows, want, -1)
    pick = jnp.where(want == lane, 1.0, 0.0).astype(BF16)
    spot = jnp.where((iota((z.pad, TILE), 0) == z.ones) & (iota((z.pad, TILE), 1) == 0), 1.0, 0.0)
    for l in range(z.layers):
        half = dot(pick, mixw_ref[:, l, :]).astype(BF16)
        offset = jnp.where(iota((TILE, z.whole), 0) == 0, mixb_ref[l : l + 1, :].astype(F32), 0.0)
        column = dot_nt(pick, offset.astype(BF16)).astype(BF16)
        full = dot_nt(half, pick) + dot_nt(column, spot.astype(BF16))
        mix_m[l] = full.astype(BF16)
        mix_t[l] = full.T.astype(BF16)

    for ref in (dm_ref, dv_ref, dub_ref):
        ref[...] = jnp.zeros(ref.shape, F32)

    def spread_left(got, target):
        tile = parts * z.mine
        row, lane = iota((groups * tile, left_all), 0), iota((groups * tile, left_all), 1)
        want = jnp.full(row.shape, -1, jnp.int32)
        for g in range(groups):
            for m in range(parts):
                base = g * tile + m * z.mine
                inside = (row >= base) & (row < base + z.mine)
                want = jnp.where(inside, row - base + m * z.left + g * z.mine, want)
        matrix = jnp.where(want == lane, 1.0, 0.0).astype(BF16)
        rows = dot(matrix, got[...].reshape(left_all, channels)).astype(BF16)
        for g in range(groups):
            target[g, z.body :, :] = rows[g * tile : (g + 1) * tile]

    def gather_left(source, target):
        tile = parts * z.mine
        row, lane = iota((left_all, groups * tile), 0), iota((left_all, groups * tile), 1)
        want = jnp.full(row.shape, -1, jnp.int32)
        for g in range(groups):
            for m in range(parts):
                base = m * z.left + g * z.mine
                inside = (row >= base) & (row < base + z.mine)
                want = jnp.where(inside, row - base + g * tile + m * z.mine, want)
        matrix = jnp.where(want == lane, 1.0, 0.0).astype(BF16)
        low = 0 if source.shape[1] == tile else z.body
        rows = jnp.concatenate([source[g, low:, :] for g in range(groups)], axis=0)
        target[...] = dot(matrix, rows).astype(BF16).reshape(parts, z.left, channels)

    def vector(ref, l):
        return ref[l : l + 1, :].astype(F32)

    tile_rows = parts * z.mine
    image_of = iota((tile_rows, 1), 0) & (z.mine - 1)
    ones_tile = jnp.where(iota((TILE, channels), 0) == 0, 1.0, 0.0).astype(BF16)

    def image_rows(ref, l, g, j):
        index = (g,) if l is None else (l, g)
        return [
            ref[(*index, pl.ds(m * z.block + j * z.main, z.main), slice(None))] for m in range(parts)
        ]

    def mixed_rows(l, g, j, left):
        gain, shift = vector(mgain_ref, l), vector(mshift_ref, l)
        pieces = [
            (gain * part.astype(F32) + shift).astype(BF16) for part in image_rows(xs, l, g, j)
        ]
        pieces.append(jnp.where(image_of == j, gain * left + shift, 0.0).astype(BF16))
        pieces.append(ones_tile)
        return jnp.concatenate(pieces, axis=0)

    def mix_forward(l, g):
        scale = vector(mscale_ref, l)
        left = xs[l, g, z.body :, :].astype(F32)
        left_total = jnp.zeros((tile_rows, channels), F32)
        for j in range(z.mine):
            mixed = mixed_rows(l, g, j, left)
            across = dot(mix_m[l, : z.mix_rows, : z.mix_cols], mixed)
            for m, part in enumerate(image_rows(xs, l, g, j)):
                rows = part.astype(F32) + scale * across[m * z.main : (m + 1) * z.main]
                firsts[l, g, pl.ds(m * z.block + j * z.main, z.main), :] = rows.astype(BF16)
            left_total = jnp.where(image_of == j, across[z.image :], left_total)
        firsts[l, g, z.body :, :] = (left + scale * left_total).astype(BF16)

    chunk = 256 if hidden % 256 == 0 else 128
    back_chunk = 512 if hidden % 512 == 0 else 128

    def kept_at(l, which, g, quarter):
        index = (l * 2 + which) * groups + g
        start = (index * z.quarters + quarter) * z.rows
        return start if isinstance(start, int) else pl.multiple_of(start, TILE)

    def pieces_of(h, chunk):
        pieces, at = [], h
        while at < h + chunk:
            quarter, lane = divmod(at, channels)
            end = min(channels, lane + h + chunk - at)
            pieces.append((quarter, lane, end))
            at += end - lane
        return pieces

    def keep_rows(l, which, g, h, value, chunk, first):
        value, at = value.astype(BF16), 0
        for quarter, lane, end in pieces_of(h, chunk):
            place = pl.ds(kept_at(l, which, g, quarter) + first, value.shape[0])
            kept[place, lane:end] = value[:, at : at + end - lane]
            at += end - lane

    def kept_rows(l, which, g, h, chunk, first, count):
        parts_ = [
            kept[pl.ds(kept_at(l, which, g, quarter) + first, count), lane:end]
            for quarter, lane, end in pieces_of(h, chunk)
        ]
        return jnp.concatenate(parts_, axis=1)

    def mlp_normed(l, g, span=slice(None)):
        rows = firsts[l, g, span, :].astype(F32)
        return rows, (vector(pgain_ref, l) * rows + vector(pshift_ref, l)).astype(BF16)

    piece = z.rows // 4 // TILE * TILE
    spans = [slice(k * piece, (k + 1) * piece if k < 3 else z.rows) for k in range(4)]

    def mlp_forward(l, g, target):
        bias = upb_ref[l : l + 1, :].astype(F32)
        normed = [mlp_normed(l, g, span)[1] for span in spans]
        steps = [(h, k) for h in range(0, hidden, chunk) for k in range(len(spans))]

        def rise(step):
            h, k = step
            return dot(normed[k], up_w[l, :, h : h + chunk]) + bias[:, h : h + chunk]

        totals, coming = [None] * len(spans), rise(steps[0])
        for at, (h, k) in enumerate(steps):
            value = coming
            if at + 1 < len(steps):
                coming = rise(steps[at + 1])
            active, grade = gelu_pair(value)
            active = active.astype(BF16)
            keep_rows(l, 0, g, h, active, chunk, spans[k].start)
            keep_rows(l, 1, g, h, grade, chunk, spans[k].start)
            term = dot(active, down_w[l, h : h + chunk, :])
            totals[k] = term if totals[k] is None else totals[k] + term
        for span, total in zip(spans, totals):
            result = firsts[l, g, span, :].astype(F32)
            result = result + vector(pscale_ref, l) * (total + vector(downb_ref, l))
            result = result.astype(BF16)
            if target is not None:
                target[g, span, :] = result
                continue
            for d in range(parts):
                low, high = max(span.start, d * z.block), min(span.stop, (d + 1) * z.block)
                if low < high:
                    send_x[g, d, low - d * z.block : high - d * z.block, :] = result[
                        low - span.start : high - span.start
                    ]
            if span.stop == z.rows:
                outs_left[g] = result[z.body - span.start :]

    def mlp_backward_down(l, g):
        branch = (vector(pscale_ref, l) * dys[g, : z.body, :].astype(F32)).astype(BF16)
        dv_ref[l, 5:6, :] += jnp.sum(branch.astype(F32), axis=0, keepdims=True)
        branch_t = branch.T
        for h in range(0, hidden, back_chunk):
            span = slice(h, h + back_chunk)
            dd_ref[:, span] += dot(branch_t, kept_rows(l, 0, g, h, back_chunk, 0, z.body))

    def left_rows(ref):
        return jnp.concatenate([ref[g, z.body :, :] for g in range(groups)], axis=0).astype(F32)

    def mlp_backward_down_left(l):
        branch = (vector(pscale_ref, l) * left_rows(dys)).astype(BF16)
        dv_ref[l, 5:6, :] += jnp.sum(branch.astype(F32), axis=0, keepdims=True)
        branch_t = branch.T
        for h in range(0, hidden, back_chunk):
            span = slice(h, h + back_chunk)
            rows = [
                kept_rows(l, 0, g, h, back_chunk, z.body, z.rows - z.body) for g in range(groups)
            ]
            dd_ref[:, span] += dot(branch_t, jnp.concatenate(rows, axis=0))

    def mlp_backward_up_left(l):
        rows = left_rows(firsts.at[l])
        normed = (vector(pgain_ref, l) * rows + vector(pshift_ref, l)).astype(BF16)
        normed_t = normed.T
        for h in range(0, hidden, back_chunk):
            span = slice(h, h + back_chunk)
            grads = jnp.concatenate([tails[g, :, span] for g in range(groups)], axis=0)
            du_ref[:, span] += dot(normed_t, grads)

    def mlp_backward_up(l, g):
        rows, normed = mlp_normed(l, g)
        upper = dys[g].astype(F32)
        branch = (vector(pscale_ref, l) * upper).astype(BF16)
        normed_t = normed[: z.body].T
        total = None
        for h in range(0, hidden, back_chunk):
            span = slice(h, h + back_chunk)
            back = dot_nt(branch, down_w[l, span, :])
            grad = (back * kept_rows(l, 1, g, h, back_chunk, 0, z.rows).astype(F32)).astype(BF16)
            dub_ref[l, :, span] += jnp.sum(grad.astype(F32), axis=0, keepdims=True)
            tails[g, :, span] = grad[z.body :]
            du_ref[:, span] += dot(normed_t, grad[: z.body])
            term = dot_nt(grad, up_w[l, :, span])
            total = term if total is None else total + term
        dv_ref[l, 3:4, :] += jnp.sum(total * rows, axis=0, keepdims=True)
        dv_ref[l, 4:5, :] += jnp.sum(total, axis=0, keepdims=True)
        dys[g] = (upper + vector(pgain_ref, l) * total).astype(BF16)

    def mix_backward(l, g, target):
        gain, scale = vector(mgain_ref, l), vector(mscale_ref, l)
        left = xs[l, g, z.body :, :].astype(F32)
        left_grad = dys[g, z.body :, :].astype(F32)
        left_total = jnp.zeros((tile_rows, channels), F32)
        sums = [jnp.zeros((1, channels), F32) for _ in range(3)]
        for j in range(z.mine):
            mixed = mixed_rows(l, g, j, left)
            grads = [part.astype(F32) for part in image_rows(dys, None, g, j)]
            pieces = [(scale * part).astype(BF16) for part in grads]
            pieces.append(jnp.where(image_of == j, scale * left_grad, 0.0).astype(BF16))
            across = jnp.concatenate(pieces, axis=0)
            dm_ref[l, : z.mix_rows, : z.mix_cols] += dot_nt(across, mixed)
            back = dot(mix_t[l, : z.mix_cols, : z.mix_rows], across)
            for m, part in enumerate(image_rows(xs, l, g, j)):
                some = back[m * z.main : (m + 1) * z.main]
                sums[0] += jnp.sum(some * part.astype(F32), axis=0, keepdims=True)
                sums[1] += jnp.sum(some, axis=0, keepdims=True)
                target[g, pl.ds(m * z.block + j * z.main, z.main), :] = (
                    grads[m] + gain * some
                ).astype(BF16)
            left_total = jnp.where(image_of == j, back[z.image : z.mix_rows], left_total)
            sums[2] += back[z.ones : z.ones + 1]
        sums[0] += jnp.sum(left_total * left, axis=0, keepdims=True)
        sums[1] += jnp.sum(left_total, axis=0, keepdims=True)
        target[g, z.body :, :] = (left_grad + gain * left_total).astype(BF16)
        for k in range(3):
            dv_ref[l, k : k + 1, :] += sums[k]

    for copy in w_loads:
        copy.wait()
    arrive(exchange_left(0, sende_x, got_x))
    spread_left(got_x, xs.at[0])

    def forward(g, carry):
        arrive(exchange(0, g, send_x, xs.at[0]))
        sent(exchange(0, g, send_x, xs.at[0]))
        for l in range(z.layers):
            mix_forward(l, g)
            mlp_forward(l, g, xs.at[l + 1] if l + 1 < z.layers else None)
        return carry

    lax.fori_loop(0, groups, forward, 0)
    gather_left(outs_left, out_left)

    arrive(exchange_left(1, sende_dy, got_dy))
    spread_left(got_dy, dys)

    low, high = lax.rem(me, 2), lax.div(me, 2)
    pair_peer = (dp, high * 2 + 1 - low)
    cross_peer = (dp, (1 - high) * 2 + low)

    def aligned(start):
        return start if isinstance(start, int) else pl.multiple_of(start, TILE)

    def span_of(start, count):
        return pl.ds(aligned(start), count)

    def remote(job, slot, source, target, peer):
        return pltpu.make_async_remote_copy(
            src_ref=source,
            dst_ref=target,
            send_sem=job_send.at[job, slot],
            recv_sem=job_recv.at[job, slot],
            device_id=peer,
            device_id_type=MESH,
        )

    class Job:
        def __init__(self, layer, kind):
            self.layer, self.kind = layer, kind
            self.number = layer * 3 + kind
            self.rows, self.share = z.job_rows[kind], z.shares[kind]
            self.place = z.places[self.number]
            self.sums = sums_hbm.at[layer]
            self.own = self.place["pay"] + low * 2 * self.rows
            self.half = self.own + near * self.rows
            self.mine = self.half + far * 2 * self.share

        def fill(self, tile_of):
            for chunk_ in range(parts):
                for t in range(self.rows // TILE):
                    k, inner = divmod(t * TILE, self.share)
                    at = self.place["pay"] + (chunk_ % 2) * 2 * self.rows
                    at += (k * 2 + chunk_ // 2) * self.share + inner
                    value = tile_of(chunk_, t)
                    if value is None:
                        kept[at : at + TILE, :] = jnp.zeros((TILE, channels), BF16)
                    else:
                        kept[at : at + TILE, : value.shape[1]] = value.astype(BF16)
                        if value.shape[1] < channels:
                            rest = channels - value.shape[1]
                            kept[at : at + TILE, value.shape[1] :] = jnp.zeros((TILE, rest), BF16)

        def pair_copy(self):
            source = kept.at[span_of(self.place["pay"] + (1 - low) * 2 * self.rows, 2 * self.rows)]
            target = kept.at[span_of(self.place["got_pair"], 2 * self.rows)]
            return remote(self.number, 0, source, target, pair_peer)

        def near_copy(self):
            source = kept.at[span_of(self.own + (1 - near) * self.rows, self.rows)]
            target = kept.at[span_of(self.place["got_near"], self.rows)]
            return remote(self.number, 1, source, target, near_peer)

        def far_copy(self, r):
            source = kept.at[span_of(self.half + far_places[r] * 2 * self.share, 2 * self.share)]
            target = kept.at[span_of(self.place["got_far"] + (r - 1) * 2 * self.share, 2 * self.share)]
            return remote(self.number, 3 + r, source, target, far_peers[r])

        def cross_copy(self):
            source = kept.at[span_of(self.mine + (1 - high) * self.share, self.share)]
            target = kept.at[span_of(self.place["got_cross"], self.share)]
            return remote(self.number, 2, source, target, cross_peer)

        def place_of(self, near_, far_):
            start = z.job_at[self.kind] + (near_ * z.far + far_) * self.share
            return self.sums.at[span_of(start, self.share)]

        def share_copy(self, r):
            source = kept.at[span_of(self.place["final"], self.share)]
            return remote(self.number, 3 + z.far + r, source, self.place_of(near, far), far_peers[r])

        def rest_copy(self, r):
            source = kept.at[span_of(self.mine + high * self.share, self.share)]
            target = kept.at[span_of(self.place["got_rest"] + (r - 1) * self.share, self.share)]
            return remote(self.number, 3 + 2 * z.far + r, source, target, rest_peers[r])

        def own_copy(self):
            source = kept.at[span_of(self.place["final"], self.share)]
            return pltpu.make_async_copy(source, self.place_of(near, far), own_sem.at[4, self.number])

        def back_copy(self):
            start = z.job_at[self.kind] + near * z.far * self.share
            block = self.sums.at[span_of(start, z.far * self.share)]
            return remote(self.number, 3, block, block, near_peer)

        def add(self, start, count, *others):
            for at in range(0, count, 8 * TILE):
                size = min(8 * TILE, count - at)
                total = kept[span_of(start + at, size), :].astype(F32)
                for other in others:
                    total += kept[span_of(other + at, size), :].astype(F32)
                yield at, size, total.astype(BF16)

        def step(self, number):
            if number == 0:
                self.pair_copy().start()
            elif number == 1:
                self.pair_copy().wait_recv()
                for half in (1 - near, near):
                    start = half * self.rows
                    for at, size, total in self.add(
                        self.own + start, self.rows, self.place["got_pair"] + start
                    ):
                        kept[span_of(self.own + start + at, size), :] = total
                    if half is not near:
                        self.near_copy().start()
            elif number == 2:
                self.near_copy().wait_recv()
                for at, size, total in self.add(self.half, self.rows, self.place["got_near"]):
                    kept[span_of(self.half + at, size), :] = total
                for r in range(1, z.far):
                    self.far_copy(r).start()
            elif number == 3:
                for r in range(1, z.far):
                    self.far_copy(r).wait_recv()
                others = [self.place["got_far"] + (r - 1) * 2 * self.share for r in range(1, z.far)]
                for at, size, total in self.add(self.mine, 2 * self.share, *others):
                    kept[span_of(self.mine + at, size), :] = total
                self.cross_copy().start()
            elif number == 4:
                self.cross_copy().wait_recv()
                start = self.mine + high * self.share
                for at, size, total in self.add(start, self.share, self.place["got_cross"]):
                    kept[span_of(start + at, size), :] = total
                for r in range(1, z.rest):
                    self.rest_copy(r).start()
                for r in range(1, z.rest):
                    self.rest_copy(r).wait_recv()
                others = [self.place["got_rest"] + r * self.share for r in range(z.rest - 1)]
                for at, size, total in self.add(start, self.share, *others):
                    kept[span_of(self.place["final"] + at, size), :] = total
                self.own_copy().start()
                for r in range(1, z.far):
                    self.share_copy(r).start()
            elif number == 5:
                self.own_copy().wait()
                for r in range(1, z.far):
                    self.share_copy(r).wait_recv()
                self.back_copy().start()
            else:
                self.back_copy().wait()
                self.pair_copy().wait_send()
                self.near_copy().wait_send()
                self.cross_copy().wait_send()
                for r in range(1, z.far):
                    self.far_copy(r).wait_send()
                    self.share_copy(r).wait_send()
                for r in range(1, z.rest):
                    self.rest_copy(r).wait_send()

    def chunk_lanes(ref, chunk_):
        return slice(chunk_ * channels, (chunk_ + 1) * channels)

    def down_tile(chunk_, t):
        if t * TILE >= channels:
            return None
        return dd_ref[t * TILE : (t + 1) * TILE, chunk_lanes(dd_ref, chunk_)]

    def up_tile(l, first):
        def tile_of(chunk_, t):
            at = t * TILE + first
            if first == 0 and at >= z.split:
                return None
            if at < channels:
                return du_ref[at : at + TILE, chunk_lanes(du_ref, chunk_)]
            at -= channels
            if at < z.main:
                return dm_ref[l, chunk_ * z.main + at : chunk_ * z.main + at + TILE, :]
            if at == z.main:
                return dm_ref[l, z.image : z.image + TILE, :]
            if at == z.main + TILE:
                bias = dub_ref[l, :, chunk_lanes(dub_ref, chunk_)]
                rows = [dv_ref[l, 0:7, :], bias, jnp.zeros((TILE - 8, channels), F32)]
                return jnp.concatenate(rows, axis=0)
            return None

        return tile_of

    def down_sums(l):
        total = None
        for h in range(0, hidden, 2 * 128):
            span = slice(h, h + 2 * 128)
            term = dd_ref[:, span].T * down_w[l, span, :].astype(F32)
            total = term if total is None else total + term
        total = jnp.sum(total, axis=0, keepdims=True) + vector(downb_ref, l) * dv_ref[l, 5:6, :]
        dv_ref[l, 6:7, :] = total / vector(pscale_ref, l)

    def mix_sums(l):
        total = vector(mgain_ref, l) * dv_ref[l, 0:1, :] + vector(mshift_ref, l) * dv_ref[l, 1:2, :]
        dv_ref[l, 2:3, :] = (total + dv_ref[l, 2:3, :]) / vector(mscale_ref, l)

    jobs = {(l, kind): Job(l, kind) for l in range(z.layers) for kind in range(3)}
    top = z.layers - 1

    def clear(*refs):
        for ref in refs:
            ref[...] = jnp.zeros(ref.shape, F32)

    def greet(number):
        for peer in job_peers:
            pl.semaphore_signal(free_sem.at[number], inc=1, device_id=peer, device_id_type=MESH)

    def met(number):
        pl.semaphore_wait(free_sem.at[number], len(job_peers))

    def run(text):
        for entry in text.split():
            l, kind, number = int(entry[0]), "dab".index(entry[1]), int(entry[2])
            jobs[l, kind].step(number)

    thirds = [groups * k // 3 for k in range(4)]

    def backward(l, plan):
        def down(g, carry):
            if l == top:
                arrive(exchange(1, g, send_dy, dys))
            mlp_backward_down(l, g)
            return carry

        def up(g, carry):
            mlp_backward_up(l, g)
            mix_backward(l, g, dys)
            return carry

        def send_back(k, source, target, first, last):
            for g in range(first, last):
                start(exchange_back(k, g, source, target))

        clear(du_ref, dd_ref)
        if l == top:
            send_back(2, send_x, out_w, 0, thirds[1])
        lax.fori_loop(0, groups, down, 0)
        mlp_backward_down_left(l)
        if l == top:
            greet(0)
            send_back(2, send_x, out_w, thirds[1], thirds[2])
        run(plan[0])
        down_sums(l)
        jobs[l, 0].fill(down_tile)
        met(top - l)
        jobs[l, 0].step(0)
        for k in range(3):
            lax.fori_loop(thirds[k], thirds[k + 1], up, 0)
            if l == top and k == 0:
                send_back(2, send_x, out_w, thirds[2], groups)
                start(exchange_left(2, out_left, out_e))
            if l == top and k == 2:
                greet(1)
            run(plan[k + 1])
            if l == 0:
                send_back(3, dys, dx_w, thirds[k], thirds[k + 1])
        if l == 0:
            sent(exchange_left(0, sende_x, got_x))
            gather_left(dys, sende_x)
            start(exchange_left(3, sende_x, dx_e))
        mlp_backward_up_left(l)
        mix_sums(l)
        jobs[l, 1].fill(up_tile(l, 0))
        jobs[l, 1].step(0)
        jobs[l, 2].fill(up_tile(l, z.split))
        jobs[l, 2].step(0)
        run(plan[4])

    backward(1, ("", "1d1", "", "1d2", ""))
    backward(
        0,
        (
            "1a1 1b1",
            "1d3 1a2 0d1",
            "1b2 1a3 1d4",
            "0d2 1b3",
            "0a1 0b1 1a4 1b4 0d3 1d5 0a2 0b2 0d4 1a5 1b5 0a3 0b3 0d5 0a4 0b4 0a5 0b5",
        ),
    )
    run("1d6 1a6 1b6 0d6 0a6 0b6")

    for g in range(groups):
        sent(exchange(1, g, send_dy, dys))
    sent(exchange_left(1, sende_dy, got_dy))
    for copies in [exchange_left(2, out_left, out_e), exchange_left(3, sende_x, dx_e)]:
        arrive(copies)
        sent(copies)
    for g in range(groups):
        for copies in [exchange_back(2, g, send_x, out_w), exchange_back(3, g, dys, dx_w)]:
            arrive(copies)
            sent(copies)


def finish_kernel(
    z, mask_ref, out_w, out_e, dx_w, dx_e, sums,
    out_ref, dx_ref, gain_ref, shift_ref, scale_ref, mixw_ref, mixb_ref, pgain_ref, pshift_ref, pscale_ref,
    up_ref, upb_ref, down_ref, downb_ref,
):
    g = pl.program_id(0)
    swap = swap_matrix()
    pick = iota((1, GROUP * TILE), 1) >> 4
    masked = (swap * mask_lanes(mask_ref, g * GROUP, GROUP, pick)).astype(BF16)
    left_all = z.parts * z.left
    row, lane = iota((GROUP, left_all), 0), iota((GROUP, left_all), 1)
    want = row + g * z.mine
    for d in range(1, z.parts):
        want = want + jnp.where(row >= d * z.mine, z.left - z.mine, 0)
    last = jnp.where(want == lane, 1.0, 0.0)
    lanes = jnp.zeros((GROUP, 1), F32)
    for k in range(GROUP):
        lanes = jnp.where(iota((GROUP, 1), 0) == k, mask_ref[g * GROUP + k].astype(F32), lanes)
    for wire, left, target, matrix, tail in (
        (out_w, out_e, out_ref, masked, (last * lanes).astype(BF16)),
        (dx_w, dx_e, dx_ref, swap.astype(BF16), last.astype(BF16)),
    ):
        for t in range(z.main // TILE):
            block = jnp.concatenate(
                [
                    wire[0, i * z.main + t * TILE : i * z.main + (t + 1) * TILE, :]
                    for i in range(GROUP)
                ],
                axis=0,
            )
            rows = dot(matrix, block).reshape(TILE, GROUP, z.channels)
            target[t * TILE : (t + 1) * TILE] = rows.astype(target.dtype)
        rows = dot(tail, left[...].reshape(left_all, z.channels))
        target[z.patches - 1] = rows.astype(target.dtype)


    def layer_sums(l):
        me = lax.axis_index("mix")
        channels, share = z.channels, z.channels // z.parts
        row, lane = iota((z.pad, z.whole), 0), iota((z.pad, z.whole), 1)
        want = row
        for m in range(1, z.parts):
            want = want + jnp.where(row >= m * z.main, 1, 0)
        for m in range(z.parts):
            base = z.image + m * z.mine
            inside = (row >= base) & (row < base + z.mine)
            want = jnp.where(inside, m * z.patches + z.patches - 1, want)
        want = jnp.where(row < z.mix_rows, want, -1)
        order = jnp.where(want == lane, 1.0, 0.0).astype(BF16)
        lanes_in, lanes_out = iota((channels, share), 0), iota((channels, share), 1)
        own = jnp.where(lanes_in == lanes_out + me * share, 1.0, 0.0).astype(BF16)
        size = z.main + TILE
        at = iota((size, 1), 0) - z.main - me * z.mine
        edge = jnp.where((at >= 0) & (at < z.mine), 1.0, 0.0)
        fold_row, fold_lane = iota((size, z.patches), 0), iota((size, z.patches), 1)
        fold_at = fold_row - z.main - me * z.mine
        fold_to = jnp.where(
            fold_row < z.main, fold_row, jnp.where((fold_at >= 0) & (fold_at < z.mine), z.main, -1)
        )
        fold = jnp.where(fold_to == fold_lane, 1.0, 0.0).astype(BF16)
        spot = jnp.where((iota((8, z.pad), 0) == 0) & (iota((8, z.pad), 1) == z.ones), 1.0, 0.0)
        down_ref[0] = sums[0, :channels, :].astype(F32).T
        up_ref[0, : z.split, :] = sums[0, z.job_at[1] : z.job_at[1] + z.split, :].astype(F32)
        start = z.job_at[2] + channels - z.split
        up_ref[0, z.split :, :] = sums[0, z.job_at[2] : start, :].astype(F32)
        rows = sums[0, start : start + size, : z.pad]
        weight = dot(rows, order)
        mixw_ref[: z.main, l, :] = weight[: z.main]
        mixw_ref[z.main, l : l + 1, :] = jnp.sum(weight * edge, axis=0, keepdims=True)
        bias = dot_nt(spot.astype(BF16), rows).astype(BF16)
        mixb_ref[l : l + 1, :] = dot(bias, fold)[:1]
        tile = sums[0, start + size : start + size + TILE, :]
        vectors = dot(tile, own)
        for k, ref in enumerate(
            (gain_ref, shift_ref, scale_ref, pgain_ref, pshift_ref, downb_ref, pscale_ref)
        ):
            ref[l : l + 1, :] = vectors[k : k + 1]
        upb_ref[l : l + 1, :] = tile[7:8, :].astype(F32)

    for l in range(z.layers):
        pl.when(g == l)(functools.partial(layer_sums, l))


def local(parts, copies, images_in, out_grad, slot_mask, mix_gain, mix_shift, mix_scale, mix_weight, mix_bias,
          mlp_gain, mlp_shift, mlp_scale, up_weight, up_bias, down_weight, down_bias):
    slots, patches, channels = images_in.shape
    layers, _, hidden = up_weight.shape
    z = Sizes(parts, copies, slots, patches, channels, hidden, layers)
    vmem = pl.BlockSpec(memory_space=pltpu.VMEM)
    smem = pl.BlockSpec(memory_space=pltpu.SMEM)
    hbm = pl.BlockSpec(memory_space=pl.ANY)
    wire = jax.ShapeDtypeStruct((z.groups, parts, z.block, channels), BF16)
    left = jax.ShapeDtypeStruct((parts, z.left, channels), BF16)
    dma = pltpu.SemaphoreType.DMA
    rows = (z.groups, z.rows, channels)
    out_w, out_e, dx_w, dx_e, sums = pl.pallas_call(
        functools.partial(whole_kernel, z),
        out_shape=(
            wire, left, wire, left,
            jax.ShapeDtypeStruct((layers, sum(z.job_rows), channels), BF16),
        ),
        in_specs=[hbm, hbm, smem] + [vmem] * 10 + [hbm, hbm],
        out_specs=(hbm,) * 5,
        scratch_shapes=[
            pltpu.VMEM((channels, hidden), F32),
            pltpu.VMEM((channels, hidden), F32),
            pltpu.VMEM((layers, z.pad, z.pad), F32),
            pltpu.VMEM((layers, 8, channels), F32),
            pltpu.VMEM((layers, 1, hidden), F32),
            pltpu.VMEM((z.groups, patches, GROUP, channels), BF16),
            pltpu.VMEM((z.groups, parts, z.block, channels), BF16),
            pltpu.VMEM((z.groups, parts, z.block, channels), BF16),
            pltpu.VMEM((parts, z.left, channels), BF16),
            pltpu.VMEM((parts, z.left, channels), BF16),
            pltpu.VMEM((parts, z.left, channels), BF16),
            pltpu.VMEM((parts, z.left, channels), BF16),
            pltpu.VMEM((layers, *rows), BF16),
            pltpu.VMEM((layers, *rows), BF16),
            pltpu.VMEM(rows, BF16),
            pltpu.VMEM((z.groups, parts * z.mine, channels), BF16),
            pltpu.VMEM((parts, z.left, channels), BF16),
            pltpu.VMEM((z.groups, parts * z.mine, hidden), BF16),
            pltpu.VMEM((z.kept_rows, channels), BF16),
            pltpu.VMEM((layers, channels, hidden), BF16),
            pltpu.VMEM((layers, hidden, channels), BF16),
            pltpu.VMEM((layers, z.pad, z.pad), BF16),
            pltpu.VMEM((layers, z.pad, z.pad), BF16),
            dma((2 * z.groups + 2,)),
            dma((5, max(z.groups, 3 * layers))),
            dma((4, z.groups, parts)),
            dma((4, z.groups, parts)),
            dma((4, parts)),
            dma((4, parts)),
            dma((3 * layers, 3 + 2 * z.far + z.rest)),
            dma((3 * layers, 3 + 2 * z.far + z.rest)),
            pltpu.SemaphoreType.REGULAR((2,)),
        ],
        compiler_params=pltpu.CompilerParams(
            collective_id=0, has_side_effects=True, vmem_limit_bytes=64 << 20
        ),
        name="layers",
    )(
        jnp.transpose(images_in, (1, 0, 2)),
        jnp.transpose(out_grad, (1, 0, 2)),
        slot_mask,
        jnp.transpose(mix_weight, (1, 0, 2)),
        mix_bias, mix_gain, mix_shift, mix_scale, mlp_gain, mlp_shift, mlp_scale, down_bias, up_bias,
        up_weight, down_weight,
    )

    flat = (z.groups, parts * z.block, channels)
    block = pl.BlockSpec((1, *flat[1:]), lambda g: (g, 0, 0))
    whole = pl.BlockSpec(left.shape, lambda g: (0, 0, 0))
    turned = pl.BlockSpec((patches, GROUP, channels), lambda g: (0, g, 0))
    share = channels // parts
    small = jax.ShapeDtypeStruct((layers, share), F32)
    small_block = pl.BlockSpec(small.shape, lambda g: (0, 0))
    shapes = [
        jax.ShapeDtypeStruct((patches, slots, channels), BF16),
        jax.ShapeDtypeStruct((patches, slots, channels), F32),
        small, small, small,
        jax.ShapeDtypeStruct((patches, layers, z.whole), F32),
        jax.ShapeDtypeStruct((layers, patches), F32),
        small, small, small,
        jax.ShapeDtypeStruct((layers, channels, hidden // parts), F32),
        jax.ShapeDtypeStruct((layers, hidden // parts), F32),
        jax.ShapeDtypeStruct((layers, hidden // parts, channels), F32),
        small,
    ]

    def by_layer(shape):
        return pl.BlockSpec((1, *shape[1:]), lambda g: (jnp.minimum(g, layers - 1), 0, 0))

    def fixed(shape):
        return pl.BlockSpec(shape, lambda g: (0,) * len(shape))

    results = list(
        pl.pallas_call(
            functools.partial(finish_kernel, z),
            grid=(z.groups,),
            out_shape=shapes,
            in_specs=[smem, block, whole, block, whole, by_layer(sums.shape)],
            out_specs=[turned, turned]
            + [by_layer(s.shape) if k in (8, 10) else fixed(s.shape) for k, s in enumerate(shapes[2:])],
            compiler_params=pltpu.CompilerParams(vmem_limit_bytes=64 << 20),
            name="finish",
        )(slot_mask, out_w.reshape(flat), out_e, dx_w.reshape(flat), dx_e, sums)
    )
    for k in (0, 1, 5):
        results[k] = jnp.transpose(results[k], (1, 0, 2))
    return tuple(results)


def solution(mesh):
    in_specs = (P("dp", "mix", None), P("dp", "mix", None), P("dp")) + (P(),) * 12
    out_specs = (
        P("dp", "mix", None),
        P("dp", "mix", None),
        P(None, "mix"),
        P(None, "mix"),
        P(None, "mix"),
        P(None, "mix", None),
        P(None, "mix"),
        P(None, "mix"),
        P(None, "mix"),
        P(None, "mix"),
        P(None, None, "mix"),
        P(None, "mix"),
        P(None, "mix", None),
        P(None, "mix"),
    )
    return jax.shard_map(
        functools.partial(local, mesh.shape["mix"], mesh.shape["dp"]),
        mesh=mesh,
        in_specs=in_specs,
        out_specs=out_specs,
        check_vma=False,
    )
```
